32 devices in a mesh: seq: 8 (over z, x), head: 4 (over y, core).
Axes of the slice: x: 2, y: 2, z: 4, core: 2. Of those that a mesh axis runs over, the one named last changes fastest.
Arguments:
- ref_audio: bfloat16 [1024, 1024], P('seq', 'head'), may hold values from -32 to 32
- val_audio: bfloat16 [1024, 1024], P('seq', 'head'), may hold values from -6 to 6
- ref_video: bfloat16 [192, 1024], P('seq', 'head'), may hold values from -32 to 32
- val_video: bfloat16 [192, 1024], P('seq', 'head'), may hold values from -6 to 6
- audio_proj: bfloat16 [1024, 1024], P('head'), may hold values from -1.25 to 1.25
- video_proj: bfloat16 [1024, 1024], P('head'), may hold values from -1.25 to 1.25
Outputs:
- audio_out: bfloat16 [1024, 1024], P('seq', 'head')
- video_out: bfloat16 [192, 1024], P('seq', 'head')
The draws below stay inside these ranges and needn't reach their ends.
All inputs are finite; a program needn't handle non-finite values.
Results may differ from the reference program's by a relative error of at most 0.012.
Values may be sent and summed in bfloat16 or wider, within the bound.
No kernel may reach another device: no remote copies, remote signals or barrier semaphores. Data moves between devices by JAX's collectives and lax.ppermute only.
A program may use at most 64 MiB of HBM per device.

```python
import jax
import jax.numpy as jnp
from jax import lax

D = 1024
HEADS = 16
HEAD_DIM = 64
NA = 1024
NV = 192


def shaped_field(key, total):
    field_vals = 1.5 * jnp.clip(jax.random.normal(key, (total, HEADS * HEAD_DIM), jnp.float32), -4.0, 4.0)
    return field_vals


def draw_ref_audio(key, part):
    key = jax.random.fold_in(key, 11)
    return shaped_field(key, NA).astype(jnp.bfloat16)


def draw_ref_video(key, part):
    key = jax.random.fold_in(key, 12)
    return shaped_field(key, NV).astype(jnp.bfloat16)


def steps_of(stream_key, extent, pieces, least, high):
    factor_of = 1.0
    for dim, parts in pieces:
        steps = jax.random.uniform(jax.random.fold_in(jax.random.fold_in(stream_key, 6), dim), (parts,), jnp.float32, least / len(pieces), high / len(pieces))
        factor_of = factor_of * jnp.repeat(jnp.exp(steps), extent[dim] // parts).reshape((-1,) + (1,) * (len(extent) - 1 - dim))
    return factor_of


def normal_values(key, dims, width, limit, pieces=(), held_as=jnp.bfloat16):
    result = width * jax.random.normal(key, dims, jnp.float32)
    if pieces:
        result = result * steps_of(key, dims, pieces, -0.22, 0.18)
    return jnp.clip(result, -limit, limit).astype(held_as)


def setup_inputs(seed: int = 0) -> dict:
    keys = jax.random.split(jax.random.key(seed), 7)
    return {
        "ref_audio": draw_ref_audio(jax.random.fold_in(keys[6], 71), 0),
        "val_audio": normal_values(keys[1], (NA, D), 1.0, 6.0, ((0, 8), (1, 4))),
        "ref_video": draw_ref_video(jax.random.fold_in(keys[6], 71), 0),
        "val_video": normal_values(keys[3], (NV, D), 1.0, 6.0, ((0, 8), (1, 4))),
        "audio_proj": normal_values(keys[4], (D, D), (max(D // 40, 1)) ** -0.5, 1.25, ((0, 4),)),
        "video_proj": normal_values(keys[5], (D, D), (max(D // 40, 1)) ** -0.5, 1.25, ((0, 4),)),
    }


def split_heads(values):
    total = values.shape[0]
    return values.reshape(total, HEADS, HEAD_DIM).transpose(1, 0, 2)


def one_head(head_items):
    aud_ref, aud_val, vid_ref, vid_val = head_items
    scores = jnp.dot(aud_ref, vid_ref.T, preferred_element_type=jnp.float32) * (HEAD_DIM ** -0.5)
    row_probs = jnp.exp(scores - jnp.max(scores, axis=1, keepdims=True))
    aud_mix = jnp.dot(row_probs.astype(jnp.bfloat16), vid_val, preferred_element_type=jnp.float32)
    aud_mix = (aud_mix / jnp.sum(row_probs, axis=1, keepdims=True)).astype(jnp.bfloat16)
    col_probs = jnp.exp(scores - jnp.max(scores, axis=0, keepdims=True))
    vid_mix = jnp.dot(col_probs.astype(jnp.bfloat16).T, aud_val, preferred_element_type=jnp.float32)
    vid_mix = (vid_mix / jnp.sum(col_probs, axis=0)[:, None]).astype(jnp.bfloat16)
    return aud_mix, vid_mix


def reference(ref_audio, val_audio, ref_video, val_video, audio_proj, video_proj):
    aud_mix, vid_mix = lax.map(one_head, (split_heads(ref_audio), split_heads(val_audio), split_heads(ref_video), split_heads(val_video)))
    aud_mix = aud_mix.transpose(1, 0, 2).reshape(NA, D)
    vid_mix = vid_mix.transpose(1, 0, 2).reshape(NV, D)
    audio_out = jnp.dot(aud_mix, audio_proj, preferred_element_type=jnp.float32).astype(jnp.bfloat16)
    video_out = jnp.dot(vid_mix, video_proj, preferred_element_type=jnp.float32).astype(jnp.bfloat16)
    return audio_out, video_out
```

```python
import jax
import jax.numpy as jnp
from jax import lax
from jax.experimental import pallas as pl
from jax.experimental.pallas import tpu as pltpu
from jax.sharding import PartitionSpec as P

HEAD_DIM = 64
LANES = 128
SCALE = HEAD_DIM ** (-0.5)
VMEM_LIMIT = 48 * 1024 * 1024


def dot(a, b, dims=((1,), (0,))):
    return lax.dot_general(a, b, (dims, ((), ())), preferred_element_type=jnp.float32)


def normalised(ref, other, values):
    scores = dot(ref, other, ((1,), (1,)))
    top = jnp.max(scores, axis=1, keepdims=True)
    probs = jnp.exp((scores - top) * SCALE)
    total = jnp.sum(probs, axis=1, keepdims=True)
    mix = dot(probs.astype(jnp.bfloat16), values) / total
    return mix, top * SCALE + jnp.log(total)


def attend(aud_ref, aud_val, video, proj, aud_out, col_out):
    width = aud_ref.shape[1]
    heads = width // HEAD_DIM
    vid_rows = video.shape[0]
    lane = lax.broadcasted_iota(jnp.int32, (vid_rows, LANES), 1)
    stats = jnp.zeros((vid_rows, LANES), jnp.float32)
    aud_mix, col_mix = [], []
    for h in range(heads):
        cols = slice(h * HEAD_DIM, (h + 1) * HEAD_DIM)
        vals = slice(width + h * HEAD_DIM, width + (h + 1) * HEAD_DIM)
        q, a, k, v = aud_ref[:, cols], aud_val[:, cols], video[:, cols], video[:, vals]
        aud_mix.append(normalised(q, k, v)[0])
        mix, logsum = normalised(k, q, a)
        col_mix.append(mix)
        for part in range(3):
            piece = logsum.astype(jnp.bfloat16).astype(jnp.float32)
            stats = jnp.where(lane == part * heads + h, piece, stats)
            logsum = logsum - piece
    col_out[:, :width] = jnp.concatenate(col_mix, axis=1).astype(jnp.bfloat16)
    col_out[:, width:] = stats.astype(jnp.bfloat16)
    mixed = jnp.concatenate(aud_mix, axis=1).astype(jnp.bfloat16)
    peers = aud_out.shape[0]
    step = aud_out.shape[2]
    for p in range(peers):
        aud_out[p] = dot(mixed, proj[:, p * step : (p + 1) * step]).astype(jnp.bfloat16)


def combine(state, proj, vid_out):
    blocks, rows, _ = state.shape
    width = proj.shape[0]
    heads = width // HEAD_DIM
    source = lax.broadcasted_iota(jnp.int32, (LANES, width), 0)
    target = lax.broadcasted_iota(jnp.int32, (LANES, width), 1)
    spread = ((source < 3 * heads) & (source % heads == target // HEAD_DIM)).astype(jnp.bfloat16)
    logsums = [dot(state[b, :, width:], spread) for b in range(blocks)]
    top = logsums[0]
    for b in range(1, blocks):
        top = jnp.maximum(top, logsums[b])
    total = jnp.zeros((rows, width), jnp.float32)
    mix = jnp.zeros((rows, width), jnp.float32)
    for b in range(blocks):
        weight = jnp.exp(logsums[b] - top)
        total += weight
        mix += weight * state[b, :, :width].astype(jnp.float32)
    mixed = (mix / total).astype(jnp.bfloat16)
    step = vid_out.shape[2]
    for p in range(vid_out.shape[0]):
        vid_out[p] = dot(mixed, proj[:, p * step : (p + 1) * step]).astype(jnp.bfloat16)


def call(body, out_shape, *args):
    vmem = pl.BlockSpec(memory_space=pltpu.VMEM)
    return pl.pallas_call(
        body,
        out_shape=out_shape,
        in_specs=[vmem] * len(args),
        out_specs=jax.tree.map(lambda _: vmem, out_shape),
        compiler_params=pltpu.CompilerParams(vmem_limit_bytes=VMEM_LIMIT),
    )(*args)


def exchange(blocks, axis):
    return lax.all_to_all(blocks, axis, split_axis=0, concat_axis=0, tiled=True)


def per_device(ref_audio, val_audio, ref_video, val_video, audio_proj, video_proj):
    blocks = lax.axis_size("seq")
    peers = lax.axis_size("head")
    aud_rows, width = ref_audio.shape
    vid_rows = ref_video.shape[0]
    model = audio_proj.shape[1]
    bf16 = jnp.bfloat16
    mine = jnp.concatenate([ref_video, val_video], axis=1)
    video = exchange(jnp.broadcast_to(mine[None], (blocks,) + mine.shape), "seq")
    aud_term, col_state = call(
        attend,
        (
            jax.ShapeDtypeStruct((peers, aud_rows, model // peers), bf16),
            jax.ShapeDtypeStruct((blocks * vid_rows, width + LANES), bf16),
        ),
        ref_audio,
        val_audio,
        video.reshape(blocks * vid_rows, 2 * width),
        audio_proj,
    )
    col_state = exchange(col_state.reshape(blocks, vid_rows, width + LANES), "seq")
    vid_term = call(
        combine,
        jax.ShapeDtypeStruct((peers, vid_rows, model // peers), bf16),
        col_state,
        video_proj,
    )
    aud_sum = jnp.sum(exchange(aud_term, "head").astype(jnp.float32), axis=0)
    vid_sum = jnp.sum(exchange(vid_term, "head").astype(jnp.float32), axis=0)
    return aud_sum.astype(bf16), vid_sum.astype(bf16)


def solution(mesh):
    in_specs = (
        P("seq", "head"),
        P("seq", "head"),
        P("seq", "head"),
        P("seq", "head"),
        P("head", None),
        P("head", None),
    )
    out_specs = (P("seq", "head"), P("seq", "head"))
    return jax.shard_map(
        per_device, mesh=mesh, in_specs=in_specs, out_specs=out_specs, check_vma=False
    )
```

```python
import jax
import jax.numpy as jnp
from jax import lax
from jax.experimental import pallas as pl
from jax.experimental.pallas import tpu as pltpu
from jax.sharding import PartitionSpec as P

HEAD_DIM = 64
LANES = 128
PIECES = 3
SCALE = HEAD_DIM ** (-0.5)
VMEM_LIMIT = 48 * 1024 * 1024
BF16 = jnp.bfloat16
F32 = jnp.float32


def dot(a, b, contract_a=1, contract_b=0):
    dims = (((contract_a,), (contract_b,)), ((), ()))
    return lax.dot_general(a, b, dims, preferred_element_type=F32)


def split_pieces(value):
    pieces = []
    for _ in range(PIECES):
        piece = value.astype(BF16).astype(F32)
        pieces.append(piece)
        value = value - piece
    return pieces


def head_lanes(rows, width, head):
    return lax.broadcasted_iota(jnp.int32, (rows, width), 1) // HEAD_DIM == head


def pack(aud_ref, aud_val, vid_ref, vid_val, aud, vid, sems):
    width = aud_ref.shape[1]
    copies = [
        pltpu.make_async_copy(source, target.at[:, start : start + width], sems.at[i])
        for i, (source, target, start) in enumerate(
            ((aud_ref, aud, 0), (aud_val, aud, width), (vid_ref, vid, 0), (vid_val, vid, width))
        )
    ]
    for copy in copies:
        copy.start()
    for copy in copies:
        copy.wait()


def attend(aud_count, vid_count, *refs):
    auds, vids = refs[:aud_count], refs[aud_count : aud_count + vid_count]
    outs = refs[aud_count + vid_count :]
    row_outs, col_outs = outs[:aud_count], outs[aud_count:]
    width = auds[0].shape[1] // 2
    heads = width // HEAD_DIM
    aud_rows, vid_rows = auds[0].shape[0], vids[0].shape[0]
    aud = jnp.concatenate([ref[...] for ref in auds], axis=0)
    vid = jnp.concatenate([ref[...].astype(F32) for ref in vids], axis=0)
    queries, aud_vals = aud[:, :width], aud[:, width:]
    total_aud, total_vid = aud.shape[0], vid.shape[0]
    masks = [head_lanes(total_vid, width, h) for h in range(heads)]
    keys = jnp.concatenate([jnp.where(m, vid[:, :width], 0.0) for m in masks], axis=0)
    vals = jnp.concatenate([jnp.where(m, vid[:, width:], 0.0) for m in masks], axis=0)
    scores = dot(keys.astype(BF16), queries, 1, 1).reshape(heads, total_vid, total_aud)

    row_top = jnp.max(scores, axis=1, keepdims=True)
    row_probs = jnp.exp((scores - row_top) * SCALE)
    row_total = jnp.sum(row_probs, axis=1, keepdims=True)
    row_probs = row_probs.reshape(heads * total_vid, total_aud).astype(BF16)
    row_mix = dot(vals.astype(BF16), row_probs, 0, 0).reshape(heads, HEAD_DIM, total_aud)
    row_mix = (row_mix / row_total).reshape(width, total_aud)
    row_log = (row_top * SCALE + jnp.log(row_total)).reshape(heads, total_aud)
    row_log = jnp.concatenate(split_pieces(row_log), axis=0)
    for i in range(aud_count):
        cols = slice(i * aud_rows, (i + 1) * aud_rows)
        row_outs[i][:width, :] = row_mix[:, cols].astype(BF16)
        row_outs[i][width:, :] = jnp.concatenate(
            [row_log[:, cols], jnp.zeros((row_outs[i].shape[0] - width - PIECES * heads, aud_rows), F32)], axis=0
        ).astype(BF16)

    col_top = jnp.max(scores, axis=2, keepdims=True)
    col_probs = jnp.exp((scores - col_top) * SCALE)
    col_total = jnp.sum(col_probs, axis=2, keepdims=True)
    col_probs = col_probs.reshape(heads * total_vid, total_aud).astype(BF16)
    every = dot(col_probs, aud_vals).reshape(heads, total_vid, width)
    col_log = col_top * SCALE + jnp.log(col_total)
    lane = lax.broadcasted_iota(jnp.int32, (total_vid, LANES), 1)
    col_mix, divisor = every[0], jnp.broadcast_to(col_total[0], (total_vid, width))
    stats = jnp.zeros((total_vid, LANES), F32)
    for h in range(heads):
        if h:
            col_mix = jnp.where(masks[h], every[h], col_mix)
            divisor = jnp.where(masks[h], col_total[h], divisor)
        for i, piece in enumerate(split_pieces(col_log[h])):
            stats = jnp.where(lane == i * heads + h, piece, stats)
    col_mix = col_mix / divisor
    for i in range(vid_count):
        rows = slice(i * vid_rows, (i + 1) * vid_rows)
        col_outs[i][:, :width] = col_mix[rows].astype(BF16)
        col_outs[i][:, width:] = stats[rows].astype(BF16)


def merged(mixes, logs):
    top = logs[0]
    for log in logs[1:]:
        top = jnp.maximum(top, log)
    weights = [jnp.exp(log - top) for log in logs]
    total = sum(weights[1:], weights[0])
    mix = weights[0] * mixes[0]
    for weight, part in zip(weights[1:], mixes[1:]):
        mix += weight * part
    return mix / total


def project(aud_count, vid_count, aud_me, *refs):
    rows, cols = refs[:aud_count], refs[aud_count : aud_count + vid_count]
    aud_proj, vid_proj = refs[aud_count + vid_count : aud_count + vid_count + 2]
    outs = refs[aud_count + vid_count + 2 :]
    width = aud_proj.shape[0]
    heads = width // HEAD_DIM
    aud_rows, vid_rows = rows[0].shape[1], cols[0].shape[0]

    logs, mixes = [], []
    for ref in rows:
        pieces = ref[width:, :].astype(F32)
        log = pieces[:heads]
        for i in range(1, PIECES):
            log = log + pieces[i * heads : (i + 1) * heads]
        logs.append(log.reshape(heads, 1, aud_rows))
        mixes.append(ref[:width, :].astype(F32).reshape(heads, HEAD_DIM, aud_rows))
    aud_mix = merged(mixes, logs).reshape(width, aud_rows).astype(BF16)

    source = lax.broadcasted_iota(jnp.int32, (LANES, width), 0)
    target = lax.broadcasted_iota(jnp.int32, (LANES, width), 1)
    spread = ((source < PIECES * heads) & (source % heads == target // HEAD_DIM)).astype(BF16)
    logs = [dot(ref[:, width:], spread) for ref in cols]
    vid_mix = merged([ref[:, :width].astype(F32) for ref in cols], logs).astype(BF16)

    step = outs[0].shape[1]
    me = aud_me[0]
    for i, out in enumerate(outs):
        block = pl.ds(pl.multiple_of(partner(me, i, len(outs)) * step, step), step)
        out[:aud_rows, :] = dot(aud_mix, aud_proj[:, block], 0, 0).astype(out.dtype)
        out[aud_rows:, :] = dot(vid_mix, vid_proj[:, block]).astype(out.dtype)


def add(*refs):
    terms, (aud_out, vid_out) = refs[:-2], refs[-2:]
    aud_rows = aud_out.shape[0]
    for out, rows in ((aud_out, slice(0, aud_rows)), (vid_out, slice(aud_rows, None))):
        total = terms[0][rows, :].astype(F32)
        for term in terms[1:]:
            total += term[rows, :].astype(F32)
        out[...] = total.astype(BF16)


def call(body, out_shape, args, in_specs=None, scratch=()):
    vmem = pl.BlockSpec(memory_space=pltpu.VMEM)
    return pl.pallas_call(
        body,
        out_shape=out_shape,
        in_specs=in_specs or [vmem] * len(args),
        out_specs=[vmem] * len(out_shape),
        scratch_shapes=scratch,
        compiler_params=pltpu.CompilerParams(vmem_limit_bytes=VMEM_LIMIT),
    )(*args)


def is_power(n):
    return n & (n - 1) == 0


def partner(index, k, size):
    return index ^ k if is_power(size) else (index + k) % size


def factors(size):
    aud = 1
    while size % (aud * 2) == 0 and (aud * 2) ** 2 <= size:
        aud *= 2
    return aud, size // aud


def route(size, inner, count, k):
    pairs = []
    for i in range(size):
        here = i // inner % count
        pairs.append((i, i + (partner(here, k, count) - here) * inner))
    return pairs


def per_device(ref_audio, val_audio, ref_video, val_video, audio_proj, video_proj):
    seq, peers = lax.axis_size("seq"), lax.axis_size("head")
    aud_count, vid_count = factors(seq)
    aud_rows, width = ref_audio.shape
    vid_rows = ref_video.shape[0]
    heads = width // HEAD_DIM
    step = audio_proj.shape[1] // peers
    shape = jax.ShapeDtypeStruct

    def send(block, inner, count, k, back=False):
        if k == 0:
            return block
        pairs = route(seq, inner, count, k)
        return lax.ppermute(block, "seq", [(b, a) for a, b in pairs] if back else pairs)

    aud, vid = call(
        pack,
        (shape((aud_rows, 2 * width), BF16), shape((vid_rows, 2 * width), BF16)),
        (ref_audio, val_audio, ref_video, val_video),
        in_specs=[pl.BlockSpec(memory_space=pl.ANY)] * 4,
        scratch=[pltpu.SemaphoreType.DMA((4,))],
    )
    auds = [send(aud, 1, aud_count, k) for k in range(aud_count)]
    vids = [send(vid, aud_count, vid_count, k) for k in range(vid_count)]
    log_rows = -(-PIECES * heads // 16) * 16
    states = call(
        lambda *refs: attend(aud_count, vid_count, *refs),
        [shape((width + log_rows, aud_rows), BF16)] * aud_count
        + [shape((vid_rows, width + LANES), BF16)] * vid_count,
        auds + vids,
    )
    rows = [send(states[k], 1, aud_count, k, True) for k in range(aud_count)]
    cols = [send(states[aud_count + k], aud_count, vid_count, k, True) for k in range(vid_count)]
    me = lax.axis_index("head").astype(jnp.int32).reshape(1)
    vmem = pl.BlockSpec(memory_space=pltpu.VMEM)
    terms = call(
        lambda *refs: project(aud_count, vid_count, *refs),
        [shape((aud_rows + vid_rows, step), F32)]
        + [shape((aud_rows + vid_rows, step), BF16)] * (peers - 1),
        [me] + rows + cols + [audio_proj, video_proj],
        in_specs=[pl.BlockSpec(memory_space=pltpu.SMEM)] + [vmem] * (seq_terms(aud_count, vid_count)),
    )
    got = [terms[0]] + [
        lax.ppermute(terms[k], "head", route(peers, 1, peers, k)) for k in range(1, peers)
    ]
    aud_out, vid_out = call(
        add, (shape((aud_rows, step), BF16), shape((vid_rows, step), BF16)), got
    )
    return aud_out, vid_out


def seq_terms(aud_count, vid_count):
    return aud_count + vid_count + 2


def solution(mesh):
    in_specs = (
        P("seq", "head"),
        P("seq", "head"),
        P("seq", "head"),
        P("seq", "head"),
        P("head", None),
        P("head", None),
    )
    out_specs = (P("seq", "head"), P("seq", "head"))
    return jax.shard_map(
        per_device, mesh=mesh, in_specs=in_specs, out_specs=out_specs, check_vma=False
    )
```

```python
import jax
import jax.numpy as jnp
from jax import lax
from jax.experimental import pallas as pl
from jax.experimental.pallas import tpu as pltpu
from jax.sharding import PartitionSpec as P

HEAD_DIM = 64
LANES = 128
PIECES = 3
SCALE = HEAD_DIM ** (-0.5)
VMEM_LIMIT = 48 * 1024 * 1024
BF16 = jnp.bfloat16
F32 = jnp.float32


def dot(a, b, contract_a=1, contract_b=0):
    dims = (((contract_a,), (contract_b,)), ((), ()))
    return lax.dot_general(a, b, dims, preferred_element_type=F32)


def split_pieces(value):
    pieces = []
    for _ in range(PIECES):
        piece = value.astype(BF16).astype(F32)
        pieces.append(piece)
        value = value - piece
    return pieces


def head_lanes(rows, width, head):
    return lax.broadcasted_iota(jnp.int32, (rows, width), 1) // HEAD_DIM == head


def pack(aud_ref, aud_val, vid_ref, vid_val, aud, vid, sems):
    width = aud_ref.shape[1]
    copies = [
        pltpu.make_async_copy(source, target.at[:, start : start + width], sems.at[i])
        for i, (source, target, start) in enumerate(
            ((aud_ref, aud, 0), (aud_val, aud, width), (vid_ref, vid, 0), (vid_val, vid, width))
        )
    ]
    for copy in copies:
        copy.start()
    for copy in copies:
        copy.wait()


def attend(aud_count, vid_count, *refs):
    auds, vids = refs[:aud_count], refs[aud_count : aud_count + vid_count]
    outs = refs[aud_count + vid_count :]
    row_outs, col_outs = outs[:aud_count], outs[aud_count:]
    width = auds[0].shape[1] // 2
    heads = width // HEAD_DIM
    aud_rows, vid_rows = auds[0].shape[0], vids[0].shape[0]
    aud = jnp.concatenate([ref[...] for ref in auds], axis=0)
    vid = jnp.concatenate([ref[...].astype(F32) for ref in vids], axis=0)
    queries, aud_vals = aud[:, :width], aud[:, width:]
    total_aud, total_vid = aud.shape[0], vid.shape[0]
    masks = [head_lanes(total_vid, width, h) for h in range(heads)]
    keys = jnp.concatenate([jnp.where(m, vid[:, :width], 0.0) for m in masks], axis=0)
    vals = jnp.concatenate([jnp.where(m, vid[:, width:], 0.0) for m in masks], axis=0)
    scores = dot(keys.astype(BF16), queries, 1, 1).reshape(heads, total_vid, total_aud)

    row_top = jnp.max(scores, axis=1, keepdims=True)
    row_probs = jnp.exp((scores - row_top) * SCALE)
    row_total = jnp.sum(row_probs, axis=1, keepdims=True)
    row_probs = row_probs.reshape(heads * total_vid, total_aud).astype(BF16)
    row_mix = dot(vals.astype(BF16), row_probs, 0, 0).reshape(heads, HEAD_DIM, total_aud)
    row_mix = (row_mix / row_total).reshape(width, total_aud)
    row_log = (row_top * SCALE + jnp.log(row_total)).reshape(heads, total_aud)
    row_log = jnp.concatenate(split_pieces(row_log), axis=0)
    for i in range(aud_count):
        cols = slice(i * aud_rows, (i + 1) * aud_rows)
        row_outs[i][:width, :] = row_mix[:, cols].astype(BF16)
        row_outs[i][width:, :] = jnp.concatenate(
            [row_log[:, cols], jnp.zeros((row_outs[i].shape[0] - width - PIECES * heads, aud_rows), F32)], axis=0
        ).astype(BF16)

    col_top = jnp.max(scores, axis=2, keepdims=True)
    col_probs = jnp.exp((scores - col_top) * SCALE)
    col_total = jnp.sum(col_probs, axis=2, keepdims=True)
    col_probs = col_probs.reshape(heads * total_vid, total_aud).astype(BF16)
    every = dot(col_probs, aud_vals).reshape(heads, total_vid, width)
    col_log = col_top * SCALE + jnp.log(col_total)
    lane = lax.broadcasted_iota(jnp.int32, (total_vid, LANES), 1)
    col_mix, divisor = every[0], jnp.broadcast_to(col_total[0], (total_vid, width))
    stats = jnp.zeros((total_vid, LANES), F32)
    for h in range(heads):
        if h:
            col_mix = jnp.where(masks[h], every[h], col_mix)
            divisor = jnp.where(masks[h], col_total[h], divisor)
        for i, piece in enumerate(split_pieces(col_log[h])):
            stats = jnp.where(lane == i * heads + h, piece, stats)
    col_mix = col_mix / divisor
    for i in range(vid_count):
        rows = slice(i * vid_rows, (i + 1) * vid_rows)
        col_outs[i][:, :width] = col_mix[rows].astype(BF16)
        col_outs[i][:, width:] = stats[rows].astype(BF16)


def merged(mixes, logs):
    top = logs[0]
    for log in logs[1:]:
        top = jnp.maximum(top, log)
    weights = [jnp.exp(log - top) for log in logs]
    total = sum(weights[1:], weights[0])
    mix = weights[0] * mixes[0]
    for weight, part in zip(weights[1:], mixes[1:]):
        mix += weight * part
    return mix / total


def project(mix, proj, me, outs):
    step = outs[0].shape[1]
    for i, out in enumerate(outs):
        block = pl.ds(pl.multiple_of(partner(me, i, len(outs)) * step, step), step)
        out[...] = dot(mix, proj[:, block]).astype(out.dtype)


def project_audio(count, me, *refs):
    rows, proj, outs = refs[:count], refs[count], refs[count + 1 :]
    width = proj.shape[0]
    heads = width // HEAD_DIM
    aud_rows = rows[0].shape[1]
    logs, mixes = [], []
    for ref in rows:
        pieces = ref[width:, :].astype(F32)
        log = pieces[:heads]
        for i in range(1, PIECES):
            log = log + pieces[i * heads : (i + 1) * heads]
        logs.append(log.reshape(heads, 1, aud_rows))
        mixes.append(ref[:width, :].astype(F32).reshape(heads, HEAD_DIM, aud_rows))
    mix = merged(mixes, logs).reshape(width, aud_rows)
    project(mix.T.astype(BF16), proj, me[0], outs)


def project_video(count, me, *refs):
    cols, proj, outs = refs[:count], refs[count], refs[count + 1 :]
    width = proj.shape[0]
    heads = width // HEAD_DIM
    source = lax.broadcasted_iota(jnp.int32, (LANES, width), 0)
    target = lax.broadcasted_iota(jnp.int32, (LANES, width), 1)
    spread = ((source < PIECES * heads) & (source % heads == target // HEAD_DIM)).astype(BF16)
    logs = [dot(ref[:, width:], spread) for ref in cols]
    mix = merged([ref[:, :width].astype(F32) for ref in cols], logs)
    project(mix.astype(BF16), proj, me[0], outs)


def add(*refs):
    terms, out = refs[:-1], refs[-1]
    total = terms[0][...].astype(F32)
    for term in terms[1:]:
        total += term[...].astype(F32)
    out[...] = total.astype(BF16)


def call(body, out_shape, args, in_specs=None, scratch=()):
    vmem = pl.BlockSpec(memory_space=pltpu.VMEM)
    return pl.pallas_call(
        body,
        out_shape=out_shape,
        in_specs=in_specs or [vmem] * len(args),
        out_specs=[vmem] * len(out_shape),
        scratch_shapes=scratch,
        compiler_params=pltpu.CompilerParams(vmem_limit_bytes=VMEM_LIMIT),
    )(*args)


def is_power(n):
    return n & (n - 1) == 0


def partner(index, k, size):
    return index ^ k if is_power(size) else (index + k) % size


def factors(size):
    aud = 1
    while size % (aud * 2) == 0 and (aud * 2) ** 2 <= size:
        aud *= 2
    return aud, size // aud


def route(size, inner, count, k):
    pairs = []
    for i in range(size):
        here = i // inner % count
        pairs.append((i, i + (partner(here, k, count) - here) * inner))
    return pairs


def per_device(ref_audio, val_audio, ref_video, val_video, audio_proj, video_proj):
    seq, peers = lax.axis_size("seq"), lax.axis_size("head")
    aud_count, vid_count = factors(seq)
    aud_rows, width = ref_audio.shape
    vid_rows = ref_video.shape[0]
    heads = width // HEAD_DIM
    step = audio_proj.shape[1] // peers
    shape = jax.ShapeDtypeStruct

    def send(block, inner, count, k, back=False):
        if k == 0:
            return block
        pairs = route(seq, inner, count, k)
        return lax.ppermute(block, "seq", [(b, a) for a, b in pairs] if back else pairs)

    aud, vid = call(
        pack,
        (shape((aud_rows, 2 * width), BF16), shape((vid_rows, 2 * width), BF16)),
        [
            pltpu.with_memory_space_constraint(x, pltpu.HBM)
            for x in (ref_audio, val_audio, ref_video, val_video)
        ],
        in_specs=[pl.BlockSpec(memory_space=pltpu.HBM)] * 4,
        scratch=[pltpu.SemaphoreType.DMA((4,))],
    )
    auds = [send(aud, 1, aud_count, k) for k in range(aud_count)]
    vids = [send(vid, aud_count, vid_count, k) for k in range(vid_count)]
    log_rows = -(-PIECES * heads // 16) * 16
    states = call(
        lambda *refs: attend(aud_count, vid_count, *refs),
        [shape((width + log_rows, aud_rows), BF16)] * aud_count
        + [shape((vid_rows, width + LANES), BF16)] * vid_count,
        auds + vids,
    )
    rows = [send(states[k], 1, aud_count, k, True) for k in range(aud_count)]
    cols = [
        send(states[aud_count + k], aud_count, vid_count, k, True) for k in reversed(range(vid_count))
    ]
    me = lax.axis_index("head").astype(jnp.int32).reshape(1)
    vmem = pl.BlockSpec(memory_space=pltpu.VMEM)

    def head_sum(body, states, proj, count):
        terms = call(
            lambda *refs: body(len(states), *refs),
            [shape((count, step), F32)] + [shape((count, step), BF16)] * (peers - 1),
            [me] + states + [proj],
            in_specs=[pl.BlockSpec(memory_space=pltpu.SMEM)] + [vmem] * (len(states) + 1),
        )
        got = [
            lax.ppermute(terms[k], "head", route(peers, 1, peers, k))
            for k in reversed(range(1, peers))
        ]
        return call(add, [shape((count, step), BF16)], [terms[0]] + got)[0]

    return (
        head_sum(project_audio, rows, audio_proj, aud_rows),
        head_sum(project_video, cols, video_proj, vid_rows),
    )


def solution(mesh):
    in_specs = (
        P("seq", "head"),
        P("seq", "head"),
        P("seq", "head"),
        P("seq", "head"),
        P("head", None),
        P("head", None),
    )
    out_specs = (P("seq", "head"), P("seq", "head"))
    return jax.shard_map(
        per_device, mesh=mesh, in_specs=in_specs, out_specs=out_specs, check_vma=False
    )
```

```python
import functools

import jax
import jax.numpy as jnp
from jax import lax
from jax.experimental import pallas as pl
from jax.experimental.pallas import tpu as pltpu
from jax.sharding import PartitionSpec as P

HEAD_DIM = 64
LANES = 128
PIECES = 3
SCALE = HEAD_DIM ** (-0.5)
VMEM_LIMIT = 48 * 1024 * 1024
COST = 5 * 10**9
BF16 = jnp.bfloat16
F32 = jnp.float32


def dot(a, b, contract_a=1, contract_b=0):
    dims = (((contract_a,), (contract_b,)), ((), ()))
    return lax.dot_general(a, b, dims, preferred_element_type=F32)


def split_pieces(value):
    pieces = []
    for _ in range(PIECES):
        piece = value.astype(BF16).astype(F32)
        pieces.append(piece)
        value = value - piece
    return pieces


def head_lanes(rows, width, head):
    return lax.broadcasted_iota(jnp.int32, (rows, width), 1) // HEAD_DIM == head


def pack(aud_ref, aud_val, vid_ref, vid_val, aud, vid, sems):
    width = aud_ref.shape[1]
    copies = [
        pltpu.make_async_copy(source, target.at[:, start : start + width], sems.at[i])
        for i, (source, target, start) in enumerate(
            ((aud_ref, aud, 0), (aud_val, aud, width), (vid_ref, vid, 0), (vid_val, vid, width))
        )
    ]
    for copy in copies:
        copy.start()
    for copy in copies:
        copy.wait()


def in_order(blocks):
    order = [0]
    bit = len(blocks) // 2
    while bit:
        order += [k + bit for k in order]
        bit //= 2
    return [blocks[len(blocks) - 1 - k] for k in order]


def attend(aud_count, *refs):
    auds, vids, (row_keep, row_give, col_keep, col_give) = refs[:aud_count], refs[aud_count:-4], refs[-4:]
    auds, vids = in_order(auds), in_order(vids)
    width = auds[0].shape[1] // 2
    heads = width // HEAD_DIM
    aud = jnp.concatenate([ref[...] for ref in auds], axis=0)
    vid = jnp.concatenate([ref[...] for ref in vids], axis=0).astype(F32)
    queries, aud_vals = aud[:, :width], aud[:, width:]
    total_aud, total_vid = aud.shape[0], vid.shape[0]
    masks = [head_lanes(total_vid, width, h) for h in range(heads)]
    keys = jnp.concatenate([jnp.where(m, vid[:, :width], 0.0) for m in masks], axis=0)
    vals = jnp.concatenate([jnp.where(m, vid[:, width:], 0.0) for m in masks], axis=0)
    scores = dot(keys.astype(BF16), queries, 1, 1).reshape(heads, total_vid, total_aud)

    row_top = jnp.max(scores, axis=1, keepdims=True)
    row_probs = jnp.exp((scores - row_top) * SCALE)
    row_total = jnp.sum(row_probs, axis=1, keepdims=True)
    row_probs = row_probs.reshape(heads * total_vid, total_aud).astype(BF16)
    row_mix = dot(vals.astype(BF16), row_probs, 0, 0).reshape(heads, HEAD_DIM, total_aud)
    row_mix = (row_mix / row_total).reshape(width, total_aud)
    row_log = (row_top * SCALE + jnp.log(row_total)).reshape(heads, total_aud)
    for i, out in enumerate((row_keep, row_give)):
        cols = slice(i * out.shape[1], (i + 1) * out.shape[1])
        put_rows(out, row_mix[:, cols], row_log[:, cols])

    col_top = jnp.max(scores, axis=2, keepdims=True)
    col_probs = jnp.exp((scores - col_top) * SCALE)
    col_total = jnp.sum(col_probs, axis=2, keepdims=True)
    col_probs = col_probs.reshape(heads * total_vid, total_aud).astype(BF16)
    every = dot(col_probs, aud_vals).reshape(heads, total_vid, width)
    col_log = col_top * SCALE + jnp.log(col_total)
    col_mix, divisor = every[0], jnp.broadcast_to(col_total[0], (total_vid, width))
    for h in range(1, heads):
        col_mix = jnp.where(masks[h], every[h], col_mix)
        divisor = jnp.where(masks[h], col_total[h], divisor)
    col_mix = col_mix / divisor
    lane = lax.broadcasted_iota(jnp.int32, (total_vid, LANES), 1) % heads
    logs = jnp.broadcast_to(col_log[0], (total_vid, LANES))
    for h in range(1, heads):
        logs = jnp.where(lane == h, col_log[h], logs)
    for i, out in enumerate((col_keep, col_give)):
        rows = slice(i * out.shape[0], (i + 1) * out.shape[0])
        put_cols(out, col_mix[rows], logs[rows])


def put_rows(out, mix, log):
    width, tokens = mix.shape
    pad = jnp.zeros((out.shape[0] - width - PIECES * log.shape[0], tokens), F32)
    out[:width, :] = mix.astype(BF16)
    out[width:, :] = jnp.concatenate(split_pieces(log) + [pad], axis=0).astype(BF16)


def get_rows(ref, width):
    heads, tokens = width // HEAD_DIM, ref.shape[1]
    pieces = ref[width:, :].astype(F32)
    log = pieces[:heads]
    for i in range(1, PIECES):
        log = log + pieces[i * heads : (i + 1) * heads]
    mix = ref[:width, :].astype(F32).reshape(heads, HEAD_DIM, tokens)
    return mix, log.reshape(heads, 1, tokens)


def put_cols(out, mix, logs):
    width = mix.shape[1]
    heads = width // HEAD_DIM
    lane = lax.broadcasted_iota(jnp.int32, logs.shape, 1)
    pieces = split_pieces(logs)
    stats = jnp.zeros_like(logs)
    for i, piece in enumerate(pieces):
        stats = jnp.where(lane // heads == i, piece, stats)
    out[:, :width] = mix.astype(BF16)
    out[:, width:] = stats.astype(BF16)


def get_cols(ref, width, log_width, lane_heads):
    heads = width // HEAD_DIM
    source = lax.broadcasted_iota(jnp.int32, (LANES, log_width), 0)
    target = lax.broadcasted_iota(jnp.int32, (LANES, log_width), 1)
    spread = (source < PIECES * heads) & (source % heads == lane_heads(target))
    return ref[:, :width].astype(F32), dot(ref[:, width:], spread.astype(BF16))


def merge_weights(logs):
    top = jnp.maximum(logs[0], logs[1])
    weights = [jnp.exp(log - top) for log in logs]
    total = weights[0] + weights[1]
    return [weight / total for weight in weights], top + jnp.log(total)


def merge_rows(mine, got, keep, give):
    width = mine.shape[0] // HEAD_DIM * HEAD_DIM
    states = [get_rows(ref, width) for ref in (mine, got)]
    weights, logs = merge_weights([log for _, log in states])
    mix = weights[0] * states[0][0] + weights[1] * states[1][0]
    mix, logs = mix.reshape(width, -1), logs.reshape(width // HEAD_DIM, -1)
    for i, out in enumerate((keep, give)):
        cols = slice(i * out.shape[1], (i + 1) * out.shape[1])
        put_rows(out, mix[:, cols], logs[:, cols])


def merge_cols(mine, got, keep, give):
    width = mine.shape[1] - LANES
    heads = width // HEAD_DIM
    wide = [get_cols(ref, width, width, lambda lane: lane // HEAD_DIM) for ref in (mine, got)]
    slim = [get_cols(ref, width, LANES, lambda lane: lane % heads)[1] for ref in (mine, got)]
    weights, _ = merge_weights([log for _, log in wide])
    _, logs = merge_weights(slim)
    mix = weights[0] * wide[0][0] + weights[1] * wide[1][0]
    for i, out in enumerate((keep, give)):
        rows = slice(i * out.shape[0], (i + 1) * out.shape[0])
        put_cols(out, mix[rows], logs[rows])


def project(mix, proj, me, outs):
    step = outs[0].shape[1]
    for i, out in enumerate(outs):
        block = pl.ds(pl.multiple_of(partner(me, i, len(outs)) * step, step), step)
        out[...] = dot(mix, proj[:, block]).astype(out.dtype)


def project_audio(me, mine, got, proj, *outs):
    width = proj.shape[0]
    states = [get_rows(ref, width) for ref in (mine, got)]
    weights, _ = merge_weights([log for _, log in states])
    mix = weights[0] * states[0][0] + weights[1] * states[1][0]
    project(mix.reshape(width, -1).T.astype(BF16), proj, me[0], outs)


def project_video(me, mine, got, proj, *outs):
    width = proj.shape[0]
    states = [get_cols(ref, width, width, lambda lane: lane // HEAD_DIM) for ref in (mine, got)]
    weights, _ = merge_weights([log for _, log in states])
    mix = weights[0] * states[0][0] + weights[1] * states[1][0]
    project(mix.astype(BF16), proj, me[0], outs)


def add(*refs):
    terms, outs = refs[:-2], refs[-2:]
    count = len(terms) // 2
    for out, group in zip(outs, (terms[:count], terms[count:])):
        total = group[0][...].astype(F32)
        for term in group[1:]:
            total += term[...].astype(F32)
        out[...] = total.astype(BF16)


def call(body, out_shape, args, in_specs=None, scratch=()):
    vmem = pl.BlockSpec(memory_space=pltpu.VMEM)
    return pl.pallas_call(
        body,
        out_shape=out_shape,
        in_specs=in_specs or [vmem] * len(args),
        out_specs=[vmem] * len(out_shape),
        scratch_shapes=scratch,
        compiler_params=pltpu.CompilerParams(vmem_limit_bytes=VMEM_LIMIT),
        cost_estimate=pl.CostEstimate(flops=COST, bytes_accessed=0, transcendentals=0),
    )(*args)


def partner(index, k, size):
    return index ^ k


def swap(block, axis, distance):
    return lax.ppermute(block, axis, [(i, i ^ distance) for i in range(lax.axis_size(axis))])


def factors(size):
    bits = size.bit_length() - 1
    assert size == 1 << bits
    return 1 << (bits // 2), 1 << (bits - bits // 2)


def bits_of(inner, count):
    return [inner << i for i in reversed(range(count.bit_length() - 1))]


def per_device(ref_audio, val_audio, ref_video, val_video, audio_proj, video_proj):
    seq, peers = lax.axis_size("seq"), lax.axis_size("head")
    aud_count, vid_count = factors(seq)
    aud_rows, width = ref_audio.shape
    vid_rows = ref_video.shape[0]
    heads = width // HEAD_DIM
    step = audio_proj.shape[1] // peers
    aud_bits, vid_bits = bits_of(1, aud_count), bits_of(aud_count, vid_count)
    log_rows = -(-PIECES * heads // 16) * 16

    def shape(rows, cols, dtype=BF16):
        return jax.ShapeDtypeStruct((rows, cols), dtype)

    def gather(block, distances):
        count = 1 << len(distances)
        return [swap(block, "seq", k * distances[-1]) for k in reversed(range(1, count))] + [block]

    def scatter(keep, give, distances, merge, axis):
        for distance in reversed(distances[1:]):
            got = swap(give, "seq", distance)
            half = list(keep.shape)
            half[axis] //= 2
            keep, give = call(merge, [shape(*half)] * 2, [keep, got])
        return keep, swap(give, "seq", distances[0])

    aud, vid = call(
        pack,
        [shape(aud_rows, 2 * width), shape(vid_rows, 2 * width)],
        [
            pltpu.with_memory_space_constraint(x, pltpu.HBM)
            for x in (ref_audio, val_audio, ref_video, val_video)
        ],
        in_specs=[pl.BlockSpec(memory_space=pltpu.HBM)] * 4,
        scratch=[pltpu.SemaphoreType.DMA((4,))],
    )
    auds = gather(aud, aud_bits)
    vids = gather(vid, vid_bits)
    rows_shape = shape(width + log_rows, aud_rows * aud_count // 2)
    cols_shape = shape(vid_rows * vid_count // 2, width + LANES)
    row_keep, row_give, col_keep, col_give = call(
        functools.partial(attend, aud_count),
        [rows_shape, rows_shape, cols_shape, cols_shape],
        [*auds, *vids],
    )
    rows = scatter(row_keep, row_give, aud_bits, merge_rows, 1)
    cols = scatter(col_keep, col_give, vid_bits, merge_cols, 0)

    me = lax.axis_index("head").astype(jnp.int32).reshape(1)
    vmem = pl.BlockSpec(memory_space=pltpu.VMEM)
    smem = pl.BlockSpec(memory_space=pltpu.SMEM)
    hbm = pl.BlockSpec(memory_space=pl.ANY)

    def head_terms(body, states, proj, count, after=()):
        return call(
            lambda *refs: body(*refs[:4], *refs[4 + len(after) :]),
            [shape(count, step, F32)] + [shape(count, step)] * (peers - 1),
            [me, *states, proj, *after],
            in_specs=[smem, vmem, vmem, vmem] + [hbm] * len(after),
        )

    def exchange(terms):
        return [terms[0]] + [swap(terms[k], "head", k) for k in range(1, peers)]

    aud_got = exchange(head_terms(project_audio, rows, audio_proj, aud_rows, cols[:1]))
    vid_got = exchange(head_terms(project_video, cols, video_proj, vid_rows, aud_got[1:2]))
    return tuple(call(add, [shape(aud_rows, step), shape(vid_rows, step)], aud_got + vid_got))


def solution(mesh):
    in_specs = (
        P("seq", "head"),
        P("seq", "head"),
        P("seq", "head"),
        P("seq", "head"),
        P("head", None),
        P("head", None),
    )
    out_specs = (P("seq", "head"), P("seq", "head"))
    return jax.shard_map(
        per_device, mesh=mesh, in_specs=in_specs, out_specs=out_specs, check_vma=False
    )
```

```python
import functools

import jax
import jax.numpy as jnp
from jax import lax
from jax.experimental import pallas as pl
from jax.experimental.pallas import tpu as pltpu
from jax.sharding import PartitionSpec as P

HEAD_DIM = 64
LANES = 128
PIECES = 3
SCALE = HEAD_DIM ** (-0.5)
VMEM_LIMIT = 48 * 1024 * 1024
COST = 5 * 10**9
BF16 = jnp.bfloat16
F32 = jnp.float32


def dot(a, b, contract_a=1, contract_b=0):
    dims = (((contract_a,), (contract_b,)), ((), ()))
    return lax.dot_general(a, b, dims, preferred_element_type=F32)


def split_pieces(value):
    pieces = []
    for _ in range(PIECES):
        piece = value.astype(BF16).astype(F32)
        pieces.append(piece)
        value = value - piece
    return pieces


def head_lanes(rows, width, head):
    return lax.broadcasted_iota(jnp.int32, (rows, width), 1) // HEAD_DIM == head


def pack(aud_ref, aud_val, vid_ref, vid_val, aud, vid, sems):
    width = aud_ref.shape[1]
    copies = [
        pltpu.make_async_copy(source, target.at[:, start : start + width], sems.at[i])
        for i, (source, target, start) in enumerate(
            ((aud_ref, aud, 0), (aud_val, aud, width), (vid_ref, vid, 0), (vid_val, vid, width))
        )
    ]
    for copy in copies:
        copy.start()
    for copy in copies:
        copy.wait()


def attend(aud_count, vid_count, *refs):
    auds, vids = refs[:aud_count], refs[aud_count : aud_count + vid_count]
    row_outs = refs[aud_count + vid_count : 2 * aud_count + vid_count]
    col_outs = refs[2 * aud_count + vid_count :]
    width = auds[0].shape[1] // 2
    heads = width // HEAD_DIM
    aud = jnp.concatenate([ref[...] for ref in auds], axis=0)
    vid = jnp.concatenate([ref[...] for ref in vids], axis=0).astype(F32)
    queries, aud_vals = aud[:, :width], aud[:, width:]
    total_aud, total_vid = aud.shape[0], vid.shape[0]
    masks = [head_lanes(total_vid, width, h) for h in range(heads)]
    keys = jnp.concatenate([jnp.where(m, vid[:, :width], 0.0) for m in masks], axis=0)
    vals = jnp.concatenate([jnp.where(m, vid[:, width:], 0.0) for m in masks], axis=0)
    scores = dot(keys.astype(BF16), queries, 1, 1).reshape(heads, total_vid, total_aud)

    row_top = jnp.max(scores, axis=1, keepdims=True)
    row_probs = jnp.exp((scores - row_top) * SCALE)
    row_total = jnp.sum(row_probs, axis=1, keepdims=True)
    row_probs = row_probs.reshape(heads * total_vid, total_aud).astype(BF16)
    row_mix = dot(vals.astype(BF16), row_probs, 0, 0).reshape(heads, HEAD_DIM, total_aud)
    row_mix = (row_mix / row_total).reshape(width, total_aud)
    row_log = (row_top * SCALE + jnp.log(row_total)).reshape(heads, total_aud)
    for i, out in enumerate(row_outs):
        cols = slice(i * out.shape[1], (i + 1) * out.shape[1])
        put_rows(out, row_mix[:, cols], row_log[:, cols])

    col_top = jnp.max(scores, axis=2, keepdims=True)
    col_probs = jnp.exp((scores - col_top) * SCALE)
    col_total = jnp.sum(col_probs, axis=2, keepdims=True)
    col_probs = col_probs.reshape(heads * total_vid, total_aud).astype(BF16)
    every = dot(col_probs, aud_vals).reshape(heads, total_vid, width)
    col_log = col_top * SCALE + jnp.log(col_total)
    col_mix, divisor = every[0], jnp.broadcast_to(col_total[0], (total_vid, width))
    for h in range(1, heads):
        col_mix = jnp.where(masks[h], every[h], col_mix)
        divisor = jnp.where(masks[h], col_total[h], divisor)
    col_mix = col_mix / divisor
    lane = lax.broadcasted_iota(jnp.int32, (total_vid, LANES), 1) % heads
    logs = jnp.broadcast_to(col_log[0], (total_vid, LANES))
    for h in range(1, heads):
        logs = jnp.where(lane == h, col_log[h], logs)
    for i, out in enumerate(col_outs):
        rows = slice(i * out.shape[0], (i + 1) * out.shape[0])
        put_cols(out, col_mix[rows], logs[rows])


def put_rows(out, mix, log):
    width, tokens = mix.shape
    pad = jnp.zeros((out.shape[0] - width - PIECES * log.shape[0], tokens), F32)
    out[:width, :] = mix.astype(BF16)
    out[width:, :] = jnp.concatenate(split_pieces(log) + [pad], axis=0).astype(BF16)


def get_rows(ref, width):
    heads, tokens = width // HEAD_DIM, ref.shape[1]
    pieces = ref[width:, :].astype(F32)
    log = pieces[:heads]
    for i in range(1, PIECES):
        log = log + pieces[i * heads : (i + 1) * heads]
    mix = ref[:width, :].astype(F32).reshape(heads, HEAD_DIM, tokens)
    return mix, log.reshape(heads, 1, tokens)


def put_cols(out, mix, logs):
    width = mix.shape[1]
    heads = width // HEAD_DIM
    lane = lax.broadcasted_iota(jnp.int32, logs.shape, 1)
    pieces = split_pieces(logs)
    stats = jnp.zeros_like(logs)
    for i, piece in enumerate(pieces):
        stats = jnp.where(lane // heads == i, piece, stats)
    out[:, :width] = mix.astype(BF16)
    out[:, width:] = stats.astype(BF16)


def get_cols(ref, width):
    heads = width // HEAD_DIM
    source = lax.broadcasted_iota(jnp.int32, (LANES, width), 0)
    target = lax.broadcasted_iota(jnp.int32, (LANES, width), 1)
    spread = (source < PIECES * heads) & (source % heads == target // HEAD_DIM)
    return ref[:, :width].astype(F32), dot(ref[:, width:], spread.astype(BF16))


def merge(states):
    top = states[0][1]
    for _, log in states[1:]:
        top = jnp.maximum(top, log)
    total, mix = 0.0, 0.0
    for part, log in states:
        weight = jnp.exp(log - top)
        total += weight
        mix += weight * part
    return mix / total


def project(mix, proj, me, outs):
    step = outs[0].shape[1]
    for i, out in enumerate(outs):
        block = pl.ds(pl.multiple_of(partner(me, i, len(outs)) * step, step), step)
        out[: mix.shape[0], :] = dot(mix, proj[:, block]).astype(out.dtype)


def project_audio(me, proj, states, outs):
    width = proj.shape[0]
    mix = merge([get_rows(ref, width) for ref in states]).reshape(width, -1)
    project(mix.T.astype(BF16), proj, me[0], outs)


def project_video(me, proj, states, aud_core, outs):
    mix = merge([get_cols(ref, proj.shape[0]) for ref in states])
    aud_rows = aud_core.shape[0]
    outs[1][:aud_rows, :] = aud_core[...]
    project(mix.astype(BF16), proj, me[0], [outs[0], outs[1].at[aud_rows:, :], *outs[2:]])


def add(*refs):
    terms, vid_out, aud_out = refs[:-2], refs[-2], refs[-1]
    count = len(terms) // 2 + 1
    aud_rows = aud_out.shape[0]
    core = terms[1][...].astype(F32)
    vid = terms[0][...] + core[aud_rows:]
    aud = terms[count][...] + core[:aud_rows]
    for vid_term, aud_term in zip(terms[2:count], terms[count + 1 :]):
        vid += vid_term[...].astype(F32)
        aud += aud_term[:aud_rows].astype(F32)
    vid_out[...] = vid.astype(BF16)
    aud_out[...] = aud.astype(BF16)


def call(body, out_shape, args, in_specs=None, scratch=()):
    vmem = pl.BlockSpec(memory_space=pltpu.VMEM)
    return pl.pallas_call(
        body,
        out_shape=out_shape,
        in_specs=in_specs or [vmem] * len(args),
        out_specs=[vmem] * len(out_shape),
        scratch_shapes=scratch,
        compiler_params=pltpu.CompilerParams(vmem_limit_bytes=VMEM_LIMIT),
        cost_estimate=pl.CostEstimate(flops=COST, bytes_accessed=0, transcendentals=0),
    )(*args)


def partner(index, k, size):
    return index ^ k


def swap(block, axis, distance):
    return lax.ppermute(block, axis, [(i, i ^ distance) for i in range(lax.axis_size(axis))])


def factors(size):
    bits = size.bit_length() - 1
    assert size == 1 << bits
    return 1 << (bits // 2), 1 << (bits - bits // 2)


def per_device(ref_audio, val_audio, ref_video, val_video, audio_proj, video_proj):
    seq, peers = lax.axis_size("seq"), lax.axis_size("head")
    aud_count, vid_count = factors(seq)
    aud_rows, width = ref_audio.shape
    vid_rows = ref_video.shape[0]
    heads = width // HEAD_DIM
    step = audio_proj.shape[1] // peers
    log_rows = -(-PIECES * heads // 16) * 16

    def shape(rows, cols, dtype=BF16):
        return jax.ShapeDtypeStruct((rows, cols), dtype)

    def gather(block, stride, count):
        return [swap(block, "seq", k * stride) for k in range(1, count)] + [block]

    def scatter(blocks, stride):
        count = len(blocks)
        return [swap(blocks[k - 1], "seq", k * stride) for k in reversed(range(1, count))] + [blocks[-1]]

    aud, vid = call(
        pack,
        [shape(aud_rows, 2 * width), shape(vid_rows, 2 * width)],
        [
            pltpu.with_memory_space_constraint(x, pltpu.HBM)
            for x in (ref_audio, val_audio, ref_video, val_video)
        ],
        in_specs=[pl.BlockSpec(memory_space=pltpu.HBM)] * 4,
        scratch=[pltpu.SemaphoreType.DMA((4,))],
    )
    auds, vids = gather(aud, 1, aud_count), gather(vid, aud_count, vid_count)
    states = call(
        functools.partial(attend, aud_count, vid_count),
        [shape(width + log_rows, aud_rows)] * aud_count + [shape(vid_rows, width + LANES)] * vid_count,
        [*auds, *vids],
    )
    rows = scatter(states[:aud_count], 1)
    cols = scatter(states[aud_count:], aud_count)

    me = lax.axis_index("head").astype(jnp.int32).reshape(1)
    vmem = pl.BlockSpec(memory_space=pltpu.VMEM)
    smem = pl.BlockSpec(memory_space=pltpu.SMEM)
    hbm = pl.BlockSpec(memory_space=pl.ANY)

    aud_terms = call(
        lambda me, proj, *refs: project_audio(me, proj, refs[:aud_count], refs[aud_count:]),
        [shape(aud_rows, step, F32), shape(aud_rows, step)]
        + [shape(aud_rows + vid_rows + 8, step)] * (peers - 2),
        [me, audio_proj, *rows],
        in_specs=[smem, vmem] + [vmem] * aud_count,
    )
    vid_terms = call(
        lambda me, proj, *refs: project_video(
            me, proj, refs[:vid_count], refs[vid_count], refs[vid_count + 1 :]
        ),
        [shape(vid_rows, step, F32), shape(aud_rows + vid_rows, step)]
        + [shape(vid_rows, step)] * (peers - 2),
        [me, video_proj, *cols, aud_terms[1]],
        in_specs=[smem] + [vmem] * (vid_count + 2),
    )
    vid_got = [vid_terms[0]] + [swap(vid_terms[k], "head", k) for k in range(1, peers)]
    aud_got = [aud_terms[0]] + [swap(aud_terms[k], "head", k) for k in range(2, peers)]
    vid_out, aud_out = call(
        add, [shape(vid_rows, step), shape(aud_rows, step)], vid_got + aud_got
    )
    return aud_out, vid_out


def solution(mesh):
    in_specs = (
        P("seq", "head"),
        P("seq", "head"),
        P("seq", "head"),
        P("seq", "head"),
        P("head", None),
        P("head", None),
    )
    out_specs = (P("seq", "head"), P("seq", "head"))
    return jax.shard_map(
        per_device, mesh=mesh, in_specs=in_specs, out_specs=out_specs, check_vma=False
    )
```

```python
import functools

import jax
import jax.numpy as jnp
from jax import lax
from jax.experimental import pallas as pl
from jax.experimental.pallas import tpu as pltpu
from jax.sharding import PartitionSpec as P

HEAD_DIM = 64
LANES = 128
PIECES = 3
SCALE = HEAD_DIM ** (-0.5)
NEVER = -1e30
VMEM_LIMIT = 48 * 1024 * 1024
COST = 5 * 10**9
BF16 = jnp.bfloat16
F32 = jnp.float32


GATHER_4 = [
    {0: 1, 2: 3},
    {1: 0, 0: 3, 2: 1, 3: 2},
    {0: 2, 3: 0, 1: 3},
    {2: 0, 3: 1, 1: 2},
]
SCATTER_4 = [
    {3: 2, 1: 0},
    {0: 2, 3: 0, 2: 1, 1: 3},
    {0: 3, 3: 1, 2: 0},
    {0: 1, 2: 3, 1: 2},
]


def dot(a, b, contract_a=1, contract_b=0):
    dims = (((contract_a,), (contract_b,)), ((), ()))
    return lax.dot_general(a, b, dims, preferred_element_type=F32)


def split_pieces(value):
    pieces = []
    for _ in range(PIECES):
        piece = value.astype(BF16).astype(F32)
        pieces.append(piece)
        value = value - piece
    return pieces


def head_lanes(rows, width, head):
    return lax.broadcasted_iota(jnp.int32, (rows, width), 1) // HEAD_DIM == head


def pack(aud_ref, aud_val, vid_ref, vid_val, aud, vid, sems):
    width = aud_ref.shape[1]
    copies = [
        pltpu.make_async_copy(source, target.at[:, start : start + width], sems.at[i])
        for i, (source, target, start) in enumerate(
            ((aud_ref, aud, 0), (aud_val, aud, width), (vid_ref, vid, 0), (vid_val, vid, width))
        )
    ]
    for copy in copies:
        copy.start()
    for copy in copies:
        copy.wait()


def lookup(table, index):
    value = jnp.int32(table[0])
    for i, entry in enumerate(table[1:], 1):
        value = jnp.where(index == i, entry, value)
    return value


def sources(step, count):
    back = {target: source for source, target in step.items()}
    return [back.get(i, -1) for i in range(count)]


def targets(step, count):
    return [step.get(i, -1) for i in range(count)]


def attend(aud_count, vid_count, gather, scatter, here, *refs):
    auds, refs = refs[:aud_count], refs[aud_count:]
    gots, mine, refs = refs[: len(gather)], refs[len(gather)], refs[len(gather) + 1 :]
    row_outs, col_outs, (blocks, states) = refs[:aud_count], refs[aud_count:-2], refs[-2:]
    me = here[0]
    blocks[me] = mine[...]
    for step, got in zip(gather, gots):
        source = lookup(sources(step, vid_count), me)

        @pl.when(source >= 0)
        def _():
            blocks[source] = got[...]

    width = auds[0].shape[1] // 2
    heads = width // HEAD_DIM
    aud = jnp.concatenate([ref[...] for ref in auds], axis=0)
    vid = blocks[...].astype(F32).reshape(-1, 2 * width)
    queries, aud_vals = aud[:, :width], aud[:, width:]
    total_aud, total_vid = aud.shape[0], vid.shape[0]
    masks = [head_lanes(total_vid, width, h) for h in range(heads)]
    keys = jnp.concatenate([jnp.where(m, vid[:, :width], 0.0) for m in masks], axis=0)
    vals = jnp.concatenate([jnp.where(m, vid[:, width:], 0.0) for m in masks], axis=0)
    scores = dot(keys.astype(BF16), queries, 1, 1).reshape(heads, total_vid, total_aud)

    row_top = jnp.max(scores, axis=1, keepdims=True)
    row_probs = jnp.exp((scores - row_top) * SCALE)
    row_total = jnp.sum(row_probs, axis=1, keepdims=True)
    row_probs = row_probs.reshape(heads * total_vid, total_aud).astype(BF16)
    row_mix = dot(vals.astype(BF16), row_probs, 0, 0).reshape(heads, HEAD_DIM, total_aud)
    row_mix = (row_mix / row_total).reshape(width, total_aud)
    row_log = (row_top * SCALE + jnp.log(row_total)).reshape(heads, total_aud)
    for i, out in enumerate(row_outs):
        cols = slice(i * out.shape[1], (i + 1) * out.shape[1])
        put_rows(out, row_mix[:, cols], row_log[:, cols])

    col_top = jnp.max(scores, axis=2, keepdims=True)
    col_probs = jnp.exp((scores - col_top) * SCALE)
    col_total = jnp.sum(col_probs, axis=2, keepdims=True)
    col_probs = col_probs.reshape(heads * total_vid, total_aud).astype(BF16)
    every = dot(col_probs, aud_vals).reshape(heads, total_vid, width)
    col_log = col_top * SCALE + jnp.log(col_total)
    col_mix, divisor = every[0], jnp.broadcast_to(col_total[0], (total_vid, width))
    for h in range(1, heads):
        col_mix = jnp.where(masks[h], every[h], col_mix)
        divisor = jnp.where(masks[h], col_total[h], divisor)
    col_mix = col_mix / divisor
    lane = lax.broadcasted_iota(jnp.int32, (total_vid, LANES), 1) % heads
    logs = jnp.broadcast_to(col_log[0], (total_vid, LANES))
    for h in range(1, heads):
        logs = jnp.where(lane == h, col_log[h], logs)
    vid_rows = mine.shape[0]
    for i in range(vid_count):
        rows = slice(i * vid_rows, (i + 1) * vid_rows)
        put_cols(states.at[i], col_mix[rows], logs[rows])
    for step, out in zip(scatter, col_outs):
        out[...] = states[jnp.maximum(lookup(targets(step, vid_count), me), 0)]
    col_outs[-1][...] = states[me]


def put_rows(out, mix, log):
    width, tokens = mix.shape
    pad = jnp.zeros((out.shape[0] - width - PIECES * log.shape[0], tokens), F32)
    out[:width, :] = mix.astype(BF16)
    out[width:, :] = jnp.concatenate(split_pieces(log) + [pad], axis=0).astype(BF16)


def get_rows(ref, width):
    heads, tokens = width // HEAD_DIM, ref.shape[1]
    pieces = ref[width:, :].astype(F32)
    log = pieces[:heads]
    for i in range(1, PIECES):
        log = log + pieces[i * heads : (i + 1) * heads]
    mix = ref[:width, :].astype(F32).reshape(heads, HEAD_DIM, tokens)
    return mix, log.reshape(heads, 1, tokens)


def put_cols(out, mix, logs):
    width = mix.shape[1]
    heads = width // HEAD_DIM
    lane = lax.broadcasted_iota(jnp.int32, logs.shape, 1)
    pieces = split_pieces(logs)
    stats = jnp.zeros_like(logs)
    for i, piece in enumerate(pieces):
        stats = jnp.where(lane // heads == i, piece, stats)
    out[:, :width] = mix.astype(BF16)
    out[:, width:] = stats.astype(BF16)


def get_cols(ref, width):
    heads = width // HEAD_DIM
    source = lax.broadcasted_iota(jnp.int32, (LANES, width), 0)
    target = lax.broadcasted_iota(jnp.int32, (LANES, width), 1)
    spread = (source < PIECES * heads) & (source % heads == target // HEAD_DIM)
    return ref[:, :width].astype(F32), dot(ref[:, width:], spread.astype(BF16))


def merge(states):
    top = states[0][1]
    for _, log in states[1:]:
        top = jnp.maximum(top, log)
    total, mix = 0.0, 0.0
    for part, log in states:
        weight = jnp.exp(log - top)
        total += weight
        mix += weight * part
    return mix / total


def project(mix, proj, me, outs):
    step = outs[0].shape[1]
    for i, out in enumerate(outs):
        block = pl.ds(pl.multiple_of(partner(me, i, len(outs)) * step, step), step)
        out[: mix.shape[0], :] = dot(mix, proj[:, block]).astype(out.dtype)


def project_audio(me, proj, states, outs):
    width = proj.shape[0]
    mix = merge([get_rows(ref, width) for ref in states]).reshape(width, -1)
    project(mix.T.astype(BF16), proj, me[0], outs)


def project_video(vid_count, scatter, me, here, proj, gots, mine, aud_core, outs):
    states = [get_cols(mine, proj.shape[0])]
    for step, got in zip(scatter, gots):
        mix, log = get_cols(got, proj.shape[0])
        sent = lookup(sources(step, vid_count), here[0]) >= 0
        states.append((mix, log + jnp.where(sent, 0.0, NEVER)))
    mix = merge(states)
    aud_rows = aud_core.shape[0]
    outs[1][:aud_rows, :] = aud_core[...]
    project(mix.astype(BF16), proj, me[0], [outs[0], outs[1].at[aud_rows:, :], *outs[2:]])


def add(*refs):
    terms, vid_out, aud_out = refs[:-2], refs[-2], refs[-1]
    count = len(terms) // 2 + 1
    aud_rows = aud_out.shape[0]
    core = terms[count - 1][...].astype(F32)
    vid = terms[0][...] + core[aud_rows:]
    aud = terms[count][...] + core[:aud_rows]
    for vid_term, aud_term in zip(terms[1 : count - 1], terms[count + 1 :]):
        vid += vid_term[...].astype(F32)
        aud += aud_term[:aud_rows].astype(F32)
    vid_out[...] = vid.astype(BF16)
    aud_out[...] = aud.astype(BF16)


def call(body, out_shape, args, in_specs=None, scratch=()):
    vmem = pl.BlockSpec(memory_space=pltpu.VMEM)
    return pl.pallas_call(
        body,
        out_shape=out_shape,
        in_specs=in_specs or [vmem] * len(args),
        out_specs=[vmem] * len(out_shape),
        scratch_shapes=scratch,
        compiler_params=pltpu.CompilerParams(vmem_limit_bytes=VMEM_LIMIT),
        cost_estimate=pl.CostEstimate(flops=COST, bytes_accessed=0, transcendentals=0),
    )(*args)


def partner(index, k, size):
    return index ^ k


def swap(block, axis, distance):
    return lax.ppermute(block, axis, [(i, i ^ distance) for i in range(lax.axis_size(axis))])


def factors(size):
    bits = size.bit_length() - 1
    assert size == 1 << bits
    return 1 << (bits // 2), 1 << (bits - bits // 2)


def gather_plan(count):
    if count == 4:
        return GATHER_4
    return [{i: i ^ k for i in range(count)} for k in range(1, count)]


def scatter_plan(count):
    if count == 4:
        return SCATTER_4
    return [{i: i ^ k for i in range(count)} for k in reversed(range(1, count))]


def move(block, axis, stride, count, step):
    pairs = []
    for i in range(lax.axis_size(axis)):
        here = i // stride % count
        if here in step:
            pairs.append((i, i + (step[here] - here) * stride))
    return lax.ppermute(block, axis, pairs)


def per_device(ref_audio, val_audio, ref_video, val_video, audio_proj, video_proj):
    seq, peers = lax.axis_size("seq"), lax.axis_size("head")
    aud_count, vid_count = factors(seq)
    aud_rows, width = ref_audio.shape
    vid_rows = ref_video.shape[0]
    heads = width // HEAD_DIM
    block = audio_proj.shape[1] // peers
    log_rows = -(-PIECES * heads // 16) * 16

    def shape(rows, cols, dtype=BF16):
        return jax.ShapeDtypeStruct((rows, cols), dtype)

    aud, vid = call(
        pack,
        [shape(aud_rows, 2 * width), shape(vid_rows, 2 * width)],
        [
            pltpu.with_memory_space_constraint(x, pltpu.HBM)
            for x in (ref_audio, val_audio, ref_video, val_video)
        ],
        in_specs=[pl.BlockSpec(memory_space=pltpu.HBM)] * 4,
        scratch=[pltpu.SemaphoreType.DMA((4,))],
    )
    vmem = pl.BlockSpec(memory_space=pltpu.VMEM)
    smem = pl.BlockSpec(memory_space=pltpu.SMEM)
    here = (lax.axis_index("seq") // aud_count).astype(jnp.int32).reshape(1)
    gather, scatter = gather_plan(vid_count), scatter_plan(vid_count)
    auds = [swap(aud, "seq", k) for k in range(1, aud_count)] + [aud]
    vids = [move(vid, "seq", aud_count, vid_count, step) for step in gather]
    state = shape(vid_rows, width + LANES)
    states = call(
        functools.partial(attend, aud_count, vid_count, gather, scatter),
        [shape(width + log_rows, aud_rows)] * aud_count + [state] * (len(scatter) + 1),
        [here, *auds, *vids, vid],
        in_specs=[smem] + [vmem] * (aud_count + len(gather) + 1),
        scratch=[
            pltpu.VMEM((vid_count, *vid.shape), BF16),
            pltpu.VMEM((vid_count, *state.shape), BF16),
        ],
    )
    rows = [swap(states[k - 1], "seq", k) for k in range(1, aud_count)] + [states[aud_count - 1]]
    cols = [
        move(states[aud_count + i], "seq", aud_count, vid_count, step)
        for i, step in enumerate(scatter)
    ] + [states[-1]]
    me = lax.axis_index("head").astype(jnp.int32).reshape(1)

    aud_terms = call(
        lambda me, proj, *refs: project_audio(me, proj, refs[:aud_count], refs[aud_count:]),
        [shape(aud_rows, block, F32), shape(aud_rows, block)]
        + [shape(aud_rows + vid_rows + 8, block)] * (peers - 2),
        [me, audio_proj, *rows],
        in_specs=[smem, vmem] + [vmem] * aud_count,
    )
    vid_terms = call(
        lambda me, here, proj, *refs: project_video(
            vid_count,
            scatter,
            me,
            here,
            proj,
            refs[: len(scatter)],
            refs[len(scatter)],
            refs[len(scatter) + 1],
            refs[len(scatter) + 2 :],
        ),
        [shape(vid_rows, block, F32), shape(aud_rows + vid_rows, block)]
        + [shape(vid_rows, block)] * (peers - 2),
        [me, here, video_proj, *cols, aud_terms[1]],
        in_specs=[smem, smem] + [vmem] * (len(cols) + 2),
    )
    vid_got = [vid_terms[0]] + [
        swap(vid_terms[k], "head", k) for k in reversed(range(1, peers))
    ]
    aud_got = [aud_terms[0]] + [swap(aud_terms[k], "head", k) for k in range(2, peers)]
    vid_out, aud_out = call(
        add, [shape(vid_rows, block), shape(aud_rows, block)], vid_got + aud_got
    )
    return aud_out, vid_out


def solution(mesh):
    in_specs = (
        P("seq", "head"),
        P("seq", "head"),
        P("seq", "head"),
        P("seq", "head"),
        P("head", None),
        P("head", None),
    )
    out_specs = (P("seq", "head"), P("seq", "head"))
    return jax.shard_map(
        per_device, mesh=mesh, in_specs=in_specs, out_specs=out_specs, check_vma=False
    )
```

```python
import functools

import jax
import jax.numpy as jnp
from jax import lax
from jax.experimental import pallas as pl
from jax.experimental.pallas import tpu as pltpu
from jax.sharding import PartitionSpec as P

HEAD_DIM = 64
LANES = 128
PIECES = 3
SCALE = HEAD_DIM ** (-0.5)
NEVER = -1e30
VMEM_LIMIT = 48 * 1024 * 1024
COST = 5 * 10**9
BF16 = jnp.bfloat16
F32 = jnp.float32


GATHER_4 = [
    {0: 1, 1: 0, 2: 3, 3: 2},
    {0: 3, 1: 2, 2: 0, 3: 1},
    {0: 2, 1: 3, 2: 1, 3: 0},
]
SCATTER_4 = [
    {0: 1, 1: 3, 2: 2, 3: 0},
    {0: 2, 1: 1, 2: 0, 3: 3},
    {0: 3, 1: 0, 2: 1, 3: 2},
    {0: 0, 1: 2, 2: 3, 3: 1},
]


def dot(a, b, contract_a=1, contract_b=0):
    dims = (((contract_a,), (contract_b,)), ((), ()))
    return lax.dot_general(a, b, dims, preferred_element_type=F32)


def split_pieces(value):
    pieces = []
    for _ in range(PIECES):
        piece = value.astype(BF16).astype(F32)
        pieces.append(piece)
        value = value - piece
    return pieces


def head_lanes(rows, width, head):
    return lax.broadcasted_iota(jnp.int32, (rows, width), 1) // HEAD_DIM == head


def pack(aud_ref, aud_val, vid_ref, vid_val, aud, vid, sems):
    width = aud_ref.shape[1]
    copies = [
        pltpu.make_async_copy(source, target.at[:, start : start + width], sems.at[i])
        for i, (source, target, start) in enumerate(
            ((aud_ref, aud, 0), (aud_val, aud, width), (vid_ref, vid, 0), (vid_val, vid, width))
        )
    ]
    for copy in copies:
        copy.start()
    for copy in copies:
        copy.wait()


def lookup(table, index):
    value = jnp.int32(table[0])
    for i, entry in enumerate(table[1:], 1):
        value = jnp.where(index == i, entry, value)
    return value


def sources(step):
    return sorted(step, key=step.get)


def targets(step):
    return [step[i] for i in sorted(step)]


def attend(aud_count, vid_count, gather, scatter, here, *refs):
    auds, refs = refs[:aud_count], refs[aud_count:]
    gots, mine, refs = refs[: len(gather)], refs[len(gather)], refs[len(gather) + 1 :]
    row_outs, col_outs, (blocks, states) = refs[:aud_count], refs[aud_count:-2], refs[-2:]
    me = here[0]
    blocks[me] = mine[...]
    for step, got in zip(gather, gots):
        blocks[lookup(sources(step), me)] = got[...]

    width = auds[0].shape[1] // 2
    heads = width // HEAD_DIM
    aud = jnp.concatenate([ref[...] for ref in auds], axis=0)
    vid = blocks[...].astype(F32).reshape(-1, 2 * width)
    queries, aud_vals = aud[:, :width], aud[:, width:]
    total_aud, total_vid = aud.shape[0], vid.shape[0]
    masks = [head_lanes(total_vid, width, h) for h in range(heads)]
    keys = jnp.concatenate([jnp.where(m, vid[:, :width], 0.0) for m in masks], axis=0)
    vals = jnp.concatenate([jnp.where(m, vid[:, width:], 0.0) for m in masks], axis=0)
    scores = dot(keys.astype(BF16), queries, 1, 1).reshape(heads, total_vid, total_aud)

    row_top = jnp.max(scores, axis=1, keepdims=True)
    row_probs = jnp.exp((scores - row_top) * SCALE)
    row_total = jnp.sum(row_probs, axis=1, keepdims=True)
    row_probs = row_probs.reshape(heads * total_vid, total_aud).astype(BF16)
    row_mix = dot(vals.astype(BF16), row_probs, 0, 0).reshape(heads, HEAD_DIM, total_aud)
    row_mix = (row_mix / row_total).reshape(width, total_aud)
    row_log = (row_top * SCALE + jnp.log(row_total)).reshape(heads, total_aud)
    for i, out in enumerate(row_outs):
        cols = slice(i * out.shape[1], (i + 1) * out.shape[1])
        put_rows(out, row_mix[:, cols], row_log[:, cols])

    col_top = jnp.max(scores, axis=2, keepdims=True)
    col_probs = jnp.exp((scores - col_top) * SCALE)
    col_total = jnp.sum(col_probs, axis=2, keepdims=True)
    col_probs = col_probs.reshape(heads * total_vid, total_aud).astype(BF16)
    every = dot(col_probs, aud_vals).reshape(heads, total_vid, width)
    col_log = col_top * SCALE + jnp.log(col_total)
    col_mix, divisor = every[0], jnp.broadcast_to(col_total[0], (total_vid, width))
    for h in range(1, heads):
        col_mix = jnp.where(masks[h], every[h], col_mix)
        divisor = jnp.where(masks[h], col_total[h], divisor)
    col_mix = col_mix / divisor
    lane = lax.broadcasted_iota(jnp.int32, (total_vid, LANES), 1) % heads
    logs = jnp.broadcast_to(col_log[0], (total_vid, LANES))
    for h in range(1, heads):
        logs = jnp.where(lane == h, col_log[h], logs)
    vid_rows = mine.shape[0]
    for i in range(vid_count):
        rows = slice(i * vid_rows, (i + 1) * vid_rows)
        put_cols(states.at[i], col_mix[rows], logs[rows])
    for step, out in zip(scatter, col_outs):
        out[...] = states[lookup(targets(step), me)]
    col_outs[-1][...] = states[me]


def put_rows(out, mix, log):
    width, tokens = mix.shape
    pad = jnp.zeros((out.shape[0] - width - PIECES * log.shape[0], tokens), F32)
    out[:width, :] = mix.astype(BF16)
    out[width:, :] = jnp.concatenate(split_pieces(log) + [pad], axis=0).astype(BF16)


def get_rows(ref, width):
    heads, tokens = width // HEAD_DIM, ref.shape[1]
    pieces = ref[width:, :].astype(F32)
    log = pieces[:heads]
    for i in range(1, PIECES):
        log = log + pieces[i * heads : (i + 1) * heads]
    mix = ref[:width, :].astype(F32).reshape(heads, HEAD_DIM, tokens)
    return mix, log.reshape(heads, 1, tokens)


def put_cols(out, mix, logs):
    width = mix.shape[1]
    heads = width // HEAD_DIM
    lane = lax.broadcasted_iota(jnp.int32, logs.shape, 1)
    pieces = split_pieces(logs)
    stats = jnp.zeros_like(logs)
    for i, piece in enumerate(pieces):
        stats = jnp.where(lane // heads == i, piece, stats)
    out[:, :width] = mix.astype(BF16)
    out[:, width:] = stats.astype(BF16)


def get_cols(ref, width):
    heads = width // HEAD_DIM
    source = lax.broadcasted_iota(jnp.int32, (LANES, width), 0)
    target = lax.broadcasted_iota(jnp.int32, (LANES, width), 1)
    spread = (source < PIECES * heads) & (source % heads == target // HEAD_DIM)
    return ref[:, :width].astype(F32), dot(ref[:, width:], spread.astype(BF16))


def merge(states):
    top = states[0][1]
    for _, log in states[1:]:
        top = jnp.maximum(top, log)
    total, mix = 0.0, 0.0
    for part, log in states:
        weight = jnp.exp(log - top)
        total += weight
        mix += weight * part
    return mix / total


def project(mix, proj, me, outs):
    step = outs[0].shape[1]
    for i, out in enumerate(outs):
        block = pl.ds(pl.multiple_of(partner(me, i, len(outs)) * step, step), step)
        out[: mix.shape[0], :] = dot(mix, proj[:, block]).astype(out.dtype)


def project_audio(me, proj, states, outs):
    width = proj.shape[0]
    mix = merge([get_rows(ref, width) for ref in states]).reshape(width, -1)
    project(mix.T.astype(BF16), proj, me[0], outs)


def project_video(scatter, me, here, proj, gots, mine, aud_core, outs):
    states = [get_cols(mine, proj.shape[0])]
    for step, got in zip(scatter, gots):
        mix, log = get_cols(got, proj.shape[0])
        own = lookup(sources(step), here[0]) == here[0]
        states.append((mix, log + jnp.where(own, NEVER, 0.0)))
    mix = merge(states)
    aud_rows = aud_core.shape[0]
    outs[1][:aud_rows, :] = aud_core[...]
    project(mix.astype(BF16), proj, me[0], [outs[0], outs[1].at[aud_rows:, :], *outs[2:]])


def add(*refs):
    terms, vid_out, aud_out = refs[:-2], refs[-2], refs[-1]
    count = len(terms) // 2 + 1
    aud_rows = aud_out.shape[0]
    core = terms[count - 1][...].astype(F32)
    vid = terms[0][...] + core[aud_rows:]
    aud = terms[count][...] + core[:aud_rows]
    for vid_term, aud_term in zip(terms[1 : count - 1], terms[count + 1 :]):
        vid += vid_term[...].astype(F32)
        aud += aud_term[:aud_rows].astype(F32)
    vid_out[...] = vid.astype(BF16)
    aud_out[...] = aud.astype(BF16)


def call(body, out_shape, args, in_specs=None, scratch=()):
    vmem = pl.BlockSpec(memory_space=pltpu.VMEM)
    return pl.pallas_call(
        body,
        out_shape=out_shape,
        in_specs=in_specs or [vmem] * len(args),
        out_specs=[vmem] * len(out_shape),
        scratch_shapes=scratch,
        compiler_params=pltpu.CompilerParams(vmem_limit_bytes=VMEM_LIMIT),
        cost_estimate=pl.CostEstimate(flops=COST, bytes_accessed=0, transcendentals=0),
    )(*args)


def partner(index, k, size):
    return index ^ k


def swap(block, axis, distance):
    return lax.ppermute(block, axis, [(i, i ^ distance) for i in range(lax.axis_size(axis))])


def factors(size):
    bits = size.bit_length() - 1
    assert size == 1 << bits
    return 1 << (bits // 2), 1 << (bits - bits // 2)


def gather_plan(count):
    if count == 4:
        return GATHER_4
    return [{i: i ^ k for i in range(count)} for k in range(1, count)]


def scatter_plan(count):
    if count == 4:
        return SCATTER_4
    return [{i: i ^ k for i in range(count)} for k in reversed(range(1, count))]


def move(block, axis, stride, count, step):
    pairs = []
    for i in range(lax.axis_size(axis)):
        here = i // stride % count
        pairs.append((i, i + (step[here] - here) * stride))
    return lax.ppermute(block, axis, pairs)


def per_device(ref_audio, val_audio, ref_video, val_video, audio_proj, video_proj):
    seq, peers = lax.axis_size("seq"), lax.axis_size("head")
    aud_count, vid_count = factors(seq)
    aud_rows, width = ref_audio.shape
    vid_rows = ref_video.shape[0]
    heads = width // HEAD_DIM
    block = audio_proj.shape[1] // peers
    log_rows = -(-PIECES * heads // 16) * 16

    def shape(rows, cols, dtype=BF16):
        return jax.ShapeDtypeStruct((rows, cols), dtype)

    aud, vid = call(
        pack,
        [shape(aud_rows, 2 * width), shape(vid_rows, 2 * width)],
        [
            pltpu.with_memory_space_constraint(x, pltpu.HBM)
            for x in (ref_audio, val_audio, ref_video, val_video)
        ],
        in_specs=[pl.BlockSpec(memory_space=pltpu.HBM)] * 4,
        scratch=[pltpu.SemaphoreType.DMA((4,))],
    )
    vmem = pl.BlockSpec(memory_space=pltpu.VMEM)
    smem = pl.BlockSpec(memory_space=pltpu.SMEM)
    here = (lax.axis_index("seq") // aud_count).astype(jnp.int32).reshape(1)
    gather, scatter = gather_plan(vid_count), scatter_plan(vid_count)
    auds = [swap(aud, "seq", k) for k in range(1, aud_count)] + [aud]
    vids = [move(vid, "seq", aud_count, vid_count, step) for step in gather]
    state = shape(vid_rows, width + LANES)
    states = call(
        functools.partial(attend, aud_count, vid_count, gather, scatter),
        [shape(width + log_rows, aud_rows)] * aud_count + [state] * (len(scatter) + 1),
        [here, *auds, *vids, vid],
        in_specs=[smem] + [vmem] * (aud_count + len(gather) + 1),
        scratch=[
            pltpu.VMEM((vid_count, *vid.shape), BF16),
            pltpu.VMEM((vid_count, *state.shape), BF16),
        ],
    )
    rows = [swap(states[k - 1], "seq", k) for k in range(1, aud_count)] + [states[aud_count - 1]]
    cols = [
        move(states[aud_count + i], "seq", aud_count, vid_count, step)
        for i, step in enumerate(scatter)
    ] + [states[-1]]
    me = lax.axis_index("head").astype(jnp.int32).reshape(1)

    aud_terms = call(
        lambda me, proj, *refs: project_audio(me, proj, refs[:aud_count], refs[aud_count:]),
        [shape(aud_rows, block, F32), shape(aud_rows, block)]
        + [shape(aud_rows + vid_rows + 8, block)] * (peers - 2),
        [me, audio_proj, *rows],
        in_specs=[smem, vmem] + [vmem] * aud_count,
    )
    vid_terms = call(
        lambda me, here, proj, *refs: project_video(
            scatter,
            me,
            here,
            proj,
            refs[: len(scatter)],
            refs[len(scatter)],
            refs[len(scatter) + 1],
            refs[len(scatter) + 2 :],
        ),
        [shape(vid_rows, block, F32), shape(aud_rows + vid_rows, block)]
        + [shape(vid_rows, block)] * (peers - 2),
        [me, here, video_proj, *cols, aud_terms[1]],
        in_specs=[smem, smem] + [vmem] * (len(cols) + 2),
    )
    vid_got = [vid_terms[0]] + [
        swap(vid_terms[k], "head", k) for k in reversed(range(1, peers))
    ]
    aud_got = [aud_terms[0]] + [swap(aud_terms[k], "head", k) for k in range(2, peers)]
    vid_out, aud_out = call(
        add, [shape(vid_rows, block), shape(aud_rows, block)], vid_got + aud_got
    )
    return aud_out, vid_out


def solution(mesh):
    in_specs = (
        P("seq", "head"),
        P("seq", "head"),
        P("seq", "head"),
        P("seq", "head"),
        P("head", None),
        P("head", None),
    )
    out_specs = (P("seq", "head"), P("seq", "head"))
    return jax.shard_map(
        per_device, mesh=mesh, in_specs=in_specs, out_specs=out_specs, check_vma=False
    )
```

```python
import functools

import jax
import jax.numpy as jnp
from jax import lax
from jax.experimental import pallas as pl
from jax.experimental.pallas import tpu as pltpu
from jax.sharding import PartitionSpec as P

HEAD_DIM = 64
LANES = 128
PIECES = 3
SCALE = HEAD_DIM ** (-0.5)
VMEM_LIMIT = 48 * 1024 * 1024
COST = 5 * 10**9
BF16 = jnp.bfloat16
F32 = jnp.float32


def dot(a, b, contract_a=1, contract_b=0):
    dims = (((contract_a,), (contract_b,)), ((), ()))
    return lax.dot_general(a, b, dims, preferred_element_type=F32)


def split_pieces(value):
    pieces = []
    for _ in range(PIECES):
        piece = value.astype(BF16).astype(F32)
        pieces.append(piece)
        value = value - piece
    return pieces


def head_lanes(rows, width, head):
    return lax.broadcasted_iota(jnp.int32, (rows, width), 1) // HEAD_DIM == head


def pack(aud_ref, aud_val, vid_ref, vid_val, aud, vid, sems):
    width = aud_ref.shape[1]
    copies = [
        pltpu.make_async_copy(source, target.at[:, start : start + width], sems.at[i])
        for i, (source, target, start) in enumerate(
            ((aud_ref, aud, 0), (aud_val, aud, width), (vid_ref, vid, 0), (vid_val, vid, width))
        )
    ]
    for copy in copies:
        copy.start()
    for copy in copies:
        copy.wait()


def attend(aud_count, vid_count, *refs):
    auds, vids = refs[:aud_count], refs[aud_count : aud_count + vid_count]
    row_outs = refs[aud_count + vid_count : 2 * aud_count + vid_count]
    col_outs = refs[2 * aud_count + vid_count :]
    width = auds[0].shape[1] // 2
    heads = width // HEAD_DIM
    aud = jnp.concatenate([ref[...] for ref in auds], axis=0)
    vid = jnp.concatenate([ref[...] for ref in vids], axis=0).astype(F32)
    queries, aud_vals = aud[:, :width], aud[:, width:]
    total_aud, total_vid = aud.shape[0], vid.shape[0]
    masks = [head_lanes(total_vid, width, h) for h in range(heads)]
    keys = jnp.concatenate([jnp.where(m, vid[:, :width], 0.0) for m in masks], axis=0)
    vals = jnp.concatenate([jnp.where(m, vid[:, width:], 0.0) for m in masks], axis=0)
    scores = dot(keys.astype(BF16), queries, 1, 1).reshape(heads, total_vid, total_aud)

    row_top = jnp.max(scores, axis=1, keepdims=True)
    row_probs = jnp.exp((scores - row_top) * SCALE)
    row_total = jnp.sum(row_probs, axis=1, keepdims=True)
    row_probs = row_probs.reshape(heads * total_vid, total_aud).astype(BF16)
    row_mix = dot(vals.astype(BF16), row_probs, 0, 0).reshape(heads, HEAD_DIM, total_aud)
    row_mix = (row_mix / row_total).reshape(width, total_aud)
    row_log = (row_top * SCALE + jnp.log(row_total)).reshape(heads, total_aud)
    for i, out in enumerate(row_outs):
        cols = slice(i * out.shape[1], (i + 1) * out.shape[1])
        put_rows(out, row_mix[:, cols], row_log[:, cols])

    col_top = jnp.max(scores, axis=2, keepdims=True)
    col_probs = jnp.exp((scores - col_top) * SCALE)
    col_total = jnp.sum(col_probs, axis=2, keepdims=True)
    col_probs = col_probs.reshape(heads * total_vid, total_aud).astype(BF16)
    every = dot(col_probs, aud_vals).reshape(heads, total_vid, width)
    col_log = col_top * SCALE + jnp.log(col_total)
    col_mix, divisor = every[0], jnp.broadcast_to(col_total[0], (total_vid, width))
    for h in range(1, heads):
        col_mix = jnp.where(masks[h], every[h], col_mix)
        divisor = jnp.where(masks[h], col_total[h], divisor)
    col_mix = col_mix / divisor
    lane = lax.broadcasted_iota(jnp.int32, (total_vid, LANES), 1) % heads
    logs = jnp.broadcast_to(col_log[0], (total_vid, LANES))
    for h in range(1, heads):
        logs = jnp.where(lane == h, col_log[h], logs)
    for i, out in enumerate(col_outs):
        rows = slice(i * out.shape[0], (i + 1) * out.shape[0])
        put_cols(out, col_mix[rows], logs[rows])


def put_rows(out, mix, log):
    width, tokens = mix.shape
    pad = jnp.zeros((out.shape[0] - width - PIECES * log.shape[0], tokens), F32)
    out[:width, :] = mix.astype(BF16)
    out[width:, :] = jnp.concatenate(split_pieces(log) + [pad], axis=0).astype(BF16)


def get_rows(ref, width):
    heads, tokens = width // HEAD_DIM, ref.shape[1]
    pieces = ref[width:, :].astype(F32)
    log = pieces[:heads]
    for i in range(1, PIECES):
        log = log + pieces[i * heads : (i + 1) * heads]
    mix = ref[:width, :].astype(F32).reshape(heads, HEAD_DIM, tokens)
    return mix, log.reshape(heads, 1, tokens)


def put_cols(out, mix, logs):
    width = mix.shape[1]
    heads = width // HEAD_DIM
    lane = lax.broadcasted_iota(jnp.int32, logs.shape, 1)
    pieces = split_pieces(logs)
    stats = jnp.zeros_like(logs)
    for i, piece in enumerate(pieces):
        stats = jnp.where(lane // heads == i, piece, stats)
    out[:, :width] = mix.astype(BF16)
    out[:, width:] = stats.astype(BF16)


def get_cols(ref, width):
    heads = width // HEAD_DIM
    source = lax.broadcasted_iota(jnp.int32, (LANES, width), 0)
    target = lax.broadcasted_iota(jnp.int32, (LANES, width), 1)
    spread = (source < PIECES * heads) & (source % heads == target // HEAD_DIM)
    return ref[:, :width].astype(F32), dot(ref[:, width:], spread.astype(BF16))


def merge(states):
    top = states[0][1]
    for _, log in states[1:]:
        top = jnp.maximum(top, log)
    total, mix = 0.0, 0.0
    for part, log in states:
        weight = jnp.exp(log - top)
        total += weight
        mix += weight * part
    return mix / total


def project(mix, proj, me, outs):
    step = outs[0].shape[1]
    for i, out in enumerate(outs):
        block = pl.ds(pl.multiple_of(partner(me, i, len(outs)) * step, step), step)
        out[: mix.shape[0], :] = dot(mix, proj[:, block]).astype(out.dtype)


def project_audio(me, proj, states, outs):
    width = proj.shape[0]
    mix = merge([get_rows(ref, width) for ref in states]).reshape(width, -1)
    project(mix.T.astype(BF16), proj, me[0], outs)


def project_video(me, proj, states, aud_core, outs):
    mix = merge([get_cols(ref, proj.shape[0]) for ref in states])
    aud_rows = aud_core.shape[0]
    outs[1][:aud_rows, :] = aud_core[...]
    project(mix.astype(BF16), proj, me[0], [outs[0], outs[1].at[aud_rows:, :], *outs[2:]])


def add(*refs):
    terms, vid_out, aud_out = refs[:-2], refs[-2], refs[-1]
    count = len(terms) // 2 + 1
    aud_rows = aud_out.shape[0]
    core = terms[count - 1][...].astype(F32)
    vid = terms[0][...] + core[aud_rows:]
    aud = terms[count][...] + core[:aud_rows]
    for vid_term, aud_term in zip(terms[1 : count - 1], terms[count + 1 :]):
        vid += vid_term[...].astype(F32)
        aud += aud_term[:aud_rows].astype(F32)
    vid_out[...] = vid.astype(BF16)
    aud_out[...] = aud.astype(BF16)


def call(body, out_shape, args, in_specs=None, scratch=()):
    vmem = pl.BlockSpec(memory_space=pltpu.VMEM)
    return pl.pallas_call(
        body,
        out_shape=out_shape,
        in_specs=in_specs or [vmem] * len(args),
        out_specs=[vmem] * len(out_shape),
        scratch_shapes=scratch,
        compiler_params=pltpu.CompilerParams(vmem_limit_bytes=VMEM_LIMIT),
        cost_estimate=pl.CostEstimate(flops=COST, bytes_accessed=0, transcendentals=0),
    )(*args)


def partner(index, k, size):
    return index ^ k


def swap(block, axis, distance):
    return lax.ppermute(block, axis, [(i, i ^ distance) for i in range(lax.axis_size(axis))])


def factors(size):
    bits = size.bit_length() - 1
    assert size == 1 << bits
    return 1 << (bits // 2), 1 << (bits - bits // 2)


def per_device(ref_audio, val_audio, ref_video, val_video, audio_proj, video_proj):
    seq, peers = lax.axis_size("seq"), lax.axis_size("head")
    aud_count, vid_count = factors(seq)
    aud_rows, width = ref_audio.shape
    vid_rows = ref_video.shape[0]
    heads = width // HEAD_DIM
    step = audio_proj.shape[1] // peers
    log_rows = -(-PIECES * heads // 16) * 16

    def shape(rows, cols, dtype=BF16):
        return jax.ShapeDtypeStruct((rows, cols), dtype)

    def gather(block, stride, count):
        return [swap(block, "seq", k * stride) for k in range(1, count)] + [block]

    def scatter(blocks, stride):
        count = len(blocks)
        return [swap(blocks[k - 1], "seq", k * stride) for k in reversed(range(1, count))] + [blocks[-1]]

    aud, vid = call(
        pack,
        [shape(aud_rows, 2 * width), shape(vid_rows, 2 * width)],
        [
            pltpu.with_memory_space_constraint(x, pltpu.HBM)
            for x in (ref_audio, val_audio, ref_video, val_video)
        ],
        in_specs=[pl.BlockSpec(memory_space=pltpu.HBM)] * 4,
        scratch=[pltpu.SemaphoreType.DMA((4,))],
    )
    auds, vids = gather(aud, 1, aud_count), gather(vid, aud_count, vid_count)
    states = call(
        functools.partial(attend, aud_count, vid_count),
        [shape(width + log_rows, aud_rows)] * aud_count + [shape(vid_rows, width + LANES)] * vid_count,
        [*auds, *vids],
    )
    rows = scatter(states[:aud_count], 1)
    cols = scatter(states[aud_count:], aud_count)

    me = lax.axis_index("head").astype(jnp.int32).reshape(1)
    vmem = pl.BlockSpec(memory_space=pltpu.VMEM)
    smem = pl.BlockSpec(memory_space=pltpu.SMEM)
    hbm = pl.BlockSpec(memory_space=pl.ANY)

    aud_terms = call(
        lambda me, proj, *refs: project_audio(me, proj, refs[:aud_count], refs[aud_count:]),
        [shape(aud_rows, step, F32), shape(aud_rows, step)]
        + [shape(aud_rows + vid_rows + 8, step)] * (peers - 2),
        [me, audio_proj, *rows],
        in_specs=[smem, vmem] + [vmem] * aud_count,
    )
    vid_terms = call(
        lambda me, proj, *refs: project_video(
            me, proj, refs[:vid_count], refs[vid_count], refs[vid_count + 1 :]
        ),
        [shape(vid_rows, step, F32), shape(aud_rows + vid_rows, step)]
        + [shape(vid_rows, step)] * (peers - 2),
        [me, video_proj, *cols, aud_terms[1]],
        in_specs=[smem] + [vmem] * (vid_count + 2),
    )
    vid_got = [vid_terms[0]] + [
        swap(vid_terms[k], "head", k) for k in reversed(range(1, peers))
    ]
    aud_got = [aud_terms[0]] + [
        swap(aud_terms[k], "head", k) for k in reversed(range(2, peers))
    ]
    vid_out, aud_out = call(
        add, [shape(vid_rows, step), shape(aud_rows, step)], vid_got + aud_got
    )
    return aud_out, vid_out


def solution(mesh):
    in_specs = (
        P("seq", "head"),
        P("seq", "head"),
        P("seq", "head"),
        P("seq", "head"),
        P("head", None),
        P("head", None),
    )
    out_specs = (P("seq", "head"), P("seq", "head"))
    return jax.shard_map(
        per_device, mesh=mesh, in_specs=in_specs, out_specs=out_specs, check_vma=False
    )
```

```python
import functools
import math

import jax
import jax.numpy as jnp
from jax import lax
from jax.experimental import pallas as pl
from jax.experimental.pallas import tpu as pltpu
from jax.sharding import PartitionSpec as P

HEAD_DIM = 64
LANES = 128
PIECES = 3
SCALE = HEAD_DIM ** (-0.5) * math.log2(math.e)
VMEM_LIMIT = 48 * 1024 * 1024
COST = 5 * 10**9
BF16 = jnp.bfloat16
F32 = jnp.float32


def dot(a, b, contract_a=1, contract_b=0):
    dims = (((contract_a,), (contract_b,)), ((), ()))
    return lax.dot_general(a, b, dims, preferred_element_type=F32)


def split_pieces(value):
    pieces = []
    for _ in range(PIECES):
        piece = value.astype(BF16).astype(F32)
        pieces.append(piece)
        value = value - piece
    return pieces


def head_lanes(rows, width, head):
    return lax.broadcasted_iota(jnp.int32, (rows, width), 1) // HEAD_DIM == head


def pack(aud_ref, aud_val, vid_ref, vid_val, aud, vid, sems):
    pairs = ((aud_ref, aud.at[0]), (aud_val, aud.at[1]), (vid_ref, vid.at[0]), (vid_val, vid.at[1]))
    copies = [pltpu.make_async_copy(a, b, sems.at[i]) for i, (a, b) in enumerate(pairs)]
    for copy in copies:
        copy.start()
    for copy in copies:
        copy.wait()


def attend(aud_count, vid_count, *refs):
    auds, vids = refs[:aud_count], refs[aud_count : aud_count + vid_count]
    row_outs = refs[aud_count + vid_count : 2 * aud_count + vid_count]
    col_outs = refs[2 * aud_count + vid_count :]
    width = auds[0].shape[2]
    heads = width // HEAD_DIM
    queries, aud_vals = (jnp.concatenate([ref[i] for ref in auds], axis=0) for i in range(2))
    vid_refs, vid_vals = (
        jnp.concatenate([ref[i].astype(F32) for ref in vids], axis=0) for i in range(2)
    )
    total_aud, total_vid = queries.shape[0], vid_refs.shape[0]
    masks = [head_lanes(total_vid, width, h) for h in range(heads)]
    lanes = [head_lanes(1, width, h).astype(F32).astype(BF16) for h in range(heads)]
    keys = vid_refs.astype(BF16)
    keys = jnp.concatenate([keys * lane for lane in lanes], axis=0)
    scores = dot(keys, queries, 1, 1).reshape(heads, total_vid, total_aud)

    row_top = jnp.max(scores, axis=1, keepdims=True)
    row_probs = jnp.exp2((scores - row_top) * SCALE)
    row_total = jnp.sum(row_probs, axis=1, keepdims=True)
    row_probs = row_probs.astype(BF16)
    vals = vid_vals.T.astype(BF16)
    row_mix = [
        dot(vals[h * HEAD_DIM : (h + 1) * HEAD_DIM], row_probs[h]) * (1.0 / row_total[h])
        for h in range(heads)
    ]
    row_mix = jnp.concatenate(row_mix, axis=0)
    row_log = (row_top * SCALE + jnp.log2(row_total)).reshape(heads, total_aud)
    for i, out in enumerate(row_outs):
        cols = slice(i * out.shape[1], (i + 1) * out.shape[1])
        put_rows(out, row_mix[:, cols], row_log[:, cols])

    col_top = jnp.max(scores, axis=2, keepdims=True)
    col_probs = jnp.exp2((scores - col_top) * SCALE)
    col_total = jnp.sum(col_probs, axis=2, keepdims=True)
    col_probs = col_probs.reshape(heads * total_vid, total_aud).astype(BF16)
    every = dot(col_probs, aud_vals).reshape(heads, total_vid, width)
    col_log = col_top * SCALE + jnp.log2(col_total)
    col_mix, divisor = every[0], jnp.broadcast_to(col_total[0], (total_vid, width))
    for h in range(1, heads):
        col_mix = jnp.where(masks[h], every[h], col_mix)
        divisor = jnp.where(masks[h], col_total[h], divisor)
    col_mix = col_mix / divisor
    lane = lax.broadcasted_iota(jnp.int32, (total_vid, LANES), 1) % heads
    logs = jnp.broadcast_to(col_log[0], (total_vid, LANES))
    for h in range(1, heads):
        logs = jnp.where(lane == h, col_log[h], logs)
    for i, out in enumerate(col_outs):
        rows = slice(i * out.shape[0], (i + 1) * out.shape[0])
        put_cols(out, col_mix[rows], logs[rows])


def put_rows(out, mix, log):
    width, tokens = mix.shape
    pad = jnp.zeros((out.shape[0] - width - PIECES * log.shape[0], tokens), F32)
    out[:width, :] = mix.astype(BF16)
    out[width:, :] = jnp.concatenate(split_pieces(log) + [pad], axis=0).astype(BF16)


def get_rows(ref, width):
    heads, tokens = width // HEAD_DIM, ref.shape[1]
    pieces = ref[width:, :].astype(F32)
    log = pieces[:heads]
    for i in range(1, PIECES):
        log = log + pieces[i * heads : (i + 1) * heads]
    mix = ref[:width, :].astype(F32).reshape(heads, HEAD_DIM, tokens)
    return mix, log.reshape(heads, 1, tokens)


def put_cols(out, mix, logs):
    width = mix.shape[1]
    heads = width // HEAD_DIM
    lane = lax.broadcasted_iota(jnp.int32, logs.shape, 1)
    pieces = split_pieces(logs)
    stats = jnp.zeros_like(logs)
    for i, piece in enumerate(pieces):
        stats = jnp.where(lane // heads == i, piece, stats)
    out[:, :width] = mix.astype(BF16)
    out[:, width:] = stats.astype(BF16)


def get_cols(ref, width):
    heads = width // HEAD_DIM
    source = lax.broadcasted_iota(jnp.int32, (LANES, width), 0)
    target = lax.broadcasted_iota(jnp.int32, (LANES, width), 1)
    spread = (source < PIECES * heads) & (source % heads == target // HEAD_DIM)
    return ref[:, :width].astype(F32), dot(ref[:, width:], spread.astype(BF16))


def merge(states):
    top = states[0][1]
    for _, log in states[1:]:
        top = jnp.maximum(top, log)
    total, mix = 0.0, 0.0
    for part, log in states:
        weight = jnp.exp2(log - top)
        total += weight
        mix += weight * part
    return mix / total


def project(mix, proj, me, outs):
    step = outs[0].shape[1]
    for i, out in enumerate(outs):
        block = pl.ds(pl.multiple_of(partner(me, i, len(outs)) * step, step), step)
        out[: mix.shape[0], :] = dot(mix, proj[:, block]).astype(out.dtype)


def project_audio(me, proj, states, outs):
    width = proj.shape[0]
    mix = merge([get_rows(ref, width) for ref in states]).reshape(width, -1)
    project(mix.T.astype(BF16), proj, me[0], outs)


def project_video(me, proj, states, aud_core, outs):
    mix = merge([get_cols(ref, proj.shape[0]) for ref in states])
    aud_rows = aud_core.shape[0]
    outs[1][:aud_rows, :] = aud_core[...]
    project(mix.astype(BF16), proj, me[0], [outs[0], outs[1].at[aud_rows:, :], *outs[2:]])


def add(*refs):
    terms, vid_out, aud_out = refs[:-2], refs[-2], refs[-1]
    count = len(terms) // 2 + 1
    aud_rows = aud_out.shape[0]
    core = terms[count - 1][...].astype(F32)
    vid = terms[0][...] + core[aud_rows:]
    aud = terms[count][...] + core[:aud_rows]
    for vid_term, aud_term in zip(terms[1 : count - 1], terms[count + 1 :]):
        vid += vid_term[...].astype(F32)
        aud += aud_term[:aud_rows].astype(F32)
    vid_out[...] = vid.astype(BF16)
    aud_out[...] = aud.astype(BF16)


def call(body, out_shape, args, in_specs=None, scratch=()):
    vmem = pl.BlockSpec(memory_space=pltpu.VMEM)
    return pl.pallas_call(
        body,
        out_shape=out_shape,
        in_specs=in_specs or [vmem] * len(args),
        out_specs=[vmem] * len(out_shape),
        scratch_shapes=scratch,
        compiler_params=pltpu.CompilerParams(vmem_limit_bytes=VMEM_LIMIT),
        cost_estimate=pl.CostEstimate(flops=COST, bytes_accessed=0, transcendentals=0),
    )(*args)


def partner(index, k, size):
    return index ^ k


def swap(block, axis, distance):
    return lax.ppermute(block, axis, [(i, i ^ distance) for i in range(lax.axis_size(axis))])


def factors(size):
    bits = size.bit_length() - 1
    assert size == 1 << bits
    return 1 << (bits // 2), 1 << (bits - bits // 2)


def per_device(ref_audio, val_audio, ref_video, val_video, audio_proj, video_proj):
    seq, peers = lax.axis_size("seq"), lax.axis_size("head")
    aud_count, vid_count = factors(seq)
    aud_rows, width = ref_audio.shape
    vid_rows = ref_video.shape[0]
    heads = width // HEAD_DIM
    step = audio_proj.shape[1] // peers
    log_rows = -(-PIECES * heads // 16) * 16

    def shape(*dims, dtype=BF16):
        return jax.ShapeDtypeStruct(dims, dtype)

    def gather(block, stride, count):
        return [swap(block, "seq", k * stride) for k in range(1, count)] + [block]

    def scatter(blocks, stride):
        count = len(blocks)
        return [swap(blocks[k - 1], "seq", k * stride) for k in reversed(range(1, count))] + [blocks[-1]]

    aud, vid = call(
        pack,
        [shape(2, aud_rows, width), shape(2, vid_rows, width)],
        [
            pltpu.with_memory_space_constraint(x, pltpu.HBM)
            for x in (ref_audio, val_audio, ref_video, val_video)
        ],
        in_specs=[pl.BlockSpec(memory_space=pltpu.HBM)] * 4,
        scratch=[pltpu.SemaphoreType.DMA((4,))],
    )
    auds, vids = gather(aud, 1, aud_count), gather(vid, aud_count, vid_count)
    states = call(
        functools.partial(attend, aud_count, vid_count),
        [shape(width + log_rows, aud_rows)] * aud_count + [shape(vid_rows, width + LANES)] * vid_count,
        [*auds, *vids],
    )
    rows = scatter(states[:aud_count], 1)
    cols = scatter(states[aud_count:], aud_count)

    me = lax.axis_index("head").astype(jnp.int32).reshape(1)
    vmem = pl.BlockSpec(memory_space=pltpu.VMEM)
    smem = pl.BlockSpec(memory_space=pltpu.SMEM)
    hbm = pl.BlockSpec(memory_space=pl.ANY)

    aud_terms = call(
        lambda me, proj, *refs: project_audio(me, proj, refs[:aud_count], refs[aud_count:]),
        [shape(aud_rows, step, dtype=F32), shape(aud_rows, step)]
        + [shape(aud_rows + vid_rows + 8, step)] * (peers - 2),
        [me, audio_proj, *rows],
        in_specs=[smem, vmem] + [vmem] * aud_count,
    )
    vid_terms = call(
        lambda me, proj, *refs: project_video(
            me, proj, refs[:vid_count], refs[vid_count], refs[vid_count + 1 :]
        ),
        [shape(vid_rows, step, dtype=F32), shape(aud_rows + vid_rows, step)]
        + [shape(vid_rows, step)] * (peers - 2),
        [me, video_proj, *cols, aud_terms[1]],
        in_specs=[smem] + [vmem] * (vid_count + 2),
    )
    vid_got = [vid_terms[0]] + [
        swap(vid_terms[k], "head", k) for k in reversed(range(1, peers))
    ]
    aud_got = [aud_terms[0]] + [
        swap(aud_terms[k], "head", k) for k in reversed(range(2, peers))
    ]
    vid_out, aud_out = call(
        add, [shape(vid_rows, step), shape(aud_rows, step)], vid_got + aud_got
    )
    return aud_out, vid_out


def solution(mesh):
    in_specs = (
        P("seq", "head"),
        P("seq", "head"),
        P("seq", "head"),
        P("seq", "head"),
        P("head", None),
        P("head", None),
    )
    out_specs = (P("seq", "head"), P("seq", "head"))
    return jax.shard_map(
        per_device, mesh=mesh, in_specs=in_specs, out_specs=out_specs, check_vma=False
    )
```

```python
import functools
import math

import jax
import jax.numpy as jnp
from jax import lax
from jax.experimental import pallas as pl
from jax.experimental.pallas import tpu as pltpu
from jax.sharding import PartitionSpec as P

HEAD_DIM = 64
LANES = 128
PIECES = 3
SCALE = HEAD_DIM ** (-0.5) * math.log2(math.e)
VMEM_LIMIT = 48 * 1024 * 1024
COST = 5 * 10**9
COST_A = 10**9
BF16 = jnp.bfloat16
F32 = jnp.float32


def dot(a, b, contract_a=1, contract_b=0):
    dims = (((contract_a,), (contract_b,)), ((), ()))
    return lax.dot_general(a, b, dims, preferred_element_type=F32)


def split_pieces(value):
    pieces = []
    for _ in range(PIECES):
        piece = value.astype(BF16).astype(F32)
        pieces.append(piece)
        value = value - piece
    return pieces


def head_lanes(rows, width, head):
    return lax.broadcasted_iota(jnp.int32, (rows, width), 1) // HEAD_DIM == head


def pack(aud_ref, aud_val, vid_ref, vid_val, aud, vid, sems):
    pairs = ((aud_ref, aud.at[0]), (aud_val, aud.at[1]), (vid_ref, vid.at[0]), (vid_val, vid.at[1]))
    copies = [pltpu.make_async_copy(a, b, sems.at[i]) for i, (a, b) in enumerate(pairs)]
    for copy in copies:
        copy.start()
    for copy in copies:
        copy.wait()


def tile_scores(queries, vids):
    total_vid, width = sum(ref.shape[1] for ref in vids), queries.shape[1]
    heads = width // HEAD_DIM
    keys = jnp.concatenate([ref[0].astype(F32) for ref in vids], axis=0).astype(BF16)
    lanes = [head_lanes(1, width, h).astype(F32).astype(BF16) for h in range(heads)]
    keys = jnp.concatenate([keys * lane for lane in lanes], axis=0)
    return dot(keys, queries, 1, 1).reshape(heads, total_vid, queries.shape[0])


def both(auds):
    return (jnp.concatenate([ref[i] for ref in auds], axis=0) for i in range(2))


def column_states(scores, aud_vals, outs):
    heads, total_vid, total_aud = scores.shape
    width = heads * HEAD_DIM
    top = jnp.max(scores, axis=2, keepdims=True)
    probs = jnp.exp2((scores - top) * SCALE)
    total = jnp.sum(probs, axis=2, keepdims=True)
    probs = probs.reshape(heads * total_vid, total_aud).astype(BF16)
    every = dot(probs, aud_vals).reshape(heads, total_vid, width)
    log = top * SCALE + jnp.log2(total)
    lane = lax.broadcasted_iota(jnp.int32, (total_vid, LANES), 1) % heads
    mix, divisor = every[0], jnp.broadcast_to(total[0], (total_vid, width))
    logs = jnp.broadcast_to(log[0], (total_vid, LANES))
    for h in range(1, heads):
        mask = head_lanes(total_vid, width, h)
        mix = jnp.where(mask, every[h], mix)
        divisor = jnp.where(mask, total[h], divisor)
        logs = jnp.where(lane == h, log[h], logs)
    mix = mix / divisor
    for i, out in enumerate(outs):
        rows = slice(i * out.shape[0], (i + 1) * out.shape[0])
        put_cols(out, mix[rows], logs[rows])


def row_states(scores, vid_vals, outs):
    heads, _, total_aud = scores.shape
    top = jnp.max(scores, axis=1, keepdims=True)
    probs = jnp.exp2((scores - top) * SCALE)
    total = jnp.sum(probs, axis=1, keepdims=True)
    probs = probs.astype(BF16)
    vals = vid_vals.T.astype(BF16)
    mix = [
        dot(vals[h * HEAD_DIM : (h + 1) * HEAD_DIM], probs[h]) * (1.0 / total[h])
        for h in range(heads)
    ]
    mix = jnp.concatenate(mix, axis=0)
    log = (top * SCALE + jnp.log2(total)).reshape(heads, total_aud)
    for i, out in enumerate(outs):
        cols = slice(i * out.shape[1], (i + 1) * out.shape[1])
        put_rows(out, mix[:, cols], log[:, cols])


def attend_first(*refs):
    *auds, vid, col_out, scores_out = refs
    queries, aud_vals = both(auds)
    scores = tile_scores(queries, [vid])
    scores_out[...] = scores
    column_states(scores, aud_vals, [col_out])


def attend(aud_count, vid_count, *refs):
    auds, vids, refs = refs[:aud_count], refs[aud_count : aud_count + vid_count], refs[aud_count + vid_count :]
    first, first_scores, row_outs, col_outs = refs[0], refs[1], refs[2 : 2 + aud_count], refs[2 + aud_count :]
    queries, aud_vals = both(auds)
    scores = tile_scores(queries, vids)
    column_states(scores, aud_vals, col_outs)
    vals = jnp.concatenate([ref[1].astype(F32) for ref in (first, *vids)], axis=0)
    row_states(jnp.concatenate([first_scores[...], scores], axis=1), vals, row_outs)


def put_rows(out, mix, log):
    width, tokens = mix.shape
    pad = jnp.zeros((out.shape[0] - width - PIECES * log.shape[0], tokens), F32)
    out[:width, :] = mix.astype(BF16)
    out[width:, :] = jnp.concatenate(split_pieces(log) + [pad], axis=0).astype(BF16)


def get_rows(ref, width):
    heads, tokens = width // HEAD_DIM, ref.shape[1]
    pieces = ref[width:, :].astype(F32)
    log = pieces[:heads]
    for i in range(1, PIECES):
        log = log + pieces[i * heads : (i + 1) * heads]
    mix = ref[:width, :].astype(F32).reshape(heads, HEAD_DIM, tokens)
    return mix, log.reshape(heads, 1, tokens)


def put_cols(out, mix, logs):
    width = mix.shape[1]
    heads = width // HEAD_DIM
    lane = lax.broadcasted_iota(jnp.int32, logs.shape, 1)
    pieces = split_pieces(logs)
    stats = jnp.zeros_like(logs)
    for i, piece in enumerate(pieces):
        stats = jnp.where(lane // heads == i, piece, stats)
    out[:, :width] = mix.astype(BF16)
    out[:, width:] = stats.astype(BF16)


def get_cols(ref, width):
    heads = width // HEAD_DIM
    source = lax.broadcasted_iota(jnp.int32, (LANES, width), 0)
    target = lax.broadcasted_iota(jnp.int32, (LANES, width), 1)
    spread = (source < PIECES * heads) & (source % heads == target // HEAD_DIM)
    return ref[:, :width].astype(F32), dot(ref[:, width:], spread.astype(BF16))


def merge(states):
    top = states[0][1]
    for _, log in states[1:]:
        top = jnp.maximum(top, log)
    total, mix = 0.0, 0.0
    for part, log in states:
        weight = jnp.exp2(log - top)
        total += weight
        mix += weight * part
    return mix / total


def project(mix, proj, me, outs):
    step = outs[0].shape[1]
    for i, out in enumerate(outs):
        block = pl.ds(pl.multiple_of(partner(me, i, len(outs)) * step, step), step)
        out[: mix.shape[0], :] = dot(mix, proj[:, block]).astype(out.dtype)


def project_audio(me, proj, states, outs):
    width = proj.shape[0]
    mix = merge([get_rows(ref, width) for ref in states]).reshape(width, -1)
    project(mix.T.astype(BF16), proj, me[0], outs)


def merge_first(mine, got, _, mix_out, log_out):
    states = [get_cols(ref, mix_out.shape[1]) for ref in (mine, got)]
    top = jnp.maximum(states[0][1], states[1][1])
    weights = [jnp.exp2(log - top) for _, log in states]
    total = weights[0] + weights[1]
    mix_out[...] = (weights[0] * states[0][0] + weights[1] * states[1][0]) / total
    log_out[...] = top + jnp.log2(total)


def project_video(me, proj, mix_log, states, aud_core, outs):
    mix = merge([tuple(ref[...] for ref in mix_log)] + [get_cols(ref, proj.shape[0]) for ref in states])
    aud_rows = aud_core.shape[0]
    outs[1][:aud_rows, :] = aud_core[...]
    project(mix.astype(BF16), proj, me[0], [outs[0], outs[1].at[aud_rows:, :], *outs[2:]])


def add(*refs):
    terms, vid_out, aud_out = refs[:-2], refs[-2], refs[-1]
    count = len(terms) // 2 + 1
    aud_rows = aud_out.shape[0]
    core = terms[count - 1][...].astype(F32)
    vid = terms[0][...] + core[aud_rows:]
    aud = terms[count][...] + core[:aud_rows]
    for vid_term, aud_term in zip(terms[1 : count - 1], terms[count + 1 :]):
        vid += vid_term[...].astype(F32)
        aud += aud_term[:aud_rows].astype(F32)
    vid_out[...] = vid.astype(BF16)
    aud_out[...] = aud.astype(BF16)


def call(body, out_shape, args, in_specs=None, scratch=(), cost=COST):
    vmem = pl.BlockSpec(memory_space=pltpu.VMEM)
    return pl.pallas_call(
        body,
        out_shape=out_shape,
        in_specs=in_specs or [vmem] * len(args),
        out_specs=[vmem] * len(out_shape),
        scratch_shapes=scratch,
        compiler_params=pltpu.CompilerParams(vmem_limit_bytes=VMEM_LIMIT),
        cost_estimate=pl.CostEstimate(flops=cost, bytes_accessed=0, transcendentals=0),
    )(*args)


def partner(index, k, size):
    return index ^ k


def swap(block, axis, distance):
    return lax.ppermute(block, axis, [(i, i ^ distance) for i in range(lax.axis_size(axis))])


def factors(size):
    bits = size.bit_length() - 1
    assert size == 1 << bits
    return 1 << (bits // 2), 1 << (bits - bits // 2)


def per_device(ref_audio, val_audio, ref_video, val_video, audio_proj, video_proj):
    seq, peers = lax.axis_size("seq"), lax.axis_size("head")
    aud_count, vid_count = factors(seq)
    aud_rows, width = ref_audio.shape
    vid_rows = ref_video.shape[0]
    heads = width // HEAD_DIM
    step = audio_proj.shape[1] // peers
    log_rows = -(-PIECES * heads // 16) * 16

    def shape(*dims, dtype=BF16):
        return jax.ShapeDtypeStruct(dims, dtype)

    aud, vid = call(
        pack,
        [shape(2, aud_rows, width), shape(2, vid_rows, width)],
        [
            pltpu.with_memory_space_constraint(x, pltpu.HBM)
            for x in (ref_audio, val_audio, ref_video, val_video)
        ],
        in_specs=[pl.BlockSpec(memory_space=pltpu.HBM)] * 4,
        scratch=[pltpu.SemaphoreType.DMA((4,))],
    )
    early = vid_count // 2
    late = [k for k in reversed(range(1, vid_count)) if k != early]
    auds = [swap(aud, "seq", k) for k in range(1, aud_count)] + [aud]
    vids = {k: swap(vid, "seq", k * aud_count) for k in (early, *late)}
    state = shape(vid_rows, width + LANES)
    first_state, scores = call(
        attend_first,
        [state, shape(heads, vid_rows, aud_count * aud_rows, dtype=F32)],
        [*auds, vids[early]],
    )
    states = call(
        functools.partial(attend, aud_count, len(late) + 1),
        [shape(width + log_rows, aud_rows)] * aud_count + [state] * (len(late) + 1),
        [*auds, *(vids[k] for k in late), vid, vids[early], scores],
    )
    rows = [swap(states[k - 1], "seq", k) for k in range(1, aud_count)] + [states[aud_count - 1]]
    states = dict(zip((early, *late, 0), (first_state, *states[aud_count:])))
    cols = [swap(states[k], "seq", k * aud_count) for k in (early, *late)] + [states[0]]

    me = lax.axis_index("head").astype(jnp.int32).reshape(1)
    vmem = pl.BlockSpec(memory_space=pltpu.VMEM)
    smem = pl.BlockSpec(memory_space=pltpu.SMEM)
    hbm = pl.BlockSpec(memory_space=pl.ANY)

    mix_log = call(
        merge_first, [shape(vid_rows, width, dtype=F32)] * 2, [cols.pop(), cols.pop(0), audio_proj]
    )
    aud_terms = call(
        lambda me, proj, *refs: project_audio(me, proj, refs[:aud_count], refs[aud_count + 1 :]),
        [shape(aud_rows, step, dtype=F32), shape(aud_rows, step)]
        + [shape(aud_rows + vid_rows + 8, step)] * (peers - 2),
        [me, audio_proj, *rows, mix_log[0]],
        in_specs=[smem, vmem] + [vmem] * aud_count + [pl.BlockSpec(memory_space=pl.ANY)],
        cost=COST_A,
    )
    vid_terms = call(
        lambda me, proj, mix, log, core, *refs: project_video(
            me, proj, (mix, log), refs[: len(cols)], core, refs[len(cols) :]
        ),
        [shape(vid_rows, step, dtype=F32), shape(aud_rows + vid_rows, step)]
        + [shape(vid_rows, step)] * (peers - 2),
        [me, video_proj, *mix_log, aud_terms[1], *cols],
        in_specs=[smem] + [vmem] * (len(cols) + 4),
    )
    vid_got = [vid_terms[0]] + [
        swap(vid_terms[k], "head", k) for k in (*range(2, peers), 1)
    ]
    aud_got = [aud_terms[0]] + [
        swap(aud_terms[k], "head", k) for k in reversed(range(2, peers))
    ]
    vid_out, aud_out = call(
        add, [shape(vid_rows, step), shape(aud_rows, step)], vid_got + aud_got
    )
    return aud_out, vid_out


def solution(mesh):
    in_specs = (
        P("seq", "head"),
        P("seq", "head"),
        P("seq", "head"),
        P("seq", "head"),
        P("head", None),
        P("head", None),
    )
    out_specs = (P("seq", "head"), P("seq", "head"))
    return jax.shard_map(
        per_device, mesh=mesh, in_specs=in_specs, out_specs=out_specs, check_vma=False
    )
```

```python
import functools
import math

import jax
import jax.numpy as jnp
from jax import lax
from jax.experimental import pallas as pl
from jax.experimental.pallas import tpu as pltpu
from jax.sharding import PartitionSpec as P

HEAD_DIM = 64
LANES = 128
PIECES = 3
SCALE = HEAD_DIM ** (-0.5) * math.log2(math.e)
VMEM_LIMIT = 48 * 1024 * 1024
COST = 5 * 10**9
COST_A = 10**9
BF16 = jnp.bfloat16
F32 = jnp.float32


def dot(a, b, contract_a=1, contract_b=0):
    dims = (((contract_a,), (contract_b,)), ((), ()))
    return lax.dot_general(a, b, dims, preferred_element_type=F32)


def split_pieces(value):
    pieces = []
    for _ in range(PIECES):
        piece = value.astype(BF16).astype(F32)
        pieces.append(piece)
        value = value - piece
    return pieces


def head_lanes(rows, width, head):
    return lax.broadcasted_iota(jnp.int32, (rows, width), 1) // HEAD_DIM == head


def pack(aud_ref, aud_val, vid_ref, vid_val, aud, vid, sems):
    pairs = ((aud_ref, aud.at[0]), (aud_val, aud.at[1]), (vid_ref, vid.at[0]), (vid_val, vid.at[1]))
    copies = [pltpu.make_async_copy(a, b, sems.at[i]) for i, (a, b) in enumerate(pairs)]
    for copy in copies:
        copy.start()
    for copy in copies:
        copy.wait()


def tile_scores(queries, vids):
    total_vid, width = sum(ref.shape[1] for ref in vids), queries.shape[1]
    heads = width // HEAD_DIM
    keys = jnp.concatenate([ref[0].astype(F32) for ref in vids], axis=0).astype(BF16)
    lanes = [head_lanes(1, width, h).astype(F32).astype(BF16) for h in range(heads)]
    keys = jnp.concatenate([keys * lane for lane in lanes], axis=0)
    return dot(keys, queries, 1, 1).reshape(heads, total_vid, queries.shape[0])


def both(auds):
    return (jnp.concatenate([ref[i] for ref in auds], axis=0) for i in range(2))


def column_states(scores, aud_vals, outs):
    heads, total_vid, total_aud = scores.shape
    width = heads * HEAD_DIM
    top = jnp.max(scores, axis=2, keepdims=True)
    probs = jnp.exp2((scores - top) * SCALE)
    total = jnp.sum(probs, axis=2, keepdims=True)
    probs = probs.reshape(heads * total_vid, total_aud).astype(BF16)
    every = dot(probs, aud_vals).reshape(heads, total_vid, width)
    log = top * SCALE + jnp.log2(total)
    lane = lax.broadcasted_iota(jnp.int32, (total_vid, LANES), 1) % heads
    mix, divisor = every[0], jnp.broadcast_to(total[0], (total_vid, width))
    logs = jnp.broadcast_to(log[0], (total_vid, LANES))
    for h in range(1, heads):
        mask = head_lanes(total_vid, width, h)
        mix = jnp.where(mask, every[h], mix)
        divisor = jnp.where(mask, total[h], divisor)
        logs = jnp.where(lane == h, log[h], logs)
    mix = mix / divisor
    for i, out in enumerate(outs):
        rows = slice(i * out.shape[0], (i + 1) * out.shape[0])
        put_cols(out, mix[rows], logs[rows])


def row_states(scores, vid_vals, outs):
    heads, _, total_aud = scores.shape
    top = jnp.max(scores, axis=1, keepdims=True)
    probs = jnp.exp2((scores - top) * SCALE)
    total = jnp.sum(probs, axis=1, keepdims=True)
    probs = probs.astype(BF16)
    vals = vid_vals.T.astype(BF16)
    mix = [
        dot(vals[h * HEAD_DIM : (h + 1) * HEAD_DIM], probs[h]) * (1.0 / total[h])
        for h in range(heads)
    ]
    mix = jnp.concatenate(mix, axis=0)
    log = (top * SCALE + jnp.log2(total)).reshape(heads, total_aud)
    for i, out in enumerate(outs):
        cols = slice(i * out.shape[1], (i + 1) * out.shape[1])
        put_rows(out, mix[:, cols], log[:, cols])


def attend_first(*refs):
    *auds, vid, col_out, scores_out = refs
    queries, aud_vals = both(auds)
    scores = tile_scores(queries, [vid])
    scores_out[...] = scores
    column_states(scores, aud_vals, [col_out])


def attend(aud_count, vid_count, *refs):
    auds, vids, refs = refs[:aud_count], refs[aud_count : aud_count + vid_count], refs[aud_count + vid_count :]
    first, first_scores, row_outs, col_outs = refs[0], refs[1], refs[2 : 2 + aud_count], refs[2 + aud_count :]
    queries, aud_vals = both(auds)
    scores = tile_scores(queries, vids)
    column_states(scores, aud_vals, col_outs)
    vals = jnp.concatenate([ref[1].astype(F32) for ref in (first, *vids)], axis=0)
    row_states(jnp.concatenate([first_scores[...], scores], axis=1), vals, row_outs)


def put_rows(out, mix, log):
    width, tokens = mix.shape
    pad = jnp.zeros((out.shape[0] - width - PIECES * log.shape[0], tokens), F32)
    out[:width, :] = mix.astype(BF16)
    out[width:, :] = jnp.concatenate(split_pieces(log) + [pad], axis=0).astype(BF16)


def get_rows(ref, width):
    heads, tokens = width // HEAD_DIM, ref.shape[1]
    pieces = ref[width:, :].astype(F32)
    log = pieces[:heads]
    for i in range(1, PIECES):
        log = log + pieces[i * heads : (i + 1) * heads]
    mix = ref[:width, :].astype(F32).reshape(heads, HEAD_DIM, tokens)
    return mix, log.reshape(heads, 1, tokens)


def put_cols(out, mix, logs):
    width = mix.shape[1]
    heads = width // HEAD_DIM
    lane = lax.broadcasted_iota(jnp.int32, logs.shape, 1)
    pieces = split_pieces(logs)
    stats = jnp.zeros_like(logs)
    for i, piece in enumerate(pieces):
        stats = jnp.where(lane // heads == i, piece, stats)
    out[:, :width] = mix.astype(BF16)
    out[:, width:] = stats.astype(BF16)


def get_cols(ref, width):
    heads = width // HEAD_DIM
    source = lax.broadcasted_iota(jnp.int32, (LANES, width), 0)
    target = lax.broadcasted_iota(jnp.int32, (LANES, width), 1)
    spread = (source < PIECES * heads) & (source % heads == target // HEAD_DIM)
    return ref[:, :width].astype(F32), dot(ref[:, width:], spread.astype(BF16))


def merge(states):
    top = states[0][1]
    for _, log in states[1:]:
        top = jnp.maximum(top, log)
    total, mix = 0.0, 0.0
    for part, log in states:
        weight = jnp.exp2(log - top)
        total += weight
        mix += weight * part
    return mix / total


def project(mix, proj, me, outs):
    step = outs[0].shape[1]
    for i, out in enumerate(outs):
        block = pl.ds(pl.multiple_of(partner(me, i, len(outs)) * step, step), step)
        out[...] = dot(mix, proj[:, block]).astype(out.dtype)


def project_audio(me, proj, states, outs):
    width = proj.shape[0]
    mix = merge([get_rows(ref, width) for ref in states]).reshape(width, -1)
    project(mix.T.astype(BF16), proj, me[0], outs)


def merge_first(mine, got, _, mix_out, log_out):
    states = [get_cols(ref, mix_out.shape[1]) for ref in (mine, got)]
    top = jnp.maximum(states[0][1], states[1][1])
    weights = [jnp.exp2(log - top) for _, log in states]
    total = weights[0] + weights[1]
    mix_out[...] = (weights[0] * states[0][0] + weights[1] * states[1][0]) / total
    log_out[...] = top + jnp.log2(total)


def project_video(me, proj, mix_log, states, aud_core, outs):
    mix = merge([tuple(ref[...] for ref in mix_log)] + [get_cols(ref, proj.shape[0]) for ref in states])
    aud_rows = aud_core.shape[0]
    outs[1][:aud_rows, :] = aud_core[...]
    project(mix.astype(BF16), proj, me[0], [outs[0], outs[1].at[aud_rows:, :], *outs[2:]])


def add_audio(*refs):
    *terms, out = refs
    total = terms[0][...]
    for term in terms[1:]:
        total += term[...].astype(F32)
    out[...] = total


def add(aud_part, core, *refs):
    *vid_terms, aud_out, vid_out = refs
    aud_rows = aud_out.shape[0]
    aud_out[...] = (aud_part[...] + core[:aud_rows].astype(F32)).astype(BF16)
    vid = vid_terms[0][...] + core[aud_rows:].astype(F32)
    for term in vid_terms[1:]:
        vid += term[...].astype(F32)
    vid_out[...] = vid.astype(BF16)


def call(body, out_shape, args, in_specs=None, scratch=(), cost=COST):
    vmem = pl.BlockSpec(memory_space=pltpu.VMEM)
    return pl.pallas_call(
        body,
        out_shape=out_shape,
        in_specs=in_specs or [vmem] * len(args),
        out_specs=[vmem] * len(out_shape),
        scratch_shapes=scratch,
        compiler_params=pltpu.CompilerParams(vmem_limit_bytes=VMEM_LIMIT),
        cost_estimate=pl.CostEstimate(flops=cost, bytes_accessed=0, transcendentals=0),
    )(*args)


def partner(index, k, size):
    return index ^ k


def swap(block, axis, distance):
    return lax.ppermute(block, axis, [(i, i ^ distance) for i in range(lax.axis_size(axis))])


def factors(size):
    bits = size.bit_length() - 1
    assert size == 1 << bits
    return 1 << (bits // 2), 1 << (bits - bits // 2)


def per_device(ref_audio, val_audio, ref_video, val_video, audio_proj, video_proj):
    seq, peers = lax.axis_size("seq"), lax.axis_size("head")
    aud_count, vid_count = factors(seq)
    aud_rows, width = ref_audio.shape
    vid_rows = ref_video.shape[0]
    heads = width // HEAD_DIM
    step = audio_proj.shape[1] // peers
    log_rows = -(-PIECES * heads // 16) * 16

    def shape(*dims, dtype=BF16):
        return jax.ShapeDtypeStruct(dims, dtype)

    aud, vid = call(
        pack,
        [shape(2, aud_rows, width), shape(2, vid_rows, width)],
        [
            pltpu.with_memory_space_constraint(x, pltpu.HBM)
            for x in (ref_audio, val_audio, ref_video, val_video)
        ],
        in_specs=[pl.BlockSpec(memory_space=pltpu.HBM)] * 4,
        scratch=[pltpu.SemaphoreType.DMA((4,))],
    )
    early = vid_count // 2
    late = [k for k in reversed(range(1, vid_count)) if k != early]
    auds = [swap(aud, "seq", k) for k in range(1, aud_count)] + [aud]
    vids = {k: swap(vid, "seq", k * aud_count) for k in (early, *late)}
    state = shape(vid_rows, width + LANES)
    first_state, scores = call(
        attend_first,
        [state, shape(heads, vid_rows, aud_count * aud_rows, dtype=F32)],
        [*auds, vids[early]],
    )
    states = call(
        functools.partial(attend, aud_count, len(late) + 1),
        [shape(width + log_rows, aud_rows)] * aud_count + [state] * (len(late) + 1),
        [*auds, *(vids[k] for k in late), vid, vids[early], scores],
    )
    rows = [swap(states[k - 1], "seq", k) for k in range(1, aud_count)] + [states[aud_count - 1]]
    states = dict(zip((early, *late, 0), (first_state, *states[aud_count:])))
    cols = [swap(states[k], "seq", k * aud_count) for k in (early, *late)] + [states[0]]

    me = lax.axis_index("head").astype(jnp.int32).reshape(1)
    vmem = pl.BlockSpec(memory_space=pltpu.VMEM)
    smem = pl.BlockSpec(memory_space=pltpu.SMEM)
    hbm = pl.BlockSpec(memory_space=pl.ANY)

    mix_log = call(
        merge_first, [shape(vid_rows, width, dtype=F32)] * 2, [cols.pop(), cols.pop(0), audio_proj]
    )
    aud_terms = call(
        lambda me, proj, *refs: project_audio(me, proj, refs[:aud_count], refs[aud_count + 1 :]),
        [shape(aud_rows, step, dtype=F32)] + [shape(aud_rows, step)] * (peers - 1),
        [me, audio_proj, *rows, mix_log[0]],
        in_specs=[smem, vmem] + [vmem] * aud_count + [pl.BlockSpec(memory_space=pl.ANY)],
        cost=COST_A,
    )
    vid_terms = call(
        lambda me, proj, mix, log, core, *refs: project_video(
            me, proj, (mix, log), refs[: len(cols)], core, refs[len(cols) :]
        ),
        [shape(vid_rows, step, dtype=F32), shape(aud_rows + vid_rows, step)]
        + [shape(vid_rows, step)] * (peers - 2),
        [me, video_proj, *mix_log, aud_terms[1], *cols],
        in_specs=[smem] + [vmem] * (len(cols) + 4),
    )
    vid_got = [swap(vid_terms[k], "head", k) for k in range(2, peers)]
    core_got = swap(vid_terms[1], "head", 1)
    aud_got = [swap(aud_terms[k], "head", k) for k in reversed(range(2, peers))]
    aud_part = call(add_audio, [shape(aud_rows, step, dtype=F32)], [aud_terms[0], *aud_got])[0]
    return tuple(
        call(
            add,
            [shape(aud_rows, step), shape(vid_rows, step)],
            [aud_part, core_got, vid_terms[0], *vid_got],
        )
    )


def solution(mesh):
    in_specs = (
        P("seq", "head"),
        P("seq", "head"),
        P("seq", "head"),
        P("seq", "head"),
        P("head", None),
        P("head", None),
    )
    out_specs = (P("seq", "head"), P("seq", "head"))
    return jax.shard_map(
        per_device, mesh=mesh, in_specs=in_specs, out_specs=out_specs, check_vma=False
    )
```

```python
import functools
import math

import jax
import jax.numpy as jnp
from jax import lax
from jax.experimental import pallas as pl
from jax.experimental.pallas import tpu as pltpu
from jax.sharding import PartitionSpec as P

HEAD_DIM = 64
LANES = 128
PIECES = 3
SCALE = HEAD_DIM ** (-0.5) * math.log2(math.e)
VMEM_LIMIT = 48 * 1024 * 1024
COST = 5 * 10**9
COST_A = 10**9
BF16 = jnp.bfloat16
F32 = jnp.float32


def dot(a, b, contract_a=1, contract_b=0):
    dims = (((contract_a,), (contract_b,)), ((), ()))
    return lax.dot_general(a, b, dims, preferred_element_type=F32)


def split_pieces(value):
    pieces = []
    for _ in range(PIECES):
        piece = value.astype(BF16).astype(F32)
        pieces.append(piece)
        value = value - piece
    return pieces


def head_lanes(rows, width, head):
    return lax.broadcasted_iota(jnp.int32, (rows, width), 1) // HEAD_DIM == head


def pack(aud_ref, aud_val, vid_ref, vid_val, aud, vid, sems):
    pairs = ((aud_ref, aud.at[0]), (aud_val, aud.at[1]), (vid_ref, vid.at[0]), (vid_val, vid.at[1]))
    copies = [pltpu.make_async_copy(a, b, sems.at[i]) for i, (a, b) in enumerate(pairs)]
    for copy in copies:
        copy.start()
    for copy in copies:
        copy.wait()


def tile_scores(queries, vids):
    total_vid, width = sum(ref.shape[1] for ref in vids), queries.shape[1]
    heads = width // HEAD_DIM
    keys = jnp.concatenate([ref[0].astype(F32) for ref in vids], axis=0).astype(BF16)
    lanes = [head_lanes(1, width, h).astype(F32).astype(BF16) for h in range(heads)]
    keys = jnp.concatenate([keys * lane for lane in lanes], axis=0)
    return dot(keys, queries, 1, 1).reshape(heads, total_vid, queries.shape[0])


def both(auds):
    return (jnp.concatenate([ref[i] for ref in auds], axis=0) for i in range(2))


def column_states(scores, aud_vals, outs):
    heads, total_vid, total_aud = scores.shape
    width = heads * HEAD_DIM
    top = jnp.max(scores, axis=2, keepdims=True)
    probs = jnp.exp2((scores - top) * SCALE)
    total = jnp.sum(probs, axis=2, keepdims=True)
    probs = probs.reshape(heads * total_vid, total_aud).astype(BF16)
    every = dot(probs, aud_vals).reshape(heads, total_vid, width)
    log = top * SCALE + jnp.log2(total)
    lane = lax.broadcasted_iota(jnp.int32, (total_vid, LANES), 1) % heads
    mix, divisor = every[0], jnp.broadcast_to(total[0], (total_vid, width))
    logs = jnp.broadcast_to(log[0], (total_vid, LANES))
    for h in range(1, heads):
        mask = head_lanes(total_vid, width, h)
        mix = jnp.where(mask, every[h], mix)
        divisor = jnp.where(mask, total[h], divisor)
        logs = jnp.where(lane == h, log[h], logs)
    mix = mix / divisor
    for i, out in enumerate(outs):
        rows = slice(i * out.shape[0], (i + 1) * out.shape[0])
        put_cols(out, mix[rows], logs[rows])


def row_states(scores, vid_vals, outs):
    heads, _, total_aud = scores.shape
    top = jnp.max(scores, axis=1, keepdims=True)
    probs = jnp.exp2((scores - top) * SCALE)
    total = jnp.sum(probs, axis=1, keepdims=True)
    probs = probs.astype(BF16)
    vals = vid_vals.T.astype(BF16)
    mix = [
        dot(vals[h * HEAD_DIM : (h + 1) * HEAD_DIM], probs[h]) * (1.0 / total[h])
        for h in range(heads)
    ]
    mix = jnp.concatenate(mix, axis=0)
    log = (top * SCALE + jnp.log2(total)).reshape(heads, total_aud)
    for i, out in enumerate(outs):
        cols = slice(i * out.shape[1], (i + 1) * out.shape[1])
        put_rows(out, mix[:, cols], log[:, cols])


def attend_first(aud_count, *refs):
    auds, vids, (scores_out, *col_outs) = refs[:aud_count], refs[aud_count : aud_count + 2], refs[aud_count + 2 :]
    queries, aud_vals = both(auds)
    scores = tile_scores(queries, vids)
    scores_out[...] = scores
    column_states(scores, aud_vals, col_outs)


def attend(aud_count, vid_count, *refs):
    auds, vids, refs = refs[:aud_count], refs[aud_count : aud_count + vid_count], refs[aud_count + vid_count :]
    firsts, first_scores, row_outs, col_outs = refs[:2], refs[2], refs[3 : 3 + aud_count], refs[3 + aud_count :]
    queries, aud_vals = both(auds)
    scores = tile_scores(queries, vids)
    column_states(scores, aud_vals, col_outs)
    vals = jnp.concatenate([ref[1].astype(F32) for ref in (*firsts, *vids)], axis=0)
    row_states(jnp.concatenate([first_scores[...], scores], axis=1), vals, row_outs)


def put_rows(out, mix, log):
    width, tokens = mix.shape
    pad = jnp.zeros((out.shape[0] - width - PIECES * log.shape[0], tokens), F32)
    out[:width, :] = mix.astype(BF16)
    out[width:, :] = jnp.concatenate(split_pieces(log) + [pad], axis=0).astype(BF16)


def get_rows(ref, width):
    heads, tokens = width // HEAD_DIM, ref.shape[1]
    pieces = ref[width:, :].astype(F32)
    log = pieces[:heads]
    for i in range(1, PIECES):
        log = log + pieces[i * heads : (i + 1) * heads]
    mix = ref[:width, :].astype(F32).reshape(heads, HEAD_DIM, tokens)
    return mix, log.reshape(heads, 1, tokens)


def put_cols(out, mix, logs):
    width = mix.shape[1]
    heads = width // HEAD_DIM
    lane = lax.broadcasted_iota(jnp.int32, logs.shape, 1)
    pieces = split_pieces(logs)
    stats = jnp.zeros_like(logs)
    for i, piece in enumerate(pieces):
        stats = jnp.where(lane // heads == i, piece, stats)
    out[:, :width] = mix.astype(BF16)
    out[:, width:] = stats.astype(BF16)


def get_cols(ref, width):
    heads = width // HEAD_DIM
    source = lax.broadcasted_iota(jnp.int32, (LANES, width), 0)
    target = lax.broadcasted_iota(jnp.int32, (LANES, width), 1)
    spread = (source < PIECES * heads) & (source % heads == target // HEAD_DIM)
    return ref[:, :width].astype(F32), dot(ref[:, width:], spread.astype(BF16))


def merge(states):
    top = states[0][1]
    for _, log in states[1:]:
        top = jnp.maximum(top, log)
    total, mix = 0.0, 0.0
    for part, log in states:
        weight = jnp.exp2(log - top)
        total += weight
        mix += weight * part
    return mix / total


def project(mix, proj, me, outs):
    step = outs[0].shape[1]
    for i, out in enumerate(outs):
        block = pl.ds(pl.multiple_of(partner(me, i, len(outs)) * step, step), step)
        out[...] = dot(mix, proj[:, block]).astype(out.dtype)


def project_audio(me, proj, states, outs):
    width = proj.shape[0]
    mix = merge([get_rows(ref, width) for ref in states]).reshape(width, -1)
    project(mix.T.astype(BF16), proj, me[0], outs)


def merge_first(mine, got, _, mix_out, log_out):
    states = [get_cols(ref, mix_out.shape[1]) for ref in (mine, got)]
    top = jnp.maximum(states[0][1], states[1][1])
    weights = [jnp.exp2(log - top) for _, log in states]
    total = weights[0] + weights[1]
    mix_out[...] = (weights[0] * states[0][0] + weights[1] * states[1][0]) / total
    log_out[...] = top + jnp.log2(total)


def project_video(me, proj, mix_log, states, aud_core, outs):
    mix = merge([tuple(ref[...] for ref in mix_log)] + [get_cols(ref, proj.shape[0]) for ref in states])
    aud_rows = aud_core.shape[0]
    outs[1][:aud_rows, :] = aud_core[...]
    project(mix.astype(BF16), proj, me[0], [outs[0], outs[1].at[aud_rows:, :], *outs[2:]])


def add_audio(*refs):
    *terms, out = refs
    total = terms[0][...]
    for term in terms[1:]:
        total += term[...].astype(F32)
    out[...] = total


def add(aud_part, core, *refs):
    *vid_terms, aud_out, vid_out = refs
    aud_rows = aud_out.shape[0]
    aud_out[...] = (aud_part[...] + core[:aud_rows].astype(F32)).astype(BF16)
    vid = vid_terms[0][...] + core[aud_rows:].astype(F32)
    for term in vid_terms[1:]:
        vid += term[...].astype(F32)
    vid_out[...] = vid.astype(BF16)


def call(body, out_shape, args, in_specs=None, scratch=(), cost=COST):
    vmem = pl.BlockSpec(memory_space=pltpu.VMEM)
    return pl.pallas_call(
        body,
        out_shape=out_shape,
        in_specs=in_specs or [vmem] * len(args),
        out_specs=[vmem] * len(out_shape),
        scratch_shapes=scratch,
        compiler_params=pltpu.CompilerParams(vmem_limit_bytes=VMEM_LIMIT),
        cost_estimate=pl.CostEstimate(flops=cost, bytes_accessed=0, transcendentals=0),
    )(*args)


def partner(index, k, size):
    return index ^ k


def swap(block, axis, distance):
    return lax.ppermute(block, axis, [(i, i ^ distance) for i in range(lax.axis_size(axis))])


def factors(size):
    bits = size.bit_length() - 1
    assert size == 1 << bits
    return 1 << (bits // 2), 1 << (bits - bits // 2)


def per_device(ref_audio, val_audio, ref_video, val_video, audio_proj, video_proj):
    seq, peers = lax.axis_size("seq"), lax.axis_size("head")
    aud_count, vid_count = factors(seq)
    aud_rows, width = ref_audio.shape
    vid_rows = ref_video.shape[0]
    heads = width // HEAD_DIM
    step = audio_proj.shape[1] // peers
    log_rows = -(-PIECES * heads // 16) * 16

    def shape(*dims, dtype=BF16):
        return jax.ShapeDtypeStruct(dims, dtype)

    aud, vid = call(
        pack,
        [shape(2, aud_rows, width), shape(2, vid_rows, width)],
        [
            pltpu.with_memory_space_constraint(x, pltpu.HBM)
            for x in (ref_audio, val_audio, ref_video, val_video)
        ],
        in_specs=[pl.BlockSpec(memory_space=pltpu.HBM)] * 4,
        scratch=[pltpu.SemaphoreType.DMA((4,))],
    )
    early = vid_count // 2
    late = [k for k in reversed(range(1, vid_count)) if k != early]
    auds = [swap(aud, "seq", k) for k in range(1, aud_count)] + [aud]
    vids = {k: swap(vid, "seq", k * aud_count) for k in (early, *late)}
    state = shape(vid_rows, width + LANES)
    scores, first_state, own_state = call(
        functools.partial(attend_first, aud_count),
        [shape(heads, 2 * vid_rows, aud_count * aud_rows, dtype=F32), state, state],
        [*auds, vids[early], vid],
    )
    states = call(
        functools.partial(attend, aud_count, len(late)),
        [shape(width + log_rows, aud_rows)] * aud_count + [state] * len(late),
        [*auds, *(vids[k] for k in late), vids[early], vid, scores],
    )
    rows = [swap(states[k - 1], "seq", k) for k in range(1, aud_count)] + [states[aud_count - 1]]
    states = dict(zip((early, 0, *late), (first_state, own_state, *states[aud_count:])))
    cols = [swap(states[k], "seq", k * aud_count) for k in (early, *late)] + [states[0]]

    me = lax.axis_index("head").astype(jnp.int32).reshape(1)
    vmem = pl.BlockSpec(memory_space=pltpu.VMEM)
    smem = pl.BlockSpec(memory_space=pltpu.SMEM)
    hbm = pl.BlockSpec(memory_space=pl.ANY)

    mix_log = call(
        merge_first, [shape(vid_rows, width, dtype=F32)] * 2, [cols.pop(), cols.pop(0), audio_proj]
    )
    aud_terms = call(
        lambda me, proj, *refs: project_audio(me, proj, refs[:aud_count], refs[aud_count + 1 :]),
        [shape(aud_rows, step, dtype=F32)] + [shape(aud_rows, step)] * (peers - 1),
        [me, audio_proj, *rows, mix_log[0]],
        in_specs=[smem, vmem] + [vmem] * aud_count + [pl.BlockSpec(memory_space=pl.ANY)],
        cost=COST_A,
    )
    vid_terms = call(
        lambda me, proj, mix, log, core, *refs: project_video(
            me, proj, (mix, log), refs[: len(cols)], core, refs[len(cols) :]
        ),
        [shape(vid_rows, step, dtype=F32), shape(aud_rows + vid_rows, step)]
        + [shape(vid_rows, step)] * (peers - 2),
        [me, video_proj, *mix_log, aud_terms[1], *cols],
        in_specs=[smem] + [vmem] * (len(cols) + 4),
    )
    vid_got = [swap(vid_terms[k], "head", k) for k in range(2, peers)]
    core_got = swap(vid_terms[1], "head", 1)
    aud_got = [swap(aud_terms[k], "head", k) for k in reversed(range(2, peers))]
    aud_part = call(add_audio, [shape(aud_rows, step, dtype=F32)], [aud_terms[0], *aud_got])[0]
    return tuple(
        call(
            add,
            [shape(aud_rows, step), shape(vid_rows, step)],
            [aud_part, core_got, vid_terms[0], *vid_got],
        )
    )


def solution(mesh):
    in_specs = (
        P("seq", "head"),
        P("seq", "head"),
        P("seq", "head"),
        P("seq", "head"),
        P("head", None),
        P("head", None),
    )
    out_specs = (P("seq", "head"), P("seq", "head"))
    return jax.shard_map(
        per_device, mesh=mesh, in_specs=in_specs, out_specs=out_specs, check_vma=False
    )
```

```python
import functools
import math

import jax
import jax.numpy as jnp
from jax import lax
from jax.experimental import pallas as pl
from jax.experimental.pallas import tpu as pltpu
from jax.sharding import PartitionSpec as P

HEAD_DIM = 64
LANES = 128
PIECES = 3
SCALE = HEAD_DIM ** (-0.5) * math.log2(math.e)
VMEM_LIMIT = 48 * 1024 * 1024
COST = 5 * 10**9
COST_A = 10**9
BF16 = jnp.bfloat16
F32 = jnp.float32


def dot(a, b, contract_a=1, contract_b=0):
    dims = (((contract_a,), (contract_b,)), ((), ()))
    return lax.dot_general(a, b, dims, preferred_element_type=F32)


def split_pieces(value):
    pieces = []
    for _ in range(PIECES):
        piece = value.astype(BF16).astype(F32)
        pieces.append(piece)
        value = value - piece
    return pieces


def head_lanes(rows, width, head):
    return lax.broadcasted_iota(jnp.int32, (rows, width), 1) // HEAD_DIM == head


def pack(aud_ref, aud_val, vid_ref, vid_val, aud, vid, sems):
    pairs = ((aud_ref, aud.at[0]), (aud_val, aud.at[1]), (vid_ref, vid.at[0]), (vid_val, vid.at[1]))
    copies = [pltpu.make_async_copy(a, b, sems.at[i]) for i, (a, b) in enumerate(pairs)]
    for copy in copies:
        copy.start()
    for copy in copies:
        copy.wait()


def tile_scores(queries_t, vids):
    total_vid, width = sum(ref.shape[1] for ref in vids), queries_t.shape[0]
    heads = width // HEAD_DIM
    keys = jnp.concatenate([ref[0].astype(F32) for ref in vids], axis=0).astype(BF16)
    lanes = [head_lanes(1, width, h).astype(F32).astype(BF16) for h in range(heads)]
    keys = jnp.concatenate([keys * lane for lane in lanes], axis=0)
    return dot(keys, queries_t).reshape(heads, total_vid, queries_t.shape[1])


def values_t(vids):
    return jnp.concatenate([ref[1].astype(F32) for ref in vids], axis=0).T.astype(BF16)


def column_states(scores, aud_vals, outs):
    heads, total_vid, total_aud = scores.shape
    width = heads * HEAD_DIM
    top = jnp.max(scores, axis=2, keepdims=True)
    probs = jnp.exp2((scores - top) * SCALE)
    total = jnp.sum(probs, axis=2, keepdims=True)
    probs = probs.reshape(heads * total_vid, total_aud).astype(BF16)
    every = dot(probs, aud_vals).reshape(heads, total_vid, width)
    log = top * SCALE + jnp.log2(total)
    lane = lax.broadcasted_iota(jnp.int32, (total_vid, LANES), 1) % heads
    mix, divisor = every[0], jnp.broadcast_to(total[0], (total_vid, width))
    logs = jnp.broadcast_to(log[0], (total_vid, LANES))
    for h in range(1, heads):
        mask = head_lanes(total_vid, width, h)
        mix = jnp.where(mask, every[h], mix)
        divisor = jnp.where(mask, total[h], divisor)
        logs = jnp.where(lane == h, log[h], logs)
    mix = mix / divisor
    for i, out in enumerate(outs):
        rows = slice(i * out.shape[0], (i + 1) * out.shape[0])
        put_cols(out, mix[rows], logs[rows])


def row_states(parts, outs):
    heads, _, total_aud = parts[0][0].shape
    top = jnp.max(parts[0][0], axis=1, keepdims=True)
    for scores, _ in parts[1:]:
        top = jnp.maximum(top, jnp.max(scores, axis=1, keepdims=True))
    total, mix = 0.0, [0.0] * heads
    for scores, vals in parts:
        probs = jnp.exp2((scores - top) * SCALE)
        total += jnp.sum(probs, axis=1, keepdims=True)
        probs = probs.astype(BF16)
        for h in range(heads):
            mix[h] += dot(vals[h * HEAD_DIM : (h + 1) * HEAD_DIM], probs[h])
    mix = jnp.concatenate([mix[h] * (1.0 / total[h]) for h in range(heads)], axis=0)
    log = (top * SCALE + jnp.log2(total)).reshape(heads, total_aud)
    for i, out in enumerate(outs):
        cols = slice(i * out.shape[1], (i + 1) * out.shape[1])
        put_rows(out, mix[:, cols], log[:, cols])


def attend_first(aud_count, *refs):
    auds, vids, outs = refs[:aud_count], refs[aud_count : aud_count + 2], refs[aud_count + 2 :]
    scores_out, queries_out, aud_vals_out, vals_out, *col_outs = outs
    queries, aud_vals = (jnp.concatenate([ref[i] for ref in auds], axis=0) for i in range(2))
    queries_t = queries.astype(F32).T.astype(BF16)
    queries_out[...] = queries_t
    aud_vals_out[...] = aud_vals
    scores = tile_scores(queries_t, vids)
    scores_out[...] = scores
    vals_out[...] = values_t(vids)
    column_states(scores, aud_vals, col_outs)


def attend(aud_count, vid_count, queries, aud_vals, first_scores, first_vals, *refs):
    vids, refs = refs[:vid_count], refs[vid_count:]
    row_outs, col_outs = refs[:aud_count], refs[aud_count:]
    scores = tile_scores(queries[...], vids)
    column_states(scores, aud_vals[...], col_outs)
    row_states([(first_scores[...], first_vals[...]), (scores, values_t(vids))], row_outs)


def put_rows(out, mix, log):
    width, tokens = mix.shape
    pad = jnp.zeros((out.shape[0] - width - PIECES * log.shape[0], tokens), F32)
    out[:width, :] = mix.astype(BF16)
    out[width:, :] = jnp.concatenate(split_pieces(log) + [pad], axis=0).astype(BF16)


def get_rows(ref, width):
    heads, tokens = width // HEAD_DIM, ref.shape[1]
    pieces = ref[width:, :].astype(F32)
    log = pieces[:heads]
    for i in range(1, PIECES):
        log = log + pieces[i * heads : (i + 1) * heads]
    mix = ref[:width, :].astype(F32).reshape(heads, HEAD_DIM, tokens)
    return mix, log.reshape(heads, 1, tokens)


def put_cols(out, mix, logs):
    width = mix.shape[1]
    heads = width // HEAD_DIM
    lane = lax.broadcasted_iota(jnp.int32, logs.shape, 1)
    pieces = split_pieces(logs)
    stats = jnp.zeros_like(logs)
    for i, piece in enumerate(pieces):
        stats = jnp.where(lane // heads == i, piece, stats)
    out[:, :width] = mix.astype(BF16)
    out[:, width:] = stats.astype(BF16)


def get_cols(ref, width):
    heads = width // HEAD_DIM
    source = lax.broadcasted_iota(jnp.int32, (LANES, width), 0)
    target = lax.broadcasted_iota(jnp.int32, (LANES, width), 1)
    spread = (source < PIECES * heads) & (source % heads == target // HEAD_DIM)
    return ref[:, :width].astype(F32), dot(ref[:, width:], spread.astype(BF16))


def merge(states):
    top = states[0][1]
    for _, log in states[1:]:
        top = jnp.maximum(top, log)
    total, mix = 0.0, 0.0
    for part, log in states:
        weight = jnp.exp2(log - top)
        total += weight
        mix += weight * part
    return mix / total


def project(mix, proj, me, outs):
    step = outs[0].shape[1]
    for i, out in enumerate(outs):
        block = pl.ds(pl.multiple_of(partner(me, i, len(outs)) * step, step), step)
        out[...] = dot(mix, proj[:, block]).astype(out.dtype)


def project_audio(me, proj, states, outs):
    width = proj.shape[0]
    mix = merge([get_rows(ref, width) for ref in states]).reshape(width, -1)
    project(mix.T.astype(BF16), proj, me[0], outs)


def merge_first(mine, got, _, mix_out, log_out):
    states = [get_cols(ref, mix_out.shape[1]) for ref in (mine, got)]
    top = jnp.maximum(states[0][1], states[1][1])
    weights = [jnp.exp2(log - top) for _, log in states]
    total = weights[0] + weights[1]
    mix_out[...] = (weights[0] * states[0][0] + weights[1] * states[1][0]) / total
    log_out[...] = top + jnp.log2(total)


def project_video(me, proj, mix_log, states, aud_core, outs):
    mix = merge([tuple(ref[...] for ref in mix_log)] + [get_cols(ref, proj.shape[0]) for ref in states])
    aud_rows = aud_core.shape[0]
    outs[1][:aud_rows, :] = aud_core[...]
    project(mix.astype(BF16), proj, me[0], [outs[0], outs[1].at[aud_rows:, :], *outs[2:]])


def add_audio(*refs):
    *terms, out = refs
    total = terms[0][...]
    for term in terms[1:]:
        total += term[...].astype(F32)
    out[...] = total


def add(aud_part, core, *refs):
    *vid_terms, aud_out, vid_out = refs
    aud_rows = aud_out.shape[0]
    aud_out[...] = (aud_part[...] + core[:aud_rows].astype(F32)).astype(BF16)
    vid = vid_terms[0][...] + core[aud_rows:].astype(F32)
    for term in vid_terms[1:]:
        vid += term[...].astype(F32)
    vid_out[...] = vid.astype(BF16)


def call(body, out_shape, args, in_specs=None, scratch=(), cost=COST):
    vmem = pl.BlockSpec(memory_space=pltpu.VMEM)
    return pl.pallas_call(
        body,
        out_shape=out_shape,
        in_specs=in_specs or [vmem] * len(args),
        out_specs=[vmem] * len(out_shape),
        scratch_shapes=scratch,
        compiler_params=pltpu.CompilerParams(vmem_limit_bytes=VMEM_LIMIT),
        cost_estimate=pl.CostEstimate(flops=cost, bytes_accessed=0, transcendentals=0),
    )(*args)


def partner(index, k, size):
    return index ^ k


def swap(block, axis, distance):
    return lax.ppermute(block, axis, [(i, i ^ distance) for i in range(lax.axis_size(axis))])


def factors(size):
    bits = size.bit_length() - 1
    assert size == 1 << bits
    return 1 << (bits // 2), 1 << (bits - bits // 2)


def per_device(ref_audio, val_audio, ref_video, val_video, audio_proj, video_proj):
    seq, peers = lax.axis_size("seq"), lax.axis_size("head")
    aud_count, vid_count = factors(seq)
    aud_rows, width = ref_audio.shape
    vid_rows = ref_video.shape[0]
    heads = width // HEAD_DIM
    step = audio_proj.shape[1] // peers
    log_rows = -(-PIECES * heads // 16) * 16

    def shape(*dims, dtype=BF16):
        return jax.ShapeDtypeStruct(dims, dtype)

    aud, vid = call(
        pack,
        [shape(2, aud_rows, width), shape(2, vid_rows, width)],
        [
            pltpu.with_memory_space_constraint(x, pltpu.HBM)
            for x in (ref_audio, val_audio, ref_video, val_video)
        ],
        in_specs=[pl.BlockSpec(memory_space=pltpu.HBM)] * 4,
        scratch=[pltpu.SemaphoreType.DMA((4,))],
    )
    early = vid_count // 2
    late = [k for k in reversed(range(1, vid_count)) if k != early]
    auds = [swap(aud, "seq", k) for k in range(1, aud_count)] + [aud]
    vids = {k: swap(vid, "seq", k * aud_count) for k in (early, *late)}
    state = shape(vid_rows, width + LANES)
    total_aud = aud_count * aud_rows
    *shared, first_state, own_state = call(
        functools.partial(attend_first, aud_count),
        [
            shape(heads, 2 * vid_rows, total_aud, dtype=F32),
            shape(width, total_aud),
            shape(total_aud, width),
            shape(width, 2 * vid_rows),
            state,
            state,
        ],
        [*auds, vids[early], vid],
    )
    scores, queries_t, aud_vals, vals_t = shared
    states = call(
        functools.partial(attend, aud_count, len(late)),
        [shape(width + log_rows, aud_rows)] * aud_count + [state] * len(late),
        [queries_t, aud_vals, scores, vals_t, *(vids[k] for k in late)],
    )
    rows = [swap(states[k - 1], "seq", k) for k in range(1, aud_count)] + [states[aud_count - 1]]
    states = dict(zip((early, 0, *late), (first_state, own_state, *states[aud_count:])))
    cols = [swap(states[k], "seq", k * aud_count) for k in (early, *late)] + [states[0]]

    me = lax.axis_index("head").astype(jnp.int32).reshape(1)
    vmem = pl.BlockSpec(memory_space=pltpu.VMEM)
    smem = pl.BlockSpec(memory_space=pltpu.SMEM)
    hbm = pl.BlockSpec(memory_space=pl.ANY)

    mix_log = call(
        merge_first, [shape(vid_rows, width, dtype=F32)] * 2, [cols.pop(), cols.pop(0), audio_proj]
    )
    aud_terms = call(
        lambda me, proj, *refs: project_audio(me, proj, refs[:aud_count], refs[aud_count + 1 :]),
        [shape(aud_rows, step, dtype=F32)] + [shape(aud_rows, step)] * (peers - 1),
        [me, audio_proj, *rows, mix_log[0]],
        in_specs=[smem, vmem] + [vmem] * aud_count + [pl.BlockSpec(memory_space=pl.ANY)],
        cost=COST_A,
    )
    vid_terms = call(
        lambda me, proj, mix, log, core, *refs: project_video(
            me, proj, (mix, log), refs[: len(cols)], core, refs[len(cols) :]
        ),
        [shape(vid_rows, step, dtype=F32), shape(aud_rows + vid_rows, step)]
        + [shape(vid_rows, step)] * (peers - 2),
        [me, video_proj, *mix_log, aud_terms[1], *cols],
        in_specs=[smem] + [vmem] * (len(cols) + 4),
    )
    vid_got = [swap(vid_terms[k], "head", k) for k in range(2, peers)]
    core_got = swap(vid_terms[1], "head", 1)
    aud_got = [swap(aud_terms[k], "head", k) for k in reversed(range(2, peers))]
    aud_part = call(add_audio, [shape(aud_rows, step, dtype=F32)], [aud_terms[0], *aud_got])[0]
    return tuple(
        call(
            add,
            [shape(aud_rows, step), shape(vid_rows, step)],
            [aud_part, core_got, vid_terms[0], *vid_got],
        )
    )


def solution(mesh):
    in_specs = (
        P("seq", "head"),
        P("seq", "head"),
        P("seq", "head"),
        P("seq", "head"),
        P("head", None),
        P("head", None),
    )
    out_specs = (P("seq", "head"), P("seq", "head"))
    return jax.shard_map(
        per_device, mesh=mesh, in_specs=in_specs, out_specs=out_specs, check_vma=False
    )
```

```python
import functools
import math

import jax
import jax.numpy as jnp
from jax import lax
from jax.experimental import pallas as pl
from jax.experimental.pallas import tpu as pltpu
from jax.sharding import PartitionSpec as P

HEAD_DIM = 64
LANES = 128
PIECES = 3
SCALE = HEAD_DIM ** (-0.5) * math.log2(math.e)
VMEM_LIMIT = 48 * 1024 * 1024
COST = 5 * 10**9
COST_ADD = 10**3
BF16 = jnp.bfloat16
F32 = jnp.float32


def dot(a, b, contract_a=1, contract_b=0):
    dims = (((contract_a,), (contract_b,)), ((), ()))
    return lax.dot_general(a, b, dims, preferred_element_type=F32)


def split_pieces(value):
    pieces = []
    for _ in range(PIECES):
        piece = value.astype(BF16).astype(F32)
        pieces.append(piece)
        value = value - piece
    return pieces


def head_lanes(rows, width, head):
    return lax.broadcasted_iota(jnp.int32, (rows, width), 1) // HEAD_DIM == head


def pack(aud_ref, aud_val, vid_ref, vid_val, aud, vid, sems):
    pairs = ((aud_ref, aud.at[0]), (aud_val, aud.at[1]), (vid_ref, vid.at[0]), (vid_val, vid.at[1]))
    copies = [pltpu.make_async_copy(a, b, sems.at[i]) for i, (a, b) in enumerate(pairs)]
    for copy in copies:
        copy.start()
    for copy in copies:
        copy.wait()


def tile_scores(queries_t, vids):
    total_vid, width = sum(ref.shape[1] for ref in vids), queries_t.shape[0]
    heads = width // HEAD_DIM
    keys = jnp.concatenate([ref[0].astype(F32) for ref in vids], axis=0).astype(BF16)
    lanes = [head_lanes(1, width, h).astype(F32).astype(BF16) for h in range(heads)]
    keys = jnp.concatenate([keys * lane for lane in lanes], axis=0)
    return dot(keys, queries_t).reshape(heads, total_vid, queries_t.shape[1])


def values_t(vids):
    return jnp.concatenate([ref[1].astype(F32) for ref in vids], axis=0).T.astype(BF16)


def column_states(scores, aud_vals, outs):
    heads, total_vid, total_aud = scores.shape
    width = heads * HEAD_DIM
    top = jnp.max(scores, axis=2, keepdims=True)
    probs = jnp.exp2((scores - top) * SCALE)
    total = jnp.sum(probs, axis=2, keepdims=True)
    probs = probs.reshape(heads * total_vid, total_aud).astype(BF16)
    every = dot(probs, aud_vals).reshape(heads, total_vid, width)
    log = top * SCALE + jnp.log2(total)
    lane = lax.broadcasted_iota(jnp.int32, (total_vid, LANES), 1) % heads
    mix, divisor = every[0], jnp.broadcast_to(total[0], (total_vid, width))
    logs = jnp.broadcast_to(log[0], (total_vid, LANES))
    for h in range(1, heads):
        mask = head_lanes(total_vid, width, h)
        mix = jnp.where(mask, every[h], mix)
        divisor = jnp.where(mask, total[h], divisor)
        logs = jnp.where(lane == h, log[h], logs)
    mix = mix / divisor
    for i, out in enumerate(outs):
        rows = slice(i * out.shape[0], (i + 1) * out.shape[0])
        put_cols(out, mix[rows], logs[rows])


def row_states(parts, outs):
    heads, _, total_aud = parts[0][0].shape
    top = jnp.max(parts[0][0], axis=1, keepdims=True)
    for scores, _ in parts[1:]:
        top = jnp.maximum(top, jnp.max(scores, axis=1, keepdims=True))
    total, mix = 0.0, [0.0] * heads
    for scores, vals in parts:
        probs = jnp.exp2((scores - top) * SCALE)
        total += jnp.sum(probs, axis=1, keepdims=True)
        probs = probs.astype(BF16)
        for h in range(heads):
            mix[h] += dot(vals[h * HEAD_DIM : (h + 1) * HEAD_DIM], probs[h])
    mix = jnp.concatenate([mix[h] * (1.0 / total[h]) for h in range(heads)], axis=0)
    log = (top * SCALE + jnp.log2(total)).reshape(heads, total_aud)
    for i, out in enumerate(outs):
        cols = slice(i * out.shape[1], (i + 1) * out.shape[1])
        put_rows(out, mix[:, cols], log[:, cols])


def attend_first(aud_count, *refs):
    auds, vids, outs = refs[:aud_count], refs[aud_count : aud_count + 2], refs[aud_count + 2 :]
    scores_out, queries_out, aud_vals_out, vals_out, *col_outs = outs
    queries, aud_vals = (jnp.concatenate([ref[i] for ref in auds], axis=0) for i in range(2))
    queries_t = queries.astype(F32).T.astype(BF16)
    queries_out[...] = queries_t
    aud_vals_out[...] = aud_vals
    scores = tile_scores(queries_t, vids)
    scores_out[...] = scores
    vals_out[...] = values_t(vids)
    column_states(scores, aud_vals, col_outs)


def attend(aud_count, vid_count, queries, aud_vals, first_scores, first_vals, *refs):
    vids, refs = refs[:vid_count], refs[vid_count:]
    row_outs, col_outs = refs[:aud_count], refs[aud_count:]
    scores = tile_scores(queries[...], vids)
    column_states(scores, aud_vals[...], col_outs)
    row_states([(first_scores[...], first_vals[...]), (scores, values_t(vids))], row_outs)


def put_rows(out, mix, log):
    width, tokens = mix.shape
    pad = jnp.zeros((out.shape[0] - width - PIECES * log.shape[0], tokens), F32)
    out[:width, :] = mix.astype(BF16)
    out[width:, :] = jnp.concatenate(split_pieces(log) + [pad], axis=0).astype(BF16)


def get_rows(ref, width):
    heads, tokens = width // HEAD_DIM, ref.shape[1]
    pieces = ref[width:, :].astype(F32)
    log = pieces[:heads]
    for i in range(1, PIECES):
        log = log + pieces[i * heads : (i + 1) * heads]
    mix = ref[:width, :].astype(F32).reshape(heads, HEAD_DIM, tokens)
    return mix, log.reshape(heads, 1, tokens)


def put_cols(out, mix, logs):
    width = mix.shape[1]
    heads = width // HEAD_DIM
    lane = lax.broadcasted_iota(jnp.int32, logs.shape, 1)
    pieces = split_pieces(logs)
    stats = jnp.zeros_like(logs)
    for i, piece in enumerate(pieces):
        stats = jnp.where(lane // heads == i, piece, stats)
    out[:, :width] = mix.astype(BF16)
    out[:, width:] = stats.astype(BF16)


def get_cols(ref, width):
    heads = width // HEAD_DIM
    source = lax.broadcasted_iota(jnp.int32, (LANES, width), 0)
    target = lax.broadcasted_iota(jnp.int32, (LANES, width), 1)
    spread = (source < PIECES * heads) & (source % heads == target // HEAD_DIM)
    return ref[:, :width].astype(F32), dot(ref[:, width:], spread.astype(BF16))


def merge(states):
    top = states[0][1]
    for _, log in states[1:]:
        top = jnp.maximum(top, log)
    total, mix = 0.0, 0.0
    for part, log in states:
        weight = jnp.exp2(log - top)
        total += weight
        mix += weight * part
    return mix / total


def project(mix, proj, me, outs):
    step = outs[0].shape[1]
    for i, out in enumerate(outs):
        block = pl.ds(pl.multiple_of(partner(me, i, len(outs)) * step, step), step)
        out[...] = dot(mix, proj[:, block]).astype(out.dtype)


def project_audio(me, proj, states, outs):
    width = proj.shape[0]
    mix = merge([get_rows(ref, width) for ref in states]).reshape(width, -1)
    project(mix.T.astype(BF16), proj, me[0], outs)


def merge_first(mine, got, _, mix_out, log_out):
    states = [get_cols(ref, mix_out.shape[1]) for ref in (mine, got)]
    top = jnp.maximum(states[0][1], states[1][1])
    weights = [jnp.exp2(log - top) for _, log in states]
    total = weights[0] + weights[1]
    mix_out[...] = (weights[0] * states[0][0] + weights[1] * states[1][0]) / total
    log_out[...] = top + jnp.log2(total)


def project_video(me, proj, mix_log, states, aud_core, outs):
    mix = merge([tuple(ref[...] for ref in mix_log)] + [get_cols(ref, proj.shape[0]) for ref in states])
    aud_rows = aud_core.shape[0]
    outs[1][:aud_rows, :] = aud_core[...]
    project(mix.astype(BF16), proj, me[0], [outs[0], outs[1].at[aud_rows:, :], *outs[2:]])


def add_terms(*refs):
    *terms, out = refs
    total = terms[0][...]
    for term in terms[1:]:
        total += term[...].astype(F32)
    out[...] = total


def add_core(aud_sum, vid_sum, core, aud_out, vid_out):
    aud_rows = aud_out.shape[0]
    aud_out[...] = (aud_sum[...] + core[:aud_rows].astype(F32)).astype(BF16)
    vid_out[...] = (vid_sum[...] + core[aud_rows:].astype(F32)).astype(BF16)


def call(body, out_shape, args, in_specs=None, scratch=(), cost=COST):
    vmem = pl.BlockSpec(memory_space=pltpu.VMEM)
    return pl.pallas_call(
        body,
        out_shape=out_shape,
        in_specs=in_specs or [vmem] * len(args),
        out_specs=[vmem] * len(out_shape),
        scratch_shapes=scratch,
        compiler_params=pltpu.CompilerParams(vmem_limit_bytes=VMEM_LIMIT),
        cost_estimate=pl.CostEstimate(flops=cost, bytes_accessed=0, transcendentals=0),
    )(*args)


def partner(index, k, size):
    return index ^ k


def swap(block, axis, distance):
    return lax.ppermute(block, axis, [(i, i ^ distance) for i in range(lax.axis_size(axis))])


def factors(size):
    bits = size.bit_length() - 1
    assert size == 1 << bits
    return 1 << (bits // 2), 1 << (bits - bits // 2)


def per_device(ref_audio, val_audio, ref_video, val_video, audio_proj, video_proj):
    seq, peers = lax.axis_size("seq"), lax.axis_size("head")
    aud_count, vid_count = factors(seq)
    aud_rows, width = ref_audio.shape
    vid_rows = ref_video.shape[0]
    heads = width // HEAD_DIM
    step = audio_proj.shape[1] // peers
    log_rows = -(-PIECES * heads // 16) * 16

    def shape(*dims, dtype=BF16):
        return jax.ShapeDtypeStruct(dims, dtype)

    aud, vid = call(
        pack,
        [shape(2, aud_rows, width), shape(2, vid_rows, width)],
        [
            pltpu.with_memory_space_constraint(x, pltpu.HBM)
            for x in (ref_audio, val_audio, ref_video, val_video)
        ],
        in_specs=[pl.BlockSpec(memory_space=pltpu.HBM)] * 4,
        scratch=[pltpu.SemaphoreType.DMA((4,))],
    )
    early = vid_count // 2
    late = [k for k in reversed(range(1, vid_count)) if k != early]
    auds = [swap(aud, "seq", k) for k in range(1, aud_count)] + [aud]
    vids = {k: swap(vid, "seq", k * aud_count) for k in (early, *late)}
    state = shape(vid_rows, width + LANES)
    total_aud = aud_count * aud_rows
    *shared, first_state, own_state = call(
        functools.partial(attend_first, aud_count),
        [
            shape(heads, 2 * vid_rows, total_aud, dtype=F32),
            shape(width, total_aud),
            shape(total_aud, width),
            shape(width, 2 * vid_rows),
            state,
            state,
        ],
        [*auds, vids[early], vid],
    )
    scores, queries_t, aud_vals, vals_t = shared
    states = call(
        functools.partial(attend, aud_count, len(late)),
        [shape(width + log_rows, aud_rows)] * aud_count + [state] * len(late),
        [queries_t, aud_vals, scores, vals_t, *(vids[k] for k in late)],
    )
    rows = [swap(states[k - 1], "seq", k) for k in range(1, aud_count)] + [states[aud_count - 1]]
    states = dict(zip((early, 0, *late), (first_state, own_state, *states[aud_count:])))
    cols = [swap(states[k], "seq", k * aud_count) for k in (early, *late)] + [states[0]]

    me = lax.axis_index("head").astype(jnp.int32).reshape(1)
    vmem = pl.BlockSpec(memory_space=pltpu.VMEM)
    smem = pl.BlockSpec(memory_space=pltpu.SMEM)
    hbm = pl.BlockSpec(memory_space=pl.ANY)

    mix_log = call(
        merge_first, [shape(vid_rows, width, dtype=F32)] * 2, [cols.pop(), cols.pop(0), audio_proj]
    )
    aud_terms = call(
        lambda me, proj, *refs: project_audio(me, proj, refs[:aud_count], refs[aud_count + 1 :]),
        [shape(aud_rows, step, dtype=F32)] + [shape(aud_rows, step)] * (peers - 1),
        [me, audio_proj, *rows, mix_log[0]],
        in_specs=[smem, vmem] + [vmem] * aud_count + [pl.BlockSpec(memory_space=pl.ANY)],
    )
    vid_terms = call(
        lambda me, proj, mix, log, core, *refs: project_video(
            me, proj, (mix, log), refs[: len(cols)], core, refs[len(cols) :]
        ),
        [shape(vid_rows, step, dtype=F32), shape(aud_rows + vid_rows, step)]
        + [shape(vid_rows, step)] * (peers - 2),
        [me, video_proj, *mix_log, aud_terms[1], *cols],
        in_specs=[smem] + [vmem] * (len(cols) + 4),
    )
    vid_got = [swap(vid_terms[k], "head", k) for k in range(2, peers)]
    core_got = swap(vid_terms[1], "head", 1)
    aud_got = [swap(aud_terms[k], "head", k) for k in reversed(range(2, peers))]
    aud_sum = call(add_terms, [shape(aud_rows, step, dtype=F32)], [aud_terms[0], *aud_got])[0]
    vid_sum = call(
        add_terms, [shape(vid_rows, step, dtype=F32)], [vid_terms[0], *vid_got], cost=COST_ADD
    )[0]
    return tuple(
        call(add_core, [shape(aud_rows, step), shape(vid_rows, step)], [aud_sum, vid_sum, core_got])
    )


def solution(mesh):
    in_specs = (
        P("seq", "head"),
        P("seq", "head"),
        P("seq", "head"),
        P("seq", "head"),
        P("head", None),
        P("head", None),
    )
    out_specs = (P("seq", "head"), P("seq", "head"))
    return jax.shard_map(
        per_device, mesh=mesh, in_specs=in_specs, out_specs=out_specs, check_vma=False
    )
```

```python
import functools
import math

import jax
import jax.numpy as jnp
from jax import lax
from jax.experimental import pallas as pl
from jax.experimental.pallas import tpu as pltpu
from jax.sharding import PartitionSpec as P

HEAD_DIM = 64
LANES = 128
PIECES = 3
SCALE = HEAD_DIM ** (-0.5) * math.log2(math.e)
VMEM_LIMIT = 48 * 1024 * 1024
COST = 5 * 10**9
COST_LOW = 10**3
BF16 = jnp.bfloat16
F32 = jnp.float32


def dot(a, b, contract_a=1, contract_b=0):
    dims = (((contract_a,), (contract_b,)), ((), ()))
    return lax.dot_general(a, b, dims, preferred_element_type=F32)


def split_pieces(value):
    pieces = []
    for _ in range(PIECES):
        piece = value.astype(BF16).astype(F32)
        pieces.append(piece)
        value = value - piece
    return pieces


def head_lanes(rows, width, head):
    return lax.broadcasted_iota(jnp.int32, (rows, width), 1) // HEAD_DIM == head


def pack(aud_ref, aud_val, vid_ref, vid_val, aud, vid, sems):
    pairs = ((aud_ref, aud.at[0]), (aud_val, aud.at[1]), (vid_ref, vid.at[0]), (vid_val, vid.at[1]))
    copies = [pltpu.make_async_copy(a, b, sems.at[i]) for i, (a, b) in enumerate(pairs)]
    for copy in copies:
        copy.start()
    for copy in copies:
        copy.wait()


def tile_scores(queries_t, vids):
    total_vid, width = sum(ref.shape[1] for ref in vids), queries_t.shape[0]
    heads = width // HEAD_DIM
    keys = jnp.concatenate([ref[0].astype(F32) for ref in vids], axis=0).astype(BF16)
    lanes = [head_lanes(1, width, h).astype(F32).astype(BF16) for h in range(heads)]
    keys = jnp.concatenate([keys * lane for lane in lanes], axis=0)
    return dot(keys, queries_t).reshape(heads, total_vid, queries_t.shape[1])


def values_t(vids):
    return jnp.concatenate([ref[1].astype(F32) for ref in vids], axis=0).T.astype(BF16)


def column_states(scores, aud_vals, outs):
    heads, total_vid, total_aud = scores.shape
    width = heads * HEAD_DIM
    top = jnp.max(scores, axis=2, keepdims=True)
    probs = jnp.exp2((scores - top) * SCALE)
    total = jnp.sum(probs, axis=2, keepdims=True)
    probs = probs.reshape(heads * total_vid, total_aud).astype(BF16)
    every = dot(probs, aud_vals).reshape(heads, total_vid, width)
    log = top * SCALE + jnp.log2(total)
    lane = lax.broadcasted_iota(jnp.int32, (total_vid, LANES), 1) % heads
    mix, divisor = every[0], jnp.broadcast_to(total[0], (total_vid, width))
    logs = jnp.broadcast_to(log[0], (total_vid, LANES))
    for h in range(1, heads):
        mask = head_lanes(total_vid, width, h)
        mix = jnp.where(mask, every[h], mix)
        divisor = jnp.where(mask, total[h], divisor)
        logs = jnp.where(lane == h, log[h], logs)
    mix = mix / divisor
    for i, out in enumerate(outs):
        rows = slice(i * out.shape[0], (i + 1) * out.shape[0])
        put_cols(out, mix[rows], logs[rows])


def row_states(parts, outs):
    heads, _, total_aud = parts[0][0].shape
    top = jnp.max(parts[0][0], axis=1, keepdims=True)
    for scores, _ in parts[1:]:
        top = jnp.maximum(top, jnp.max(scores, axis=1, keepdims=True))
    total, mix = 0.0, [0.0] * heads
    for scores, vals in parts:
        probs = jnp.exp2((scores - top) * SCALE)
        total += jnp.sum(probs, axis=1, keepdims=True)
        probs = probs.astype(BF16)
        for h in range(heads):
            mix[h] += dot(vals[h * HEAD_DIM : (h + 1) * HEAD_DIM], probs[h])
    mix = jnp.concatenate([mix[h] * (1.0 / total[h]) for h in range(heads)], axis=0)
    log = (top * SCALE + jnp.log2(total)).reshape(heads, total_aud)
    for i, out in enumerate(outs):
        cols = slice(i * out.shape[1], (i + 1) * out.shape[1])
        put_rows(out, mix[:, cols], log[:, cols])


def attend_first(aud_count, *refs):
    auds, vids, outs = refs[:aud_count], refs[aud_count : aud_count + 2], refs[aud_count + 2 :]
    scores_out, queries_out, aud_vals_out, vals_out, *col_outs = outs
    queries, aud_vals = (jnp.concatenate([ref[i] for ref in auds], axis=0) for i in range(2))
    queries_t = queries.astype(F32).T.astype(BF16)
    queries_out[...] = queries_t
    aud_vals_out[...] = aud_vals
    scores = tile_scores(queries_t, vids)
    scores_out[...] = scores
    vals_out[...] = values_t(vids)
    column_states(scores, aud_vals, col_outs)


def attend(aud_count, vid_count, queries, aud_vals, first_scores, first_vals, *refs):
    vids, refs = refs[:vid_count], refs[vid_count:]
    row_outs, col_outs = refs[:aud_count], refs[aud_count:]
    scores = tile_scores(queries[...], vids)
    column_states(scores, aud_vals[...], col_outs)
    row_states([(first_scores[...], first_vals[...]), (scores, values_t(vids))], row_outs)


def put_rows(out, mix, log):
    width, tokens = mix.shape
    pad = jnp.zeros((out.shape[0] - width - PIECES * log.shape[0], tokens), F32)
    out[:width, :] = mix.astype(BF16)
    out[width:, :] = jnp.concatenate(split_pieces(log) + [pad], axis=0).astype(BF16)


def get_rows(ref, width):
    heads, tokens = width // HEAD_DIM, ref.shape[1]
    pieces = ref[width:, :].astype(F32)
    log = pieces[:heads]
    for i in range(1, PIECES):
        log = log + pieces[i * heads : (i + 1) * heads]
    mix = ref[:width, :].astype(F32).reshape(heads, HEAD_DIM, tokens)
    return mix, log.reshape(heads, 1, tokens)


def put_cols(out, mix, logs):
    width = mix.shape[1]
    heads = width // HEAD_DIM
    lane = lax.broadcasted_iota(jnp.int32, logs.shape, 1)
    pieces = split_pieces(logs)
    stats = jnp.zeros_like(logs)
    for i, piece in enumerate(pieces):
        stats = jnp.where(lane // heads == i, piece, stats)
    out[:, :width] = mix.astype(BF16)
    out[:, width:] = stats.astype(BF16)


def get_cols(ref, width):
    heads = width // HEAD_DIM
    source = lax.broadcasted_iota(jnp.int32, (LANES, width), 0)
    target = lax.broadcasted_iota(jnp.int32, (LANES, width), 1)
    spread = (source < PIECES * heads) & (source % heads == target // HEAD_DIM)
    return ref[:, :width].astype(F32), dot(ref[:, width:], spread.astype(BF16))


def merge(states):
    top = states[0][1]
    for _, log in states[1:]:
        top = jnp.maximum(top, log)
    total, mix = 0.0, 0.0
    for part, log in states:
        weight = jnp.exp2(log - top)
        total += weight
        mix += weight * part
    return mix / total


def project(mix, proj, me, k, out):
    step = out.shape[1]
    block = pl.ds(pl.multiple_of((me ^ k) * step, step), step)
    out[...] = dot(mix, proj[:, block]).astype(out.dtype)


def project_audio(me, proj, states, mix_out, outs):
    width = proj.shape[0]
    mix = merge([get_rows(ref, width) for ref in states]).reshape(width, -1).T.astype(BF16)
    mix_out[...] = mix
    for k, out in enumerate(outs, 2):
        project(mix, proj, me[0], k, out)


def merge_first(mine, got, _, mix_out, log_out):
    states = [get_cols(ref, mix_out.shape[1]) for ref in (mine, got)]
    top = jnp.maximum(states[0][1], states[1][1])
    weights = [jnp.exp2(log - top) for _, log in states]
    total = weights[0] + weights[1]
    mix_out[...] = (weights[0] * states[0][0] + weights[1] * states[1][0]) / total
    log_out[...] = top + jnp.log2(total)


def project_video(me, proj, mix_log, states, mix_out, outs):
    mix = merge([tuple(ref[...] for ref in mix_log)] + [get_cols(ref, proj.shape[0]) for ref in states])
    mix = mix.astype(BF16)
    mix_out[...] = mix
    for k, out in enumerate(outs, 2):
        project(mix, proj, me[0], k, out)


def project_chip(me, aud_mix, vid_mix, aud_proj, vid_proj, aud_own, vid_own, core):
    aud_rows = aud_mix.shape[0]
    for mix, proj, own, rows in (
        (aud_mix, aud_proj, aud_own, slice(0, aud_rows)),
        (vid_mix, vid_proj, vid_own, slice(aud_rows, None)),
    ):
        project(mix[...], proj, me[0], 0, own)
        project(mix[...], proj, me[0], 1, core.at[rows, :])


def add_terms(*refs):
    *terms, out = refs
    total = terms[0][...]
    for term in terms[1:]:
        total += term[...].astype(F32)
    out[...] = total


def add_core(aud_sum, vid_sum, core, aud_out, vid_out):
    aud_rows = aud_out.shape[0]
    aud_out[...] = (aud_sum[...] + core[:aud_rows].astype(F32)).astype(BF16)
    vid_out[...] = (vid_sum[...] + core[aud_rows:].astype(F32)).astype(BF16)


def call(body, out_shape, args, in_specs=None, scratch=(), cost=COST):
    vmem = pl.BlockSpec(memory_space=pltpu.VMEM)
    return pl.pallas_call(
        body,
        out_shape=out_shape,
        in_specs=in_specs or [vmem] * len(args),
        out_specs=[vmem] * len(out_shape),
        scratch_shapes=scratch,
        compiler_params=pltpu.CompilerParams(vmem_limit_bytes=VMEM_LIMIT),
        cost_estimate=pl.CostEstimate(flops=cost, bytes_accessed=0, transcendentals=0),
    )(*args)


def swap(block, axis, distance):
    return lax.ppermute(block, axis, [(i, i ^ distance) for i in range(lax.axis_size(axis))])


def factors(size):
    bits = size.bit_length() - 1
    assert size == 1 << bits
    return 1 << (bits // 2), 1 << (bits - bits // 2)


def per_device(ref_audio, val_audio, ref_video, val_video, audio_proj, video_proj):
    seq, peers = lax.axis_size("seq"), lax.axis_size("head")
    aud_count, vid_count = factors(seq)
    aud_rows, width = ref_audio.shape
    vid_rows = ref_video.shape[0]
    heads = width // HEAD_DIM
    step = audio_proj.shape[1] // peers
    log_rows = -(-PIECES * heads // 16) * 16

    def shape(*dims, dtype=BF16):
        return jax.ShapeDtypeStruct(dims, dtype)

    aud, vid = call(
        pack,
        [shape(2, aud_rows, width), shape(2, vid_rows, width)],
        [
            pltpu.with_memory_space_constraint(x, pltpu.HBM)
            for x in (ref_audio, val_audio, ref_video, val_video)
        ],
        in_specs=[pl.BlockSpec(memory_space=pltpu.HBM)] * 4,
        scratch=[pltpu.SemaphoreType.DMA((4,))],
    )
    early = vid_count // 2
    late = [k for k in reversed(range(1, vid_count)) if k != early]
    auds = [swap(aud, "seq", k) for k in range(1, aud_count)] + [aud]
    vids = {k: swap(vid, "seq", k * aud_count) for k in (early, *late)}
    state = shape(vid_rows, width + LANES)
    total_aud = aud_count * aud_rows
    *shared, first_state, own_state = call(
        functools.partial(attend_first, aud_count),
        [
            shape(heads, 2 * vid_rows, total_aud, dtype=F32),
            shape(width, total_aud),
            shape(total_aud, width),
            shape(width, 2 * vid_rows),
            state,
            state,
        ],
        [*auds, vids[early], vid],
    )
    scores, queries_t, aud_vals, vals_t = shared
    states = call(
        functools.partial(attend, aud_count, len(late)),
        [shape(width + log_rows, aud_rows)] * aud_count + [state] * len(late),
        [queries_t, aud_vals, scores, vals_t, *(vids[k] for k in late)],
    )
    rows = [swap(states[k - 1], "seq", k) for k in range(1, aud_count)] + [states[aud_count - 1]]
    states = dict(zip((early, 0, *late), (first_state, own_state, *states[aud_count:])))
    cols = [swap(states[k], "seq", k * aud_count) for k in (early, *late)] + [states[0]]

    me = lax.axis_index("head").astype(jnp.int32).reshape(1)
    vmem = pl.BlockSpec(memory_space=pltpu.VMEM)
    smem = pl.BlockSpec(memory_space=pltpu.SMEM)
    hbm = pl.BlockSpec(memory_space=pl.ANY)

    mix_log = call(
        merge_first, [shape(vid_rows, width, dtype=F32)] * 2, [cols.pop(), cols.pop(0), audio_proj]
    )
    aud_mix, *aud_terms = call(
        lambda me, proj, *refs: project_audio(
            me, proj, refs[:aud_count], refs[aud_count + 1], refs[aud_count + 2 :]
        ),
        [shape(aud_rows, width)] + [shape(aud_rows, step)] * (peers - 2),
        [me, audio_proj, *rows, mix_log[0]],
        in_specs=[smem, vmem] + [vmem] * aud_count + [pl.BlockSpec(memory_space=pl.ANY)],
        cost=COST_LOW,
    )
    vid_mix, *vid_terms = call(
        lambda me, proj, mix, log, _, *refs: project_video(
            me, proj, (mix, log), refs[: len(cols)], refs[len(cols)], refs[len(cols) + 1 :]
        ),
        [shape(vid_rows, width)] + [shape(vid_rows, step)] * (peers - 2),
        [me, video_proj, *mix_log, aud_mix, *cols],
        in_specs=[smem] + [vmem] * 3 + [pl.BlockSpec(memory_space=pl.ANY)] + [vmem] * len(cols),
    )
    aud_own, vid_own, core = call(
        project_chip,
        [
            shape(aud_rows, step, dtype=F32),
            shape(vid_rows, step, dtype=F32),
            shape(aud_rows + vid_rows, step),
        ],
        [me, aud_mix, vid_mix, audio_proj, video_proj],
        in_specs=[smem] + [vmem] * 4,
        cost=COST_LOW,
    )
    vid_got = [swap(term, "head", k) for k, term in enumerate(vid_terms, 2)]
    core_got = swap(core, "head", 1)
    aud_got = [swap(term, "head", k) for k, term in reversed([*enumerate(aud_terms, 2)])]
    aud_sum = call(add_terms, [shape(aud_rows, step, dtype=F32)], [aud_own, *aud_got])[0]
    vid_sum = call(
        add_terms, [shape(vid_rows, step, dtype=F32)], [vid_own, *vid_got], cost=COST_LOW
    )[0]
    return tuple(
        call(add_core, [shape(aud_rows, step), shape(vid_rows, step)], [aud_sum, vid_sum, core_got], cost=COST_LOW)
    )


def solution(mesh):
    in_specs = (
        P("seq", "head"),
        P("seq", "head"),
        P("seq", "head"),
        P("seq", "head"),
        P("head", None),
        P("head", None),
    )
    out_specs = (P("seq", "head"), P("seq", "head"))
    return jax.shard_map(
        per_device, mesh=mesh, in_specs=in_specs, out_specs=out_specs, check_vma=False
    )
```

```python
import functools
import math

import jax
import jax.numpy as jnp
from jax import lax
from jax.experimental import pallas as pl
from jax.experimental.pallas import tpu as pltpu
from jax.sharding import PartitionSpec as P

HEAD_DIM = 64
LANES = 128
PIECES = 3
SCALE = HEAD_DIM ** (-0.5) * math.log2(math.e)
VMEM_LIMIT = 48 * 1024 * 1024
COST = 5 * 10**9
COST_ADD = 10**3
BF16 = jnp.bfloat16
F32 = jnp.float32


def dot(a, b, contract_a=1, contract_b=0):
    dims = (((contract_a,), (contract_b,)), ((), ()))
    return lax.dot_general(a, b, dims, preferred_element_type=F32)


def split_pieces(value):
    pieces = []
    for _ in range(PIECES):
        piece = value.astype(BF16).astype(F32)
        pieces.append(piece)
        value = value - piece
    return pieces


def head_lanes(rows, width, head):
    return lax.broadcasted_iota(jnp.int32, (rows, width), 1) // HEAD_DIM == head


def pack(aud_ref, aud_val, vid_ref, vid_val, aud, vid, sems):
    pairs = ((aud_ref, aud.at[0]), (aud_val, aud.at[1]), (vid_ref, vid.at[0]), (vid_val, vid.at[1]))
    copies = [pltpu.make_async_copy(a, b, sems.at[i]) for i, (a, b) in enumerate(pairs)]
    for copy in copies:
        copy.start()
    for copy in copies:
        copy.wait()


def tile_scores(queries_t, vids):
    total_vid, width = sum(ref.shape[1] for ref in vids), queries_t.shape[0]
    heads = width // HEAD_DIM
    keys = jnp.concatenate([ref[0].astype(F32) for ref in vids], axis=0).astype(BF16)
    lanes = [head_lanes(1, width, h).astype(F32).astype(BF16) for h in range(heads)]
    keys = jnp.concatenate([keys * lane for lane in lanes], axis=0)
    return dot(keys, queries_t).reshape(heads, total_vid, queries_t.shape[1])


def values_t(vids):
    return jnp.concatenate([ref[1].astype(F32) for ref in vids], axis=0).T.astype(BF16)


def column_states(scores, aud_vals, outs):
    heads, total_vid, total_aud = scores.shape
    width = heads * HEAD_DIM
    top = jnp.max(scores, axis=2, keepdims=True)
    probs = jnp.exp2((scores - top) * SCALE)
    total = jnp.sum(probs, axis=2, keepdims=True)
    probs = probs.reshape(heads * total_vid, total_aud).astype(BF16)
    every = dot(probs, aud_vals).reshape(heads, total_vid, width)
    log = top * SCALE + jnp.log2(total)
    lane = lax.broadcasted_iota(jnp.int32, (total_vid, LANES), 1) % heads
    mix, divisor = every[0], jnp.broadcast_to(total[0], (total_vid, width))
    logs = jnp.broadcast_to(log[0], (total_vid, LANES))
    for h in range(1, heads):
        mask = head_lanes(total_vid, width, h)
        mix = jnp.where(mask, every[h], mix)
        divisor = jnp.where(mask, total[h], divisor)
        logs = jnp.where(lane == h, log[h], logs)
    mix = mix / divisor
    for i, out in enumerate(outs):
        rows = slice(i * out.shape[0], (i + 1) * out.shape[0])
        put_cols(out, mix[rows], logs[rows])


def row_states(parts, outs):
    heads, _, total_aud = parts[0][0].shape
    top = jnp.max(parts[0][0], axis=1, keepdims=True)
    for scores, _ in parts[1:]:
        top = jnp.maximum(top, jnp.max(scores, axis=1, keepdims=True))
    total, mix = 0.0, [0.0] * heads
    for scores, vals in parts:
        probs = jnp.exp2((scores - top) * SCALE)
        total += jnp.sum(probs, axis=1, keepdims=True)
        probs = probs.astype(BF16)
        for h in range(heads):
            mix[h] += dot(vals[h * HEAD_DIM : (h + 1) * HEAD_DIM], probs[h])
    mix = jnp.concatenate([mix[h] * (1.0 / total[h]) for h in range(heads)], axis=0)
    log = (top * SCALE + jnp.log2(total)).reshape(heads, total_aud)
    for i, out in enumerate(outs):
        cols = slice(i * out.shape[1], (i + 1) * out.shape[1])
        put_rows(out, mix[:, cols], log[:, cols])


def attend_first(aud_count, *refs):
    auds, vids, outs = refs[:aud_count], refs[aud_count : aud_count + 2], refs[aud_count + 2 :]
    scores_out, queries_out, aud_vals_out, vals_out, *col_outs = outs
    queries, aud_vals = (jnp.concatenate([ref[i] for ref in auds], axis=0) for i in range(2))
    queries_t = queries.astype(F32).T.astype(BF16)
    queries_out[...] = queries_t
    aud_vals_out[...] = aud_vals
    scores = tile_scores(queries_t, vids)
    scores_out[...] = scores
    vals_out[...] = values_t(vids)
    column_states(scores, aud_vals, col_outs)


def attend(aud_count, vid_count, queries, aud_vals, first_scores, first_vals, *refs):
    vids, refs = refs[:vid_count], refs[vid_count:]
    row_outs, col_outs = refs[:aud_count], refs[aud_count:]
    scores = tile_scores(queries[...], vids)
    column_states(scores, aud_vals[...], col_outs)
    row_states([(first_scores[...], first_vals[...]), (scores, values_t(vids))], row_outs)


def put_rows(out, mix, log):
    width, tokens = mix.shape
    pad = jnp.zeros((out.shape[0] - width - PIECES * log.shape[0], tokens), F32)
    out[:width, :] = mix.astype(BF16)
    out[width:, :] = jnp.concatenate(split_pieces(log) + [pad], axis=0).astype(BF16)


def get_rows(ref, width):
    heads, tokens = width // HEAD_DIM, ref.shape[1]
    pieces = ref[width:, :].astype(F32)
    log = pieces[:heads]
    for i in range(1, PIECES):
        log = log + pieces[i * heads : (i + 1) * heads]
    mix = ref[:width, :].astype(F32).reshape(heads, HEAD_DIM, tokens)
    return mix, log.reshape(heads, 1, tokens)


def put_cols(out, mix, logs):
    width = mix.shape[1]
    heads = width // HEAD_DIM
    lane = lax.broadcasted_iota(jnp.int32, logs.shape, 1)
    pieces = split_pieces(logs)
    stats = jnp.zeros_like(logs)
    for i, piece in enumerate(pieces):
        stats = jnp.where(lane // heads == i, piece, stats)
    out[:, :width] = mix.astype(BF16)
    out[:, width:] = stats.astype(BF16)


def get_cols(ref, width):
    heads = width // HEAD_DIM
    source = lax.broadcasted_iota(jnp.int32, (LANES, width), 0)
    target = lax.broadcasted_iota(jnp.int32, (LANES, width), 1)
    spread = (source < PIECES * heads) & (source % heads == target // HEAD_DIM)
    return ref[:, :width].astype(F32), dot(ref[:, width:], spread.astype(BF16))


def merge(states):
    top = states[0][1]
    for _, log in states[1:]:
        top = jnp.maximum(top, log)
    total, mix = 0.0, 0.0
    for part, log in states:
        weight = jnp.exp2(log - top)
        total += weight
        mix += weight * part
    return mix / total


def project(mix, proj, me, outs):
    step = outs[0].shape[1]
    for i, out in enumerate(outs):
        block = pl.ds(pl.multiple_of(partner(me, i, len(outs)) * step, step), step)
        out[...] = dot(mix, proj[:, block]).astype(out.dtype)


def project_audio(me, proj, states, outs):
    width = proj.shape[0]
    mix = merge([get_rows(ref, width) for ref in states]).reshape(width, -1)
    project(mix.T.astype(BF16), proj, me[0], outs)


def merge_first(mine, got, _, mix_out, log_out):
    states = [get_cols(ref, mix_out.shape[1]) for ref in (mine, got)]
    top = jnp.maximum(states[0][1], states[1][1])
    weights = [jnp.exp2(log - top) for _, log in states]
    total = weights[0] + weights[1]
    mix_out[...] = (weights[0] * states[0][0] + weights[1] * states[1][0]) / total
    log_out[...] = top + jnp.log2(total)


def project_video(me, proj, mix_log, states, aud_core, outs):
    mix = merge([tuple(ref[...] for ref in mix_log)] + [get_cols(ref, proj.shape[0]) for ref in states])
    aud_rows = aud_core.shape[0]
    outs[1][:aud_rows, :] = aud_core[...]
    project(mix.astype(BF16), proj, me[0], [outs[0], outs[1].at[aud_rows:, :], *outs[2:]])


def add_terms(*refs):
    *terms, out = refs
    total = terms[0][...]
    for term in terms[1:]:
        total += term[...].astype(F32)
    out[...] = total


def add_core(aud_sum, vid_sum, core, aud_out, vid_out):
    aud_rows = aud_out.shape[0]
    aud_out[...] = (aud_sum[...] + core[:aud_rows].astype(F32)).astype(BF16)
    vid_out[...] = (vid_sum[...] + core[aud_rows:].astype(F32)).astype(BF16)


def call(body, out_shape, args, in_specs=None, scratch=(), cost=COST):
    vmem = pl.BlockSpec(memory_space=pltpu.VMEM)
    return pl.pallas_call(
        body,
        out_shape=out_shape,
        in_specs=in_specs or [vmem] * len(args),
        out_specs=[vmem] * len(out_shape),
        scratch_shapes=scratch,
        compiler_params=pltpu.CompilerParams(vmem_limit_bytes=VMEM_LIMIT),
        cost_estimate=pl.CostEstimate(flops=cost, bytes_accessed=0, transcendentals=0),
    )(*args)


def partner(index, k, size):
    return index ^ k


def swap(block, axis, distance):
    return lax.ppermute(block, axis, [(i, i ^ distance) for i in range(lax.axis_size(axis))])


def factors(size):
    bits = size.bit_length() - 1
    assert size == 1 << bits
    return 1 << (bits // 2), 1 << (bits - bits // 2)


def per_device(ref_audio, val_audio, ref_video, val_video, audio_proj, video_proj):
    seq, peers = lax.axis_size("seq"), lax.axis_size("head")
    aud_count, vid_count = factors(seq)
    aud_rows, width = ref_audio.shape
    vid_rows = ref_video.shape[0]
    heads = width // HEAD_DIM
    step = audio_proj.shape[1] // peers
    log_rows = -(-PIECES * heads // 16) * 16

    def shape(*dims, dtype=BF16):
        return jax.ShapeDtypeStruct(dims, dtype)

    aud, vid = call(
        pack,
        [shape(2, aud_rows, width), shape(2, vid_rows, width)],
        [
            pltpu.with_memory_space_constraint(x, pltpu.HBM)
            for x in (ref_audio, val_audio, ref_video, val_video)
        ],
        in_specs=[pl.BlockSpec(memory_space=pltpu.HBM)] * 4,
        scratch=[pltpu.SemaphoreType.DMA((4,))],
    )
    early = vid_count // 2
    late = [k for k in reversed(range(1, vid_count)) if k != early]
    auds = [swap(aud, "seq", k) for k in range(1, aud_count)] + [aud]
    vids = {k: swap(vid, "seq", k * aud_count) for k in (early, *late)}
    state = shape(vid_rows, width + LANES)
    total_aud = aud_count * aud_rows
    *shared, first_state, own_state = call(
        functools.partial(attend_first, aud_count),
        [
            shape(heads, 2 * vid_rows, total_aud, dtype=F32),
            shape(width, total_aud),
            shape(total_aud, width),
            shape(width, 2 * vid_rows),
            state,
            state,
        ],
        [*auds, vids[early], vid],
    )
    scores, queries_t, aud_vals, vals_t = shared
    states = call(
        functools.partial(attend, aud_count, len(late)),
        [shape(width + log_rows, aud_rows)] * aud_count + [state] * len(late),
        [queries_t, aud_vals, scores, vals_t, *(vids[k] for k in late)],
    )
    rows = [swap(states[k - 1], "seq", k) for k in range(1, aud_count)] + [states[aud_count - 1]]
    states = dict(zip((early, 0, *late), (first_state, own_state, *states[aud_count:])))
    cols = [swap(states[k], "seq", k * aud_count) for k in (early, *late)] + [states[0]]

    me = lax.axis_index("head").astype(jnp.int32).reshape(1)
    vmem = pl.BlockSpec(memory_space=pltpu.VMEM)
    smem = pl.BlockSpec(memory_space=pltpu.SMEM)
    hbm = pl.BlockSpec(memory_space=pl.ANY)

    mix_log = call(
        merge_first, [shape(vid_rows, width, dtype=F32)] * 2, [cols.pop(), cols.pop(0), audio_proj]
    )
    aud_terms = call(
        lambda me, proj, *refs: project_audio(me, proj, refs[:aud_count], refs[aud_count + 1 :]),
        [shape(aud_rows, step, dtype=F32)] + [shape(aud_rows, step)] * (peers - 1),
        [me, audio_proj, *rows, mix_log[0]],
        in_specs=[smem, vmem] + [vmem] * aud_count + [pl.BlockSpec(memory_space=pl.ANY)],
    )
    vid_terms = call(
        lambda me, proj, mix, log, core, *refs: project_video(
            me, proj, (mix, log), refs[: len(cols)], core, refs[len(cols) :]
        ),
        [shape(vid_rows, step, dtype=F32), shape(aud_rows + vid_rows, step)]
        + [shape(vid_rows, step)] * (peers - 2),
        [me, video_proj, *mix_log, aud_terms[1], *cols],
        in_specs=[smem] + [vmem] * (len(cols) + 4),
    )
    vid_got = [swap(vid_terms[k], "head", k) for k in reversed(range(2, peers))]
    core_got = swap(vid_terms[1], "head", 1)
    aud_got = [swap(aud_terms[k], "head", k) for k in reversed(range(2, peers))]
    aud_sum = call(add_terms, [shape(aud_rows, step, dtype=F32)], [aud_terms[0], *aud_got])[0]
    vid_sum = call(
        add_terms, [shape(vid_rows, step, dtype=F32)], [vid_terms[0], *vid_got], cost=COST_ADD
    )[0]
    return tuple(
        call(add_core, [shape(aud_rows, step), shape(vid_rows, step)], [aud_sum, vid_sum, core_got])
    )


def solution(mesh):
    in_specs = (
        P("seq", "head"),
        P("seq", "head"),
        P("seq", "head"),
        P("seq", "head"),
        P("head", None),
        P("head", None),
    )
    out_specs = (P("seq", "head"), P("seq", "head"))
    return jax.shard_map(
        per_device, mesh=mesh, in_specs=in_specs, out_specs=out_specs, check_vma=False
    )
```
